256 devices in a mesh: lon: 16 (over x_lo, y, core), lat: 16 (over z, x_hi).
Axes of the slice: x: 4 (x_hi: 2, x_lo: 2; x = x_hi * 2 + x_lo), y: 4, z: 8, core: 2. Of those that a mesh axis runs over, the one named last changes fastest.
Arguments:
- state: float32 [4, 8, 512, 4320], P(None, None, 'lat', 'lon'), may hold values from -6 to 6
- zonal_wind: float32 [8], replicated, may hold values from -0.1 to 0.1
- merid_wind: float32 [8], replicated, may hold values from -0.1 to 0.1
- sound_speed: float32 [8], replicated, may hold values from 0.04 to 0.12
- cutoff: int32 [512], P('lat'), may hold values from 270 to 2160, as said below
- polar_mask: int32 [512], P('lat'), may hold values from 0 to 1, as said below
Outputs:
- new_state: float32 [4, 8, 512, 4320], P(None, None, 'lat', 'lon')
The draws below stay inside these ranges and needn't reach their ends.
Inputs may be any that keep to these rules, and one draw needn't show every extreme that they name: `cutoff`: within 1 to 2160; some row has exactly 2160 in every draw. `polar_mask`: rows from 128 to 383 are always 0; the 64 rows nearest each end of the latitude range are always 1.
All inputs are finite; a program needn't handle non-finite values.
Results may differ from the reference program's by a relative error of at most 0.00005.
Values sent between devices are 32-bit elements; how exact they have to be, the bound alone decides.
No kernel may reach another device: no remote copies, remote signals or barrier semaphores. Data moves between devices by JAX's collectives and lax.ppermute only.
A program may use at most 64 MiB of HBM per device.

```python
import math
import jax
import jax.numpy as jnp
from jax import lax

NLON = 4320
LEV = 8
NLAT = 512


def draw_cutoff(key, part):
    key = jax.random.fold_in(key, 12)
    keys = jax.random.split(key, 2)
    values = jax.random.randint(keys[0], (NLAT,), NLON // 16, NLON // 2 + 1, dtype=jnp.int32)
    chosen = jax.random.randint(keys[1], (), 0, NLAT, dtype=jnp.int32)
    row_index = jnp.arange(NLAT, dtype=jnp.int32)
    return jnp.where(row_index == chosen, NLON // 2, values).astype(jnp.int32)


def draw_polar_mask(key, part):
    key = jax.random.fold_in(key, 11)
    row_index = jnp.arange(NLAT, dtype=jnp.int32)
    from_pole = jnp.minimum(row_index, NLAT - 1 - row_index)
    coins = jax.random.randint(key, (NLAT,), 0, 2, dtype=jnp.int32)
    core = from_pole < NLAT // 8
    outer = from_pole < NLAT // 4
    return jnp.where(core, 1, jnp.where(outer, coins, 0)).astype(jnp.int32)


def level_of(own_key, shape, pieces, smallest, top_value):
    gain = 1.0
    for dim, blocks in pieces:
        draws = jax.random.uniform(jax.random.fold_in(jax.random.fold_in(own_key, 6), dim), (blocks,), jnp.float32, smallest / len(pieces), top_value / len(pieces))
        gain = gain * jnp.repeat(jnp.exp(draws), shape[dim] // blocks).reshape((-1,) + (1,) * (len(shape) - 1 - dim))
    return gain


def noise(own_key, shape, spread, bound, shards=(), kind=jnp.bfloat16):
    level = level_of(own_key, shape, shards, -0.22, 0.18) if shards else 1.0
    array = jax.random.normal(own_key, shape, jnp.float32) * spread * level
    return jnp.minimum(jnp.maximum(array, -bound), bound).astype(kind)


def setup_inputs(seed: int = 0) -> dict:
    seeds = jax.random.split(jax.random.key(seed), 7)
    state = noise(seeds[0], (4, LEV, NLAT, NLON), 1.0, 6.0, ((2, 16), (3, 16)), jnp.float32)
    zonal_wind = jnp.clip(jax.random.uniform(seeds[1], (LEV,), jnp.float32, -0.1, 0.1), -0.1, 0.1)
    merid_wind = jnp.clip(jax.random.uniform(seeds[2], (LEV,), jnp.float32, -0.1, 0.1), -0.1, 0.1)
    sound_speed = jnp.clip(jnp.exp(jax.random.uniform(seeds[3], (LEV,), jnp.float32, math.log(0.04), math.log(0.12))), 0.04, 0.12)
    cutoff = draw_cutoff(jax.random.fold_in(seeds[6], 71), 0)
    polar_mask = draw_polar_mask(jax.random.fold_in(seeds[6], 71), 0)
    return {"state": state, "zonal_wind": zonal_wind, "merid_wind": merid_wind, "sound_speed": sound_speed, "cutoff": cutoff, "polar_mask": polar_mask}


CORIOLIS = 0.2


def latitude_terms(first_row, row_count, all_rows):
    row_index = first_row + jnp.arange(row_count, dtype=jnp.int32)
    latitude = -0.5 * jnp.pi + (row_index.astype(jnp.float32) + 0.5) * (jnp.pi / all_rows)
    inv_cos = 1.0 / jnp.maximum(jnp.cos(latitude), 0.25)
    return inv_cos[:, None], jnp.sin(latitude)[:, None]


def stencil(padded, inv_cos, sin_lat, zonal, merid, sound):
    middle = padded[..., 2:-2, :]
    zonal_diff = (8.0 * (middle[..., 3:-1] - middle[..., 1:-3]) - (middle[..., 4:] - middle[..., :-4])) / 12.0
    lat_inner = padded[..., 2:-2]
    merid_diff = (8.0 * (lat_inner[..., 3:-1, :] - lat_inner[..., 1:-3, :]) - (lat_inner[..., 4:, :] - lat_inner[..., :-4, :])) / 12.0
    centre = padded[..., 2:-2, 2:-2]
    advect = -(zonal * inv_cos) * zonal_diff - merid * merid_diff
    wind_u = centre[0]
    wind_v = centre[1]
    tend_u = advect[0] - sound * inv_cos * zonal_diff[2] + CORIOLIS * sin_lat * wind_v
    tend_v = advect[1] - sound * merid_diff[2] - CORIOLIS * sin_lat * wind_u
    tend_p = advect[2] - sound * (inv_cos * zonal_diff[0] + merid_diff[1])
    return jnp.stack([tend_u, tend_v, tend_p, advect[3]])


def wrap_pad(fields):
    extended = jnp.concatenate([fields[..., -2:], fields, fields[..., :2]], axis=-1)
    return jnp.pad(extended, ((0, 0), (2, 2), (0, 0)))


def reference(state, zonal_wind, merid_wind, sound_speed, cutoff, polar_mask):
    inv_cos, sin_lat = latitude_terms(0, NLAT, NLAT)
    wavenumbers = jnp.arange(NLON // 2 + 1, dtype=jnp.int32)
    kept_modes = wavenumbers[None, :] <= cutoff[:, None]

    def one_level(level_index):
        column_state = lax.dynamic_index_in_dim(state, level_index, axis=1, keepdims=False)
        zonal = zonal_wind[level_index]
        merid = merid_wind[level_index]
        sound = sound_speed[level_index]

        def tendency(fields):
            return stencil(wrap_pad(fields), inv_cos, sin_lat, zonal, merid, sound)

        first_tend = tendency(column_state)
        section_state = column_state + first_tend / 3.0
        second_tend = tendency(section_state)
        section_state = column_state + second_tend / 2.0
        increment = tendency(section_state)
        spectrum = jnp.fft.rfft(increment, axis=-1)
        spectrum = jnp.where(kept_modes, spectrum, jnp.zeros_like(spectrum))
        filtered = jnp.fft.irfft(spectrum, n=NLON, axis=-1).astype(increment.dtype)
        return column_state + jnp.where(polar_mask[:, None] == 1, filtered, increment)

    stacked = lax.map(one_level, jnp.arange(LEV, dtype=jnp.int32))
    return jnp.moveaxis(stacked, 0, 1)
```

```python
import functools
import math

import jax
import jax.numpy as jnp
import ml_dtypes
import numpy as np
from jax import lax
from jax.experimental import pallas as pl
from jax.experimental.pallas import tpu as pltpu
from jax.sharding import PartitionSpec as P

CORIOLIS = 0.2
FIELDS = 4
LEVELS = 8
ROWS = 32
COLS = 270
PARTS = 16
NLON = PARTS * COLS
HALO = 6
EXT = ROWS + 2 * HALO
LANES = 128
WIDE = 3 * LANES
BLOCK = 136
STRIP = FIELDS * HALO
STRIP_ROWS = (2 * STRIP + STRIP // 4) * 8
HALF = COLS // 2 + 1
REM = HALF - LANES


def lane_index(shape):
    return lax.broadcasted_iota(jnp.int32, shape, len(shape) - 1)


def dft_tables():
    m = np.concatenate([np.arange(256), 256 + np.arange(LANES) % 16])
    m_ok = np.concatenate([np.ones(256, bool), np.arange(LANES) % 16 < COLS - 256])
    q_cos = np.zeros(WIDE)
    is_cos = np.zeros(WIDE, bool)
    is_sin = np.zeros(WIDE, bool)
    q_cos[:LANES] = np.arange(LANES)
    is_cos[:LANES] = True
    q_cos[LANES : 2 * LANES] = np.arange(LANES)
    is_sin[LANES : 2 * LANES] = True
    q_cos[256 : 256 + REM] = LANES + np.arange(REM)
    is_cos[256 : 256 + REM] = True
    q_cos[256 + REM : 256 + 2 * REM] = LANES + np.arange(REM)
    is_sin[256 + REM : 256 + 2 * REM] = True
    phase = 2.0 * np.pi * ((m[:, None] * q_cos[None, :]) % COLS) / COLS
    cos, sin = np.cos(phase) * m_ok[:, None], np.sin(phase) * m_ok[:, None]
    table_a = np.where(is_cos, cos, 0.0) + np.where(is_sin, sin, 0.0)
    table_b = np.where(is_cos, sin, 0.0) + np.where(is_sin, cos, 0.0)
    weight = np.where((q_cos == 0) | (q_cos == HALF - 1), 1.0, 2.0) / NLON
    weight = np.where(is_cos | is_sin, weight, 0.0)
    return table_a, table_b, (table_a * weight).T, (table_b * weight).T


def split_table(table):
    table = table.astype(np.float32)
    high = table.astype(ml_dtypes.bfloat16)
    low = (table - high.astype(np.float32)).astype(ml_dtypes.bfloat16)
    main, rem = high[:256], high[256:]
    return np.concatenate([main, main, rem, rem], 0), low


def twist_table():
    rows = []
    lanes = np.arange(LANES)
    for r in range(PARTS // 2 + 1):
        for fn in (np.cos, np.sin):
            for m in (lanes, LANES + lanes, 256 + lanes % 16):
                rows.append(fn(2.0 * np.pi * r * m / NLON))
    return np.stack(rows).astype(np.float32)


def times_root(re, im, k, n, sign):
    k = k % n
    if k == 0:
        return re, im
    if 4 * k == n:
        return (im, -re) if sign < 0 else (-im, re)
    if 8 * k == n:
        h = math.sqrt(0.5)
        return ((re + im) * h, (im - re) * h) if sign < 0 else ((re - im) * h, (im + re) * h)
    c, s = math.cos(2 * math.pi * k / n), sign * math.sin(2 * math.pi * k / n)
    return re * c - im * s, im * c + re * s


def real_dft(xs):
    n = len(xs)
    if n == 2:
        return [(xs[0] + xs[1], None), (xs[0] - xs[1], None)]
    even, odd = real_dft(xs[0::2]), real_dft(xs[1::2])
    out = [None] * (n // 2 + 1)
    for k in range(n // 4 + 1):
        er, ei = even[k]
        orr, oi = odd[k]
        if k == 0:
            out[0] = (er + orr, None)
            out[n // 2] = (er - orr, None)
        elif 4 * k == n:
            out[k] = (er, -orr)
        else:
            tr, ti = times_root(orr, oi, k, n, -1)
            out[k] = (er + tr, ei + ti)
            out[n // 2 - k] = (er - tr, ti - ei)
    return out


def real_inverse(spec):
    n = 2 * (len(spec) - 1)
    if n == 2:
        return [spec[0][0] + spec[1][0], spec[0][0] - spec[1][0]]
    even, odd = [None] * (n // 4 + 1), [None] * (n // 4 + 1)
    for k in range(n // 4 + 1):
        ar, ai = spec[k]
        br, bi = spec[n // 2 - k]
        if k == 0:
            even[0], odd[0] = (ar + br, None), (ar - br, None)
        elif 4 * k == n:
            even[k], odd[k] = (ar + ar, None), (-(ai + ai), None)
        else:
            even[k] = (ar + br, ai - bi)
            odd[k] = times_root(ar - br, ai + bi, k, n, 1)
    es, os = real_inverse(even), real_inverse(odd)
    out = [None] * n
    out[0::2], out[1::2] = es, os
    return out


def load_levels(ref, field, row):
    return ref[field, pl.ds(row, LEVELS, stride=ROWS), :]


def pack_lon_kernel(first_ref, last_ref, right_ref, left_ref):
    lane = lane_index((LEVELS, LANES))
    for group in range(FIELDS * 2):
        field, half = group // 2, group % 2
        to_right = jnp.zeros((LEVELS, LANES), jnp.float32)
        to_left = jnp.zeros((LEVELS, LANES), jnp.float32)
        for slot in range(16):
            row = half * 16 + slot
            here = (lane >= 8 * slot) & (lane < 8 * slot + HALO)
            last = load_levels(last_ref, field, row)
            first = load_levels(first_ref, field, row)
            to_right = jnp.where(here, pltpu.roll(last, (8 * slot - 8) % LANES, 1), to_right)
            to_left = jnp.where(here, pltpu.roll(first, 8 * slot, 1), to_left)
        right_ref[pl.ds(group * 8, 8), :] = to_right
        left_ref[pl.ds(group * 8, 8), :] = to_left


def last_tile(tile, from_left, from_right, slot, lane):
    tile = jnp.where(
        (lane >= 14) & (lane < 14 + HALO),
        pltpu.roll(from_right, (14 - 8 * slot) % LANES, 1),
        tile,
    )
    return jnp.where(
        lane >= LANES - HALO, pltpu.roll(from_left, (LANES - HALO - 8 * slot) % LANES, 1), tile
    )


def pack_lat_kernel(tile0_ref, tile1_ref, tile2_ref, from_left_ref, from_right_ref, south_ref, north_ref):
    lane = lane_index((LEVELS, LANES))
    for out_ref, first_row in ((south_ref, ROWS - HALO), (north_ref, 0)):
        rest = None
        for n in range(STRIP):
            field, row = n // HALO, first_row + n % HALO
            group, slot = field * 2 + row // 16, row % 16
            out_ref[pl.ds(8 * n, 8), :] = load_levels(tile0_ref, field, row)
            out_ref[pl.ds(8 * (STRIP + n), 8), :] = load_levels(tile1_ref, field, row)
            tail = last_tile(
                load_levels(tile2_ref, field, row),
                from_left_ref[pl.ds(group * 8, 8), :],
                from_right_ref[pl.ds(group * 8, 8), :],
                slot,
                lane,
            )
            place = n % 4
            tail = pltpu.roll(tail, HALO + 32 * place, 1)
            rest = tail if place == 0 else jnp.where(lane >= 32 * place, tail, rest)
            if place == 3:
                out_ref[pl.ds(8 * (2 * STRIP + n // 4), 8), :] = rest


def stencil_kernel(
    ends_ref,
    tile0_ref,
    tile1_ref,
    tile2_ref,
    from_left_ref,
    from_right_ref,
    north_ref,
    south_ref,
    coef_ref,
    level_ref,
    out_ref,
    first_ref,
    second_ref,
    third_ref,
):
    lane = lane_index((LEVELS, LANES))

    def build(group, carry):
        field, half = group // 2, group % 2
        from_left = from_left_ref[pl.ds(group * 8, 8), :]
        from_right = from_right_ref[pl.ds(group * 8, 8), :]
        for slot in range(16):
            row = half * 16 + slot
            place = HALO + row
            first_ref[field, place, :, 0:LANES] = load_levels(tile0_ref, field, row)
            first_ref[field, place, :, LANES : 2 * LANES] = load_levels(tile1_ref, field, row)
            first_ref[field, place, :, 2 * LANES : WIDE] = last_tile(
                load_levels(tile2_ref, field, row), from_left, from_right, slot, lane
            )
        return carry

    lax.fori_loop(0, FIELDS * 2, build, 0)
    kept = (lane < 14 + HALO) | (lane >= LANES - HALO)
    for end, (strip_ref, start) in enumerate(((north_ref, 0), (south_ref, HALO + ROWS))):
        inside = ends_ref[end] == 0
        for n in range(STRIP):
            field, place = n // HALO, start + n % HALO
            tiles = [
                strip_ref[pl.ds(8 * n, 8), :],
                strip_ref[pl.ds(8 * (STRIP + n), 8), :],
                jnp.where(
                    kept,
                    pltpu.roll(
                        strip_ref[pl.ds(8 * (2 * STRIP + n // 4), 8), :],
                        (-HALO - 32 * (n % 4)) % LANES,
                        1,
                    ),
                    0.0,
                ),
            ]
            for t in range(3):
                first_ref[field, place, :, t * LANES : (t + 1) * LANES] = jnp.where(
                    inside, tiles[t], 0.0
                )

    merid = level_ref[0]
    sound = level_ref[1]

    def shifted(tiles, step):
        turned = [pltpu.roll(t, (-step) % LANES, 1) for t in tiles]
        out = []
        for t in range(3):
            if step > 0:
                out.append(jnp.where(lane < LANES - step, turned[t], turned[(t + 1) % 3]))
            else:
                out.append(jnp.where(lane >= -step, turned[t], turned[(t + 2) % 3]))
        return out

    def tendency(ref, row):
        zonal = coef_ref[0, row]
        sound_zonal = coef_ref[1, row]
        turn = coef_ref[2, row]

        def tiles_of(field, at):
            return [ref[field, at, :, t * LANES : (t + 1) * LANES] for t in range(3)]

        dx, dy, mid = [], [], []
        for field in range(FIELDS):
            centre = tiles_of(field, row)
            mid.append(centre)
            p1, m1 = shifted(centre, 1), shifted(centre, -1)
            p2, m2 = shifted(centre, 2), shifted(centre, -2)
            dx.append([8.0 * (p1[t] - m1[t]) - (p2[t] - m2[t]) for t in range(3)])
            n1, s1 = tiles_of(field, row + 1), tiles_of(field, row - 1)
            n2, s2 = tiles_of(field, row + 2), tiles_of(field, row - 2)
            dy.append([8.0 * (n1[t] - s1[t]) - (n2[t] - s2[t]) for t in range(3)])
        out = []
        for t in range(3):
            carry = [zonal * dx[f][t] + merid * dy[f][t] for f in range(FIELDS)]
            out.append(
                [
                    carry[0] + sound_zonal * dx[2][t] + turn * mid[1][t],
                    carry[1] + sound * dy[2][t] - turn * mid[0][t],
                    carry[2] + (sound_zonal * dx[0][t] + sound * dy[1][t]),
                    carry[3],
                ]
            )
        return out

    def stage(source, target, scale, margin):
        def body(row, carry):
            tend = tendency(source, row)
            for field in range(FIELDS):
                for t in range(3):
                    where = slice(t * LANES, (t + 1) * LANES)
                    target[field, row, :, where] = (
                        first_ref[field, row, :, where] + tend[t][field] * scale
                    )
            return carry

        lax.fori_loop(margin, EXT - margin, body, 0)
        blank = jnp.zeros((LEVELS, LANES), jnp.float32)
        for end, start in enumerate((0, HALO + ROWS)):

            @pl.when(ends_ref[end] != 0)
            def _():
                for field in range(FIELDS):
                    for i in range(HALO):
                        for t in range(3):
                            target[field, start + i, :, t * LANES : (t + 1) * LANES] = blank

    stage(first_ref, second_ref, 1.0 / 3.0, 2)
    stage(second_ref, third_ref, 0.5, 4)

    def last(dest, carry):
        rest = jnp.zeros((LEVELS, LANES), jnp.float32)
        for j in range(2):
            tend = tendency(third_ref, HALO + dest * 2 + j)
            for field in range(FIELDS):
                g = j * FIELDS + field
                out_ref[dest, pl.ds(8 * g, 8), :] = tend[0][field]
                out_ref[dest, pl.ds(64 + 8 * g, 8), :] = tend[1][field]
                tail = pltpu.roll(tend[2][field], 16 * g, 1) if g else tend[2][field]
                rest = jnp.where((lane >= 16 * g) & (lane < 16 * g + 14), tail, rest)
        out_ref[dest, pl.ds(128, 8), :] = rest
        return carry

    lax.fori_loop(0, PARTS, last, 0)


def filter_kernel(
    row_ref,
    in_ref,
    twist_ref,
    ahi_ref,
    alo_ref,
    bhi_ref,
    blo_ref,
    iahi_ref,
    ialo_ref,
    ibhi_ref,
    iblo_ref,
    out_ref,
    la_ref,
    lb_ref,
    sa_ref,
    sb_ref,
):
    count = PARTS // 2 + 1
    bf16 = jnp.bfloat16
    lane8 = lane_index((8, LANES))

    def twist(r, tile):
        at = r * 6 + tile
        return twist_ref[pl.ds(at, 1), :], twist_ref[pl.ds(at + 3, 1), :]

    def forward(xs, tile):
        spec = real_dft(xs)
        out = [(spec[0][0], None)]
        for r in range(1, count):
            cos, sin = twist(r, tile)
            re, im = spec[r]
            if im is None:
                out.append((re * cos, -(re * sin)))
            else:
                out.append((re * cos + im * sin, im * cos - re * sin))
        return out

    def backward(pairs, tile):
        spec = [(pairs[0][0], None)]
        for r in range(1, count):
            cos, sin = twist(r, tile)
            a, b = pairs[r]
            if r == count - 1:
                spec.append((a * cos - b * sin, None))
            else:
                spec.append((a * cos - b * sin, a * sin + b * cos))
        return real_inverse(spec)

    def halves(value):
        high = value.astype(bf16)
        return high, (value - high.astype(jnp.float32)).astype(bf16)

    def put_main(ref, at, tile, value):
        high, low = halves(value)
        ref[at, tile * LANES : (tile + 1) * LANES] = low
        ref[at, 256 + tile * LANES : 256 + (tile + 1) * LANES] = high

    for tile in range(2):

        def main(pair, carry):
            xs = [in_ref[d, pl.ds(64 * tile + 16 * pair, 16), :] for d in range(PARTS)]
            for r, (a, b) in enumerate(forward(xs, tile)):
                put_main(la_ref, pl.ds(r * 64 + 16 * pair, 16), tile, a)
                if b is not None:
                    put_main(lb_ref, pl.ds((r - 1) * 64 + 16 * pair, 16), tile, b)
            return carry

        lax.fori_loop(0, 4, main, 0)

    def put_rest(ref, base, value):
        high = value.astype(bf16).astype(jnp.float32)
        low = value - high
        for pair in range(4):
            for k, part in enumerate((high, low)):
                two = [
                    jnp.where((lane8 >= 16 * g) & (lane8 < 16 * g + 16), part, 0.0)
                    for g in (2 * pair, 2 * pair + 1)
                ]
                ref[pl.ds(base + 16 * pair, 16), 512 + k * LANES : 512 + (k + 1) * LANES] = (
                    jnp.concatenate(two, 0).astype(bf16)
                )

    rest_in = [in_ref[d, pl.ds(128, 8), :] for d in range(PARTS)]
    for r, (a, b) in enumerate(forward(rest_in, 2)):
        put_rest(la_ref, r * 64, a)
        if b is not None:
            put_rest(lb_ref, (r - 1) * 64, b)

    def product(l_ref, high_ref, low_ref):
        return jnp.dot(
            l_ref[...], high_ref[...], preferred_element_type=jnp.float32
        ) + jnp.dot(l_ref[:, 256:640], low_ref[...], preferred_element_type=jnp.float32)

    sa_ref[...] = product(la_ref, ahi_ref, alo_ref)
    sb_ref[...] = product(lb_ref, bhi_ref, blo_ref)

    lane = lane_index((1, WIDE))
    q = jnp.where(
        lane < 2 * LANES,
        lane % LANES,
        LANES + (lane % REM),
    )
    cos_lane = (lane < LANES) | ((lane >= 256) & (lane < 256 + REM))
    sign = jnp.where(cos_lane, 0.5, -0.5)

    def put_all(ref, at, value):
        high, low = halves(value)
        ref[at, 0:256] = low[:, 0:256]
        ref[at, 256:640] = high
        ref[at, 640:768] = low[:, 256:384]

    for r in range(count):
        up = 16 * q + r
        up = jnp.minimum(up, NLON - up)
        down = jnp.abs(16 * q - r)
        for j in range(2):
            cut = row_ref[j]
            keep_up = jnp.where(up <= cut, 1.0, 0.0)
            keep_down = jnp.where(down <= cut, 1.0, 0.0)
            same = 0.5 * (keep_up + keep_down)
            cross = sign * (keep_up - keep_down)
            for part in range(2):
                at = pl.ds(r * 64 + j * 32 + part * 16, 16)
                a = sa_ref[at, :]
                if r == 0:
                    put_all(la_ref, at, a * same)
                    continue
                at_b = pl.ds((r - 1) * 64 + j * 32 + part * 16, 16)
                b = sb_ref[at_b, :]
                put_all(la_ref, at, a * same + b * cross)
                put_all(lb_ref, at_b, b * same + a * cross)

    sa_ref[...] = product(la_ref, iahi_ref, ialo_ref)
    sb_ref[...] = product(lb_ref, ibhi_ref, iblo_ref)

    polar = [row_ref[2] == 1, row_ref[3] == 1]

    for tile in range(2):
        for j in range(2):

            def back(pair, carry):
                pairs = []
                for r in range(count):
                    where = slice(tile * LANES, (tile + 1) * LANES)
                    a = sa_ref[pl.ds(r * 64 + j * 32 + 16 * pair, 16), where]
                    b = None
                    if r:
                        b = sb_ref[pl.ds((r - 1) * 64 + j * 32 + 16 * pair, 16), where]
                    pairs.append((a, b))
                at = pl.ds(64 * tile + 32 * j + 16 * pair, 16)
                for d, value in enumerate(backward(pairs, tile)):
                    out_ref[d, at, :] = jnp.where(polar[j], value, in_ref[d, at, :])
                return carry

            lax.fori_loop(0, 2, back, 0)

    def gathered(ref, base):
        total = ref[pl.ds(base, 8), 256:384]
        for g in range(1, 8):
            total = jnp.where(lane8 >= 16 * g, ref[pl.ds(base + 8 * g, 8), 256:384], total)
        return total

    pairs = []
    for r in range(count):
        pairs.append(
            (gathered(sa_ref, r * 64), gathered(sb_ref, (r - 1) * 64) if r else None)
        )
    chosen = jnp.where(lane8 < 64, row_ref[2], row_ref[3]) == 1
    for d, value in enumerate(backward(pairs, 2)):
        out_ref[d, pl.ds(128, 8), :] = jnp.where(chosen, value, in_ref[d, pl.ds(128, 8), :])


def final_kernel(state_ref, back_ref, out_ref):
    tile = pl.program_id(0)

    def run(load):
        def one(dest, carry):
            for g, value in enumerate(load(dest)):
                at = (g % FIELDS, pl.ds(dest * 2 + g // FIELDS, LEVELS, stride=ROWS), slice(None))
                out_ref[at] = state_ref[at] + value
            return carry

        lax.fori_loop(0, PARTS, one, 0)

    def rest(dest):
        packed = back_ref[dest, pl.ds(128, 8), :]
        return [pltpu.roll(packed, (-16 * g) % LANES, 1) if g else packed for g in range(8)]

    pl.when(tile == 0)(lambda: run(lambda d: [back_ref[d, pl.ds(8 * g, 8), :] for g in range(8)]))
    pl.when(tile == 1)(
        lambda: run(lambda d: [back_ref[d, pl.ds(64 + 8 * g, 8), :] for g in range(8)])
    )
    pl.when(tile == 2)(lambda: run(rest))


def latitude_terms(first_row, row_count, all_rows):
    row_index = first_row + jnp.arange(row_count, dtype=jnp.int32)
    latitude = -0.5 * jnp.pi + (row_index.astype(jnp.float32) + 0.5) * (jnp.pi / all_rows)
    inv_cos = 1.0 / jnp.maximum(jnp.cos(latitude), 0.25)
    return inv_cos, jnp.sin(latitude)


def turn(cells, axis, step):
    count = lax.axis_size(axis)
    return lax.ppermute(cells, axis, [(i, (i + step) % count) for i in range(count)])


def tile_spec(tile):
    return pl.BlockSpec((FIELDS, LEVELS * ROWS, LANES), lambda i: (0, 0, tile))


VMEM = pl.BlockSpec(memory_space=pltpu.VMEM)
SMEM = pl.BlockSpec(memory_space=pltpu.SMEM)
PARAMS = pltpu.CompilerParams(vmem_limit_bytes=48 * 1024 * 1024)


def shape(*dims):
    return jax.ShapeDtypeStruct(dims, jnp.float32)


def on_device(state, zonal_wind, merid_wind, sound_speed, cutoff, polar_mask):
    lat_count = lax.axis_size("lat")
    lat_place = lax.axis_index("lat")
    lon_place = lax.axis_index("lon")
    flat = state.reshape(FIELDS, LEVELS * ROWS, COLS)

    to_right, to_left = pl.pallas_call(
        pack_lon_kernel,
        grid=(1,),
        out_shape=(shape(64, LANES), shape(64, LANES)),
        in_specs=[tile_spec(0), tile_spec(2)],
        out_specs=[VMEM, VMEM],
        compiler_params=PARAMS,
        name="pack_lon",
    )(flat, flat)
    from_left = turn(to_right, "lon", 1)
    from_right = turn(to_left, "lon", -1)

    to_south, to_north = pl.pallas_call(
        pack_lat_kernel,
        grid=(1,),
        out_shape=(shape(STRIP_ROWS, LANES), shape(STRIP_ROWS, LANES)),
        in_specs=[tile_spec(0), tile_spec(1), tile_spec(2), VMEM, VMEM],
        out_specs=[VMEM, VMEM],
        compiler_params=PARAMS,
        name="pack_lat",
    )(flat, flat, flat, from_left, from_right)
    from_north = turn(to_south, "lat", 1)
    from_south = turn(to_north, "lat", -1)

    inv_cos, sin_lat = latitude_terms(lat_place * ROWS - HALO, EXT, lat_count * ROWS)
    level = lambda v: (v / 12.0)[None, :, None]
    full = (EXT, LEVELS, LANES)
    coefs = jnp.stack(
        [
            jnp.broadcast_to(-level(zonal_wind) * inv_cos[:, None, None], full),
            jnp.broadcast_to(-level(sound_speed) * inv_cos[:, None, None], full),
            jnp.broadcast_to((CORIOLIS * sin_lat)[:, None, None], full),
        ]
    )
    levels = jnp.stack(
        [jnp.broadcast_to(-level(v)[0], (LEVELS, LANES)) for v in (merid_wind, sound_speed)]
    )
    ends = jnp.stack([lat_place == 0, lat_place == lat_count - 1]).astype(jnp.int32)

    scratch = pltpu.VMEM((FIELDS, EXT, LEVELS, WIDE), jnp.float32)
    blocks = pl.pallas_call(
        stencil_kernel,
        grid=(1,),
        out_shape=shape(PARTS, BLOCK, LANES),
        in_specs=[SMEM] + [tile_spec(t) for t in range(3)] + [VMEM] * 6,
        out_specs=VMEM,
        scratch_shapes=[scratch] * 3,
        compiler_params=PARAMS,
        name="stencil",
    )(ends, flat, flat, flat, from_left, from_right, from_north, from_south, coefs, levels)

    whole = lax.all_to_all(blocks, "lon", split_axis=0, concat_axis=0, tiled=True)

    mine = lambda v: lax.dynamic_slice_in_dim(v, lon_place * 2, 2)
    row_facts = jnp.concatenate([mine(cutoff), mine(polar_mask)]).astype(jnp.int32)
    tables = []
    for table in dft_tables():
        tables.extend(jnp.asarray(t) for t in split_table(table))
    count = PARTS // 2 + 1
    filtered = pl.pallas_call(
        filter_kernel,
        out_shape=shape(PARTS, BLOCK, LANES),
        in_specs=[SMEM] + [VMEM] * 10,
        scratch_shapes=[
            pltpu.VMEM((count * 64, 768), jnp.bfloat16),
            pltpu.VMEM(((count - 1) * 64, 768), jnp.bfloat16),
            pltpu.VMEM((count * 64, WIDE), jnp.float32),
            pltpu.VMEM(((count - 1) * 64, WIDE), jnp.float32),
        ],
        compiler_params=PARAMS,
        name="filter",
    )(row_facts, whole, jnp.asarray(twist_table()), *tables)

    back = lax.all_to_all(filtered, "lon", split_axis=0, concat_axis=0, tiled=True)
    out = pl.pallas_call(
        final_kernel,
        grid=(3,),
        out_shape=shape(FIELDS, LEVELS * ROWS, COLS),
        in_specs=[pl.BlockSpec((FIELDS, LEVELS * ROWS, LANES), lambda t: (0, 0, t)), VMEM],
        out_specs=pl.BlockSpec((FIELDS, LEVELS * ROWS, LANES), lambda t: (0, 0, t)),
        compiler_params=PARAMS,
        name="final",
    )(flat, back)
    return out.reshape(FIELDS, LEVELS, ROWS, COLS)


def solution(mesh):
    placed = (P(None, None, "lat", "lon"), P(), P(), P(), P("lat"), P("lat"))
    return jax.shard_map(
        on_device,
        mesh=mesh,
        in_specs=placed,
        out_specs=P(None, None, "lat", "lon"),
        check_vma=False,
    )
```

```python
import functools
import math

import jax
import jax.numpy as jnp
import ml_dtypes
import numpy as np
from jax import lax
from jax.experimental import pallas as pl
from jax.experimental.pallas import tpu as pltpu
from jax.sharding import PartitionSpec as P

CORIOLIS = 0.2
FIELDS = 4
LEVELS = 8
ROWS = 32
COLS = 270
PARTS = 16
NLON = PARTS * COLS
HALO = 6
EXT = ROWS + 2 * HALO
LANES = 128
WIDE = 3 * LANES
BLOCK = 136
STRIP = FIELDS * HALO
STRIP_ROWS = (2 * STRIP + STRIP // 4) * 8
EDGE = HALO // 2
HALF = COLS // 2 + 1
REM = HALF - LANES


def lane_index(shape):
    return lax.broadcasted_iota(jnp.int32, shape, len(shape) - 1)


def frequency_lanes():
    lanes = np.arange(WIDE)
    q = np.where(lanes < 256, lanes % LANES, LANES + lanes % REM)
    is_sin = ((lanes >= LANES) & (lanes < 256)) | ((lanes >= 256 + REM) & (lanes < 256 + 2 * REM))
    is_cos = (lanes < LANES) | ((lanes >= 256) & (lanes < 256 + 3 * REM) & ~is_sin)
    return q, is_cos, is_sin


def dft_table():
    m = np.concatenate([np.arange(256), 256 + np.arange(LANES) % 16])
    m_ok = m < COLS
    q, is_cos, is_sin = frequency_lanes()
    phase = 2.0 * np.pi * ((m[:, None] * q[None, :]) % COLS) / COLS
    table = np.where(is_cos, np.cos(phase), 0.0) + np.where(is_sin, np.sin(phase), 0.0)
    table = (table * m_ok[:, None]).astype(np.float32)
    high = table.astype(ml_dtypes.bfloat16)
    low = (table - high.astype(np.float32)).astype(ml_dtypes.bfloat16)
    return np.concatenate([high, low], 0)


def mask_table():
    q, is_cos, is_sin = frequency_lanes()
    weight = np.where((q == 0) | (q == HALF - 1), 1.0, 2.0) / NLON
    weight = np.where(np.arange(WIDE) < 256 + 2 * REM, weight, 0.0)
    sign = np.where(is_sin, -1.0, 1.0)
    return np.stack([q, 0.5 * weight, 0.5 * sign * weight] + [q * 0] * 5).astype(np.float32)


def twist_table():
    rows = []
    lanes = np.arange(LANES)
    for r in range(PARTS // 2 + 1):
        for fn in (np.cos, np.sin):
            for m in (lanes, LANES + lanes, 256 + lanes % 16):
                rows.append(fn(2.0 * np.pi * r * m / NLON))
    return np.stack(rows).astype(np.float32)


def times_root(re, im, k, n, sign):
    k = k % n
    if k == 0:
        return re, im
    if 4 * k == n:
        return (im, -re) if sign < 0 else (-im, re)
    if 8 * k == n:
        h = math.sqrt(0.5)
        return ((re + im) * h, (im - re) * h) if sign < 0 else ((re - im) * h, (im + re) * h)
    c, s = math.cos(2 * math.pi * k / n), sign * math.sin(2 * math.pi * k / n)
    return re * c - im * s, im * c + re * s


def real_dft(xs):
    n = len(xs)
    if n == 2:
        return [(xs[0] + xs[1], None), (xs[0] - xs[1], None)]
    even, odd = real_dft(xs[0::2]), real_dft(xs[1::2])
    out = [None] * (n // 2 + 1)
    for k in range(n // 4 + 1):
        er, ei = even[k]
        orr, oi = odd[k]
        if k == 0:
            out[0] = (er + orr, None)
            out[n // 2] = (er - orr, None)
        elif 4 * k == n:
            out[k] = (er, -orr)
        else:
            tr, ti = times_root(orr, oi, k, n, -1)
            out[k] = (er + tr, ei + ti)
            out[n // 2 - k] = (er - tr, ti - ei)
    return out


def real_inverse(spec):
    n = 2 * (len(spec) - 1)
    if n == 2:
        return [spec[0][0] + spec[1][0], spec[0][0] - spec[1][0]]
    even, odd = [None] * (n // 4 + 1), [None] * (n // 4 + 1)
    for k in range(n // 4 + 1):
        ar, ai = spec[k]
        br, bi = spec[n // 2 - k]
        if k == 0:
            even[0], odd[0] = (ar + br, None), (ar - br, None)
        elif 4 * k == n:
            even[k], odd[k] = (ar + ar, None), (-(ai + ai), None)
        else:
            even[k] = (ar + br, ai - bi)
            odd[k] = times_root(ar - br, ai + bi, k, n, 1)
    es, os = real_inverse(even), real_inverse(odd)
    out = [None] * n
    out[0::2], out[1::2] = es, os
    return out


def rows_of(ref, field, first_row):
    return jnp.swapaxes(ref[field, :, first_row : first_row + 8, :], 0, 1)


def pack_lon_kernel(first_ref, last_ref, right_ref, left_ref):
    lane = lane_index((LEVELS, LANES))
    for group in range(FIELDS * 2):
        field, half = group // 2, group % 2
        to_right = to_left = None
        for block in range(2):
            last = rows_of(last_ref, field, half * 16 + block * 8)
            first = rows_of(first_ref, field, half * 16 + block * 8)
            for i in range(8):
                slot = block * 8 + i
                last_i = pltpu.roll(last[i], (8 * slot - 8) % LANES, 1)
                first_i = pltpu.roll(first[i], 8 * slot, 1) if slot else first[i]
                here = lane >= 8 * slot
                to_right = jnp.where(here, last_i, to_right) if slot else last_i
                to_left = jnp.where(here, first_i, to_left) if slot else first_i
        right_ref[pl.ds(group * 8, 8), :] = to_right
        left_ref[pl.ds(group * 8, 8), :] = to_left


def last_tile(tile, from_left, from_right, slot, lane):
    tile = jnp.where(
        (lane >= 14) & (lane < 14 + HALO),
        pltpu.roll(from_right, (14 - 8 * slot) % LANES, 1),
        tile,
    )
    return jnp.where(
        lane >= LANES - HALO, pltpu.roll(from_left, (LANES - HALO - 8 * slot) % LANES, 1), tile
    )


def pack_lat_kernel(
    tile0_ref, tile1_ref, tile2_ref, from_left_ref, from_right_ref, south_ref, north_ref
):
    lane = lane_index((LEVELS, LANES))
    for out_ref, block, skip in ((south_ref, ROWS - 8, 8 - HALO), (north_ref, 0, 0)):
        rest = None
        for field in range(FIELDS):
            parts = [rows_of(ref, field, block) for ref in (tile0_ref, tile1_ref, tile2_ref)]
            for i in range(HALO):
                n = field * HALO + i
                row = block + skip + i
                group, slot = field * 2 + row // 16, row % 16
                out_ref[pl.ds(8 * n, 8), :] = parts[0][skip + i]
                out_ref[pl.ds(8 * (STRIP + n), 8), :] = parts[1][skip + i]
                tail = last_tile(
                    parts[2][skip + i],
                    from_left_ref[pl.ds(group * 8, 8), :],
                    from_right_ref[pl.ds(group * 8, 8), :],
                    slot,
                    lane,
                )
                place = n % 4
                tail = pltpu.roll(tail, HALO + 32 * place, 1)
                rest = tail if place == 0 else jnp.where(lane >= 32 * place, tail, rest)
                if place == 3:
                    out_ref[pl.ds(8 * (2 * STRIP + n // 4), 8), :] = rest


def shifted(tiles, step, lane):
    turned = [pltpu.roll(t, (-step) % LANES, 1) for t in tiles]
    if step > 0:
        return [jnp.where(lane < LANES - step, turned[t], turned[(t + 1) % 3]) for t in range(3)]
    return [jnp.where(lane >= -step, turned[t], turned[(t + 2) % 3]) for t in range(3)]


def tendency(load, row, at, coef_ref, level_ref, lane):
    zonal = coef_ref[0, at]
    sound_zonal = coef_ref[1, at]
    turn = coef_ref[2, at]
    merid = level_ref[0]
    sound = level_ref[1]
    dx, dy, mid = [], [], []
    for field in range(FIELDS):
        centre = load(field, row)
        mid.append(centre)
        p1, m1 = shifted(centre, 1, lane), shifted(centre, -1, lane)
        p2, m2 = shifted(centre, 2, lane), shifted(centre, -2, lane)
        dx.append([8.0 * (p1[t] - m1[t]) - (p2[t] - m2[t]) for t in range(3)])
        n1, s1 = load(field, row + 1), load(field, row - 1)
        n2, s2 = load(field, row + 2), load(field, row - 2)
        dy.append([8.0 * (n1[t] - s1[t]) - (n2[t] - s2[t]) for t in range(3)])
    out = []
    for t in range(3):
        carry = [zonal * dx[f][t] + merid * dy[f][t] for f in range(FIELDS)]
        out.append(
            [
                carry[0] + (sound_zonal * dx[2][t] + turn * mid[1][t]),
                carry[1] + (sound * dy[2][t] - turn * mid[0][t]),
                carry[2] + (sound_zonal * dx[0][t] + sound * dy[1][t]),
                carry[3],
            ]
        )
    return out


def tiles_of(ref, *place):
    return [ref[(*place, slice(None), slice(t * LANES, (t + 1) * LANES))] for t in range(3)]


def put_tiles(ref, tiles, *place):
    for t in range(3):
        ref[(*place, slice(None), slice(t * LANES, (t + 1) * LANES))] = tiles[t]


def put_blocks(out_ref, dest, tends, lane):
    rest = jnp.zeros((LEVELS, LANES), jnp.float32)
    for j, tend in enumerate(tends):
        for field in range(FIELDS):
            g = j * FIELDS + field
            out_ref[dest, pl.ds(8 * g, 8), :] = tend[0][field]
            out_ref[dest, pl.ds(64 + 8 * g, 8), :] = tend[1][field]
            tail = pltpu.roll(tend[2][field], 16 * g, 1) if g else tend[2][field]
            rest = jnp.where((lane >= 16 * g) & (lane < 16 * g + 14), tail, rest)
    out_ref[dest, pl.ds(128, 8), :] = rest


def interior_kernel(
    tile0_ref,
    tile1_ref,
    tile2_ref,
    from_left_ref,
    from_right_ref,
    coef_ref,
    level_ref,
    out_ref,
    kept_ref,
    first_ref,
    second_ref,
    third_ref,
):
    lane = lane_index((LEVELS, LANES))
    for field in range(FIELDS):
        for block in range(0, ROWS, 8):
            parts = [rows_of(ref, field, block) for ref in (tile0_ref, tile1_ref, tile2_ref)]
            for i in range(8):
                row = block + i
                group, slot = field * 2 + row // 16, row % 16
                tail = last_tile(
                    parts[2][i],
                    from_left_ref[pl.ds(group * 8, 8), :],
                    from_right_ref[pl.ds(group * 8, 8), :],
                    slot,
                    lane,
                )
                tiles = [parts[0][i], parts[1][i], tail]
                put_tiles(first_ref, tiles, field, row)
                if row < 4:
                    put_tiles(kept_ref, tiles, 0, 0, field, row)
                if row >= ROWS - 4:
                    put_tiles(kept_ref, tiles, 0, 1, field, row - (ROWS - 4))

    def tend_of(ref, row):
        return tendency(
            lambda f, r: tiles_of(ref, f, r), row, row + HALO, coef_ref, level_ref, lane
        )

    def stage(source, target, scale, margin, unroll):
        def body(row, carry):
            tend = tend_of(source, row)
            for field in range(FIELDS):
                base = tiles_of(first_ref, field, row)
                put_tiles(target, [base[t] + tend[t][field] * scale for t in range(3)], field, row)
            return carry

        lax.fori_loop(margin, ROWS - margin, body, 0, unroll=unroll)

    def keep(source, which, margin):
        for field in range(FIELDS):
            for i in range(4):
                put_tiles(kept_ref, tiles_of(source, field, margin + i), which, 0, field, i)
                put_tiles(
                    kept_ref, tiles_of(source, field, ROWS - margin - 4 + i), which, 1, field, i
                )

    stage(first_ref, second_ref, 1.0 / 3.0, 2, 4)
    keep(second_ref, 1, 2)
    stage(second_ref, third_ref, 0.5, 4, 4)
    keep(third_ref, 2, 4)

    def last(dest, carry):
        put_blocks(out_ref, dest, [tend_of(third_ref, dest * 2 + j) for j in range(2)], lane)
        return carry

    lax.fori_loop(EDGE, PARTS - EDGE, last, 0, unroll=2)


def edge_kernel(
    ends_ref,
    north_ref,
    south_ref,
    coef_ref,
    level_ref,
    kept_ref,
    in_ref,
    out_ref,
    first_ref,
    second_ref,
    third_ref,
):
    lane = lane_index((LEVELS, LANES))
    valid = (lane < 14 + HALO) | (lane >= LANES - HALO)
    strips = (north_ref, south_ref)
    for side in range(2):
        inside = ends_ref[side] == 0
        own = 6 * (1 - side)
        for n in range(STRIP):
            field, place = n // HALO, 4 * side + n % HALO
            strip = strips[side]
            tiles = [
                strip[pl.ds(8 * n, 8), :],
                strip[pl.ds(8 * (STRIP + n), 8), :],
                jnp.where(
                    valid,
                    pltpu.roll(
                        strip[pl.ds(8 * (2 * STRIP + n // 4), 8), :],
                        (-HALO - 32 * (n % 4)) % LANES,
                        1,
                    ),
                    0.0,
                ),
            ]
            tiles = [jnp.where(inside, tile, 0.0) for tile in tiles]
            put_tiles(first_ref, tiles, side, field, place)
        for which, ref in enumerate((first_ref, second_ref, third_ref)):
            for field in range(FIELDS):
                for i in range(4):
                    tiles = tiles_of(kept_ref, which, side, field, i)
                    put_tiles(ref, tiles, side, field, own + i)

    def tend_of(ref, side, row, at):
        return tendency(
            lambda f, r: tiles_of(ref, side, f, r), row, at, coef_ref, level_ref, lane
        )

    starts = ((-6, -4, -2), (ROWS - 4, ROWS - 6, ROWS - 8))
    blank = [jnp.zeros((LEVELS, LANES), jnp.float32)] * 3

    def stage(source, target, stage_index, scale, outside):
        for side in range(2):
            begin = starts[side][stage_index]

            def body(k, carry):
                i = 4 * side + k
                middle = begin + i - starts[side][stage_index - 1]
                tend = tend_of(source, side, middle, begin + i + HALO)
                for field in range(FIELDS):
                    base = tiles_of(first_ref, side, field, begin + i - starts[side][0])
                    put_tiles(
                        target,
                        [base[t] + tend[t][field] * scale for t in range(3)],
                        side,
                        field,
                        i,
                    )
                return carry

            lax.fori_loop(0, HALO, body, 0, unroll=3)

            @pl.when(ends_ref[side] != 0)
            def _():
                for field in range(FIELDS):
                    for i in range(outside):
                        place = i if side == 0 else 10 - outside + i
                        put_tiles(target, blank, side, field, place)

    stage(first_ref, second_ref, 1, 1.0 / 3.0, 4)
    stage(second_ref, third_ref, 2, 0.5, 2)

    def copy(dest, carry):
        for part in range(BLOCK // 8):
            out_ref[dest, pl.ds(8 * part, 8), :] = in_ref[dest, pl.ds(8 * part, 8), :]
        return carry

    lax.fori_loop(EDGE, PARTS - EDGE, copy, 0)
    for side in range(2):

        def last(pair, carry):
            first_row = 2 * pair + side * (ROWS - HALO)
            tends = [
                tend_of(third_ref, side, 2 * pair + j + 2, first_row + j + HALO) for j in range(2)
            ]
            put_blocks(out_ref, pair + side * (PARTS - EDGE), tends, lane)
            return carry

        lax.fori_loop(0, EDGE, last, 0, unroll=EDGE)


def filter_kernel(
    row_ref, in_ref, twist_ref, mask_ref, table_ref, out_ref, la_ref, lb_ref, sa_ref, sb_ref
):
    count = PARTS // 2 + 1
    bf16 = jnp.bfloat16
    lane8 = lane_index((8, LANES))

    def twist(r, tile):
        at = r * 6 + tile
        return twist_ref[pl.ds(at, 1), :], twist_ref[pl.ds(at + 3, 1), :]

    def forward(xs, tile):
        spec = real_dft(xs)
        out = [(spec[0][0], None)]
        for r in range(1, count):
            cos, sin = twist(r, tile)
            re, im = spec[r]
            if im is None:
                out.append((re * cos, -(re * sin)))
            else:
                out.append((re * cos + im * sin, im * cos - re * sin))
        return out

    def backward(pairs, tile):
        spec = [(pairs[0][0], None)]
        for r in range(1, count):
            cos, sin = twist(r, tile)
            a, b = pairs[r]
            if r == count - 1:
                spec.append((a * cos - b * sin, None))
            else:
                spec.append((a * cos - b * sin, a * sin + b * cos))
        return real_inverse(spec)

    def halves(value):
        high = value.astype(bf16)
        return high, (value - high.astype(jnp.float32)).astype(bf16)

    def put_main(ref, at, tile, value):
        high, low = halves(value)
        ref[at, tile * LANES : (tile + 1) * LANES] = high
        ref[at, WIDE + tile * LANES : WIDE + (tile + 1) * LANES] = low

    for tile in range(2):

        def main(pair, carry):
            xs = [in_ref[d, pl.ds(64 * tile + 16 * pair, 16), :] for d in range(PARTS)]
            for r, (a, b) in enumerate(forward(xs, tile)):
                put_main(la_ref, pl.ds(r * 64 + 16 * pair, 16), tile, a)
                if b is not None:
                    put_main(lb_ref, pl.ds((r - 1) * 64 + 16 * pair, 16), tile, b)
            return carry

        lax.fori_loop(0, 4, main, 0)

    def put_rest(ref, base, value):
        high = value.astype(bf16).astype(jnp.float32)
        low = value - high
        for pair in range(4):
            for k, part in enumerate((high, low)):
                two = [
                    jnp.where((lane8 >= 16 * g) & (lane8 < 16 * g + 16), part, 0.0)
                    for g in (2 * pair, 2 * pair + 1)
                ]
                ref[pl.ds(base + 16 * pair, 16), k * WIDE + 256 : (k + 1) * WIDE] = (
                    jnp.concatenate(two, 0).astype(bf16)
                )

    rest_in = [in_ref[d, pl.ds(128, 8), :] for d in range(PARTS)]
    for r, (a, b) in enumerate(forward(rest_in, 2)):
        put_rest(la_ref, r * 64, a)
        if b is not None:
            put_rest(lb_ref, (r - 1) * 64, b)

    def product(l_ref, dim):
        def times(part, table):
            return lax.dot_general(
                l_ref[:, part * WIDE : (part + 1) * WIDE],
                table_ref[table * WIDE : (table + 1) * WIDE, :],
                (((1,), (dim,)), ((), ())),
                preferred_element_type=jnp.float32,
            )

        return times(0, 0) + times(1, 0) + times(0, 1)

    sa_ref[...] = product(la_ref, 0)
    sb_ref[...] = product(lb_ref, 0)

    q = mask_ref[0:1, :].astype(jnp.int32)
    half = mask_ref[1:2, :]
    half_signed = mask_ref[2:3, :]

    def put_all(ref, at, value):
        high, low = halves(value)
        ref[at, 0:WIDE] = high
        ref[at, WIDE : 2 * WIDE] = low

    def swap(value):
        return jnp.concatenate(
            [
                value[:, LANES : 2 * LANES],
                value[:, 0:LANES],
                pltpu.roll(value[:, 2 * LANES :], LANES - REM, 1),
            ],
            axis=1,
        )

    for r in range(count):
        up = 16 * q + r
        up = jnp.minimum(up, NLON - up)
        down = jnp.abs(16 * q - r)
        for j in range(2):
            cut = row_ref[j]
            keep_up = jnp.where(up <= cut, 1.0, 0.0)
            keep_down = jnp.where(down <= cut, 1.0, 0.0)
            same = half * (keep_up + keep_down)
            cross = half_signed * (keep_up - keep_down)
            for part in range(2):
                at = pl.ds(r * 64 + j * 32 + part * 16, 16)
                a = sa_ref[at, :]
                if r == 0:
                    put_all(la_ref, at, a * same)
                    continue
                at_b = pl.ds((r - 1) * 64 + j * 32 + part * 16, 16)
                b = sb_ref[at_b, :]
                put_all(la_ref, at, a * same + swap(b) * cross)
                put_all(lb_ref, at_b, b * same - swap(a) * cross)

    sa_ref[...] = product(la_ref, 1)
    sb_ref[...] = product(lb_ref, 1)

    polar = [row_ref[2] == 1, row_ref[3] == 1]

    for tile in range(2):
        for j in range(2):

            def back(pair, carry):
                pairs = []
                for r in range(count):
                    where = slice(tile * LANES, (tile + 1) * LANES)
                    a = sa_ref[pl.ds(r * 64 + j * 32 + 16 * pair, 16), where]
                    b = None
                    if r:
                        b = sb_ref[pl.ds((r - 1) * 64 + j * 32 + 16 * pair, 16), where]
                    pairs.append((a, b))
                at = pl.ds(64 * tile + 32 * j + 16 * pair, 16)
                for d, value in enumerate(backward(pairs, tile)):
                    out_ref[d, at, :] = jnp.where(polar[j], value, in_ref[d, at, :])
                return carry

            lax.fori_loop(0, 2, back, 0)

    def gathered(ref, base):
        total = ref[pl.ds(base, 8), 256:384]
        for g in range(1, 8):
            total = jnp.where(lane8 >= 16 * g, ref[pl.ds(base + 8 * g, 8), 256:384], total)
        return total

    pairs = []
    for r in range(count):
        pairs.append(
            (gathered(sa_ref, r * 64), gathered(sb_ref, (r - 1) * 64) if r else None)
        )
    chosen = jnp.where(lane8 < 64, row_ref[2], row_ref[3]) == 1
    for d, value in enumerate(backward(pairs, 2)):
        out_ref[d, pl.ds(128, 8), :] = jnp.where(chosen, value, in_ref[d, pl.ds(128, 8), :])


def final_kernel(state_ref, back_ref, out_ref):
    tile = pl.program_id(0)
    half = pl.program_id(1)

    def run(load):
        for f in range(FIELDS // 2):
            for block in range(0, ROWS, 8):
                units = [load((block + i) // 2, i % 2, f) for i in range(8)]
                added = jnp.swapaxes(jnp.stack(units), 0, 1)
                at = (f, slice(None), slice(block, block + 8), slice(None))
                out_ref[at] = state_ref[at] + added

    def place(j, f):
        return j * FIELDS + half * (FIELDS // 2) + f

    def rest(dest, j, f):
        return pltpu.roll(back_ref[dest, pl.ds(128, 8), :], (LANES - 16 * place(j, f)) % LANES, 1)

    pl.when(tile == 0)(
        lambda: run(lambda d, j, f: back_ref[d, pl.ds(pl.multiple_of(8 * place(j, f), 8), 8), :])
    )
    pl.when(tile == 1)(
        lambda: run(
            lambda d, j, f: back_ref[d, pl.ds(pl.multiple_of(64 + 8 * place(j, f), 8), 8), :]
        )
    )
    pl.when(tile == 2)(lambda: run(rest))


def latitude_terms(first_row, row_count, all_rows):
    row_index = first_row + jnp.arange(row_count, dtype=jnp.int32)
    latitude = -0.5 * jnp.pi + (row_index.astype(jnp.float32) + 0.5) * (jnp.pi / all_rows)
    inv_cos = 1.0 / jnp.maximum(jnp.cos(latitude), 0.25)
    return inv_cos, jnp.sin(latitude)


def turn(cells, axis, step):
    count = lax.axis_size(axis)
    return lax.ppermute(cells, axis, [(i, (i + step) % count) for i in range(count)])


def tile_spec(tile):
    return pl.BlockSpec((FIELDS, LEVELS, ROWS, LANES), lambda i: (0, 0, 0, tile))


VMEM = pl.BlockSpec(memory_space=pltpu.VMEM)
SMEM = pl.BlockSpec(memory_space=pltpu.SMEM)


def grant(mib):
    return pltpu.CompilerParams(vmem_limit_bytes=mib * 1024 * 1024)


def shape(*dims):
    return jax.ShapeDtypeStruct(dims, jnp.float32)


def on_device(state, zonal_wind, merid_wind, sound_speed, cutoff, polar_mask):
    lat_count = lax.axis_size("lat")
    lat_place = lax.axis_index("lat")
    lon_place = lax.axis_index("lon")
    to_right, to_left = pl.pallas_call(
        pack_lon_kernel,
        grid=(1,),
        out_shape=(shape(64, LANES), shape(64, LANES)),
        in_specs=[tile_spec(0), tile_spec(2)],
        out_specs=[VMEM, VMEM],
        compiler_params=grant(8),
        name="pack_lon",
    )(state, state)
    from_left = turn(to_right, "lon", 1)
    from_right = turn(to_left, "lon", -1)

    to_south, to_north = pl.pallas_call(
        pack_lat_kernel,
        grid=(1,),
        out_shape=(shape(STRIP_ROWS, LANES), shape(STRIP_ROWS, LANES)),
        in_specs=[tile_spec(0), tile_spec(1), tile_spec(2), VMEM, VMEM],
        out_specs=[VMEM, VMEM],
        compiler_params=grant(8),
        name="pack_lat",
    )(state, state, state, from_left, from_right)
    from_north = turn(to_south, "lat", 1)
    from_south = turn(to_north, "lat", -1)

    inv_cos, sin_lat = latitude_terms(lat_place * ROWS - HALO, EXT, lat_count * ROWS)
    level = lambda v: (v / 12.0)[None, :, None]
    full = (EXT, LEVELS, LANES)
    coefs = jnp.stack(
        [
            jnp.broadcast_to(-level(zonal_wind) * inv_cos[:, None, None], full),
            jnp.broadcast_to(-level(sound_speed) * inv_cos[:, None, None], full),
            jnp.broadcast_to((CORIOLIS * sin_lat)[:, None, None], full),
        ]
    )
    levels = jnp.stack(
        [jnp.broadcast_to(-level(v)[0], (LEVELS, LANES)) for v in (merid_wind, sound_speed)]
    )
    ends = jnp.stack([lat_place == 0, lat_place == lat_count - 1]).astype(jnp.int32)

    scratch = pltpu.VMEM((FIELDS, ROWS, LEVELS, WIDE), jnp.float32)
    inner, kept = pl.pallas_call(
        interior_kernel,
        grid=(1,),
        out_shape=(shape(PARTS, BLOCK, LANES), shape(3, 2, FIELDS, 4, LEVELS, WIDE)),
        in_specs=[tile_spec(t) for t in range(3)] + [VMEM] * 4,
        out_specs=(VMEM, VMEM),
        scratch_shapes=[scratch] * 3,
        compiler_params=grant(20),
        cost_estimate=pl.CostEstimate(
            flops=80_000_000, bytes_accessed=6_000_000, transcendentals=0
        ),
        name="interior",
    )(state, state, state, from_left, from_right, coefs, levels)
    scratch = pltpu.VMEM((2, FIELDS, 10, LEVELS, WIDE), jnp.float32)
    blocks = pl.pallas_call(
        edge_kernel,
        out_shape=shape(PARTS, BLOCK, LANES),
        in_specs=[SMEM] + [VMEM] * 6,
        out_specs=VMEM,
        scratch_shapes=[scratch] * 3,
        compiler_params=grant(20),
        name="edge",
    )(ends, from_north, from_south, coefs, levels, kept, inner)

    whole = lax.all_to_all(blocks, "lon", split_axis=0, concat_axis=0, tiled=True)

    mine = lambda v: lax.dynamic_slice_in_dim(v, lon_place * 2, 2)
    row_facts = jnp.concatenate([mine(cutoff), mine(polar_mask)]).astype(jnp.int32)
    count = PARTS // 2 + 1
    filtered = pl.pallas_call(
        filter_kernel,
        out_shape=shape(PARTS, BLOCK, LANES),
        in_specs=[SMEM] + [VMEM] * 4,
        out_specs=VMEM,
        scratch_shapes=[
            pltpu.VMEM((count * 64, 2 * WIDE), jnp.bfloat16),
            pltpu.VMEM(((count - 1) * 64, 2 * WIDE), jnp.bfloat16),
            pltpu.VMEM((count * 64, WIDE), jnp.float32),
            pltpu.VMEM(((count - 1) * 64, WIDE), jnp.float32),
        ],
        compiler_params=grant(20),
        name="filter",
    )(
        row_facts,
        whole,
        jnp.asarray(twist_table()),
        jnp.asarray(mask_table()),
        jnp.asarray(dft_table()),
    )

    back = lax.all_to_all(filtered, "lon", split_axis=0, concat_axis=0, tiled=True)
    half_tile = pl.BlockSpec((FIELDS // 2, LEVELS, ROWS, LANES), lambda t, h: (h, 0, 0, t))
    return pl.pallas_call(
        final_kernel,
        grid=(3, 2),
        out_shape=shape(*state.shape),
        in_specs=[half_tile, VMEM],
        out_specs=half_tile,
        compiler_params=grant(12),
        name="final",
    )(state, back)


def solution(mesh):
    placed = (P(None, None, "lat", "lon"), P(), P(), P(), P("lat"), P("lat"))
    return jax.shard_map(
        on_device,
        mesh=mesh,
        in_specs=placed,
        out_specs=P(None, None, "lat", "lon"),
        check_vma=False,
    )
```

```python
import functools
import math

import jax
import jax.numpy as jnp
import ml_dtypes
import numpy as np
from jax import lax
from jax.experimental import pallas as pl
from jax.experimental.pallas import tpu as pltpu
from jax.sharding import PartitionSpec as P

CORIOLIS = 0.2
FIELDS = 4
LEVELS = 8
ROWS = 32
COLS = 270
PARTS = 16
NLON = PARTS * COLS
HALO = 6
EXT = ROWS + 2 * HALO
LANES = 128
WIDE = 3 * LANES
OUT = 144
BACK = 136
STRIP = FIELDS * HALO
STRIP_ROWS = (2 * STRIP + STRIP // 8) * 8
TAIL = COLS - 2 * LANES
EDGE = HALO // 2
HALF = COLS // 2 + 1
REM = HALF - LANES


def lane_index(shape):
    return lax.broadcasted_iota(jnp.int32, shape, len(shape) - 1)


def frequency_lanes():
    lanes = np.arange(WIDE)
    q = np.where(lanes < 256, lanes % LANES, LANES + lanes % REM)
    is_sin = ((lanes >= LANES) & (lanes < 256)) | ((lanes >= 256 + REM) & (lanes < 256 + 2 * REM))
    is_cos = (lanes < LANES) | ((lanes >= 256) & (lanes < 256 + 3 * REM) & ~is_sin)
    return q, is_cos, is_sin


def column_lanes():
    slot = np.arange(LANES) % 32
    return np.concatenate([np.arange(256), np.where(slot < HALO, slot - HALO, 256 - HALO + slot)])


def dft_table():
    m = column_lanes()
    m_ok = m < COLS + HALO
    q, is_cos, is_sin = frequency_lanes()
    phase = 2.0 * np.pi * ((m[:, None] * q[None, :]) % COLS) / COLS
    table = np.where(is_cos, np.cos(phase), 0.0) + np.where(is_sin, np.sin(phase), 0.0)
    table = (table * m_ok[:, None]).astype(np.float32)
    high = table.astype(ml_dtypes.bfloat16)
    low = (table - high.astype(np.float32)).astype(ml_dtypes.bfloat16)
    return np.concatenate([high, low], 0)


def mask_table():
    q, is_cos, is_sin = frequency_lanes()
    weight = np.where((q == 0) | (q == HALF - 1), 1.0, 2.0) / NLON
    weight = np.where(np.arange(WIDE) < 256 + 2 * REM, weight, 0.0)
    sign = np.where(is_sin, -1.0, 1.0)
    return np.stack([q, 0.5 * weight, 0.5 * sign * weight] + [q * 0] * 5).astype(np.float32)


def twist_table():
    rows = []
    for r in range(PARTS // 2 + 1):
        for fn in (np.cos, np.sin):
            for m in column_lanes().reshape(3, LANES):
                rows.append(fn(2.0 * np.pi * r * m / NLON))
    return np.stack(rows).astype(np.float32)


def times_root(re, im, k, n, sign):
    k = k % n
    if k == 0:
        return re, im
    if 4 * k == n:
        return (im, -re) if sign < 0 else (-im, re)
    if 8 * k == n:
        h = math.sqrt(0.5)
        return ((re + im) * h, (im - re) * h) if sign < 0 else ((re - im) * h, (im + re) * h)
    c, s = math.cos(2 * math.pi * k / n), sign * math.sin(2 * math.pi * k / n)
    return re * c - im * s, im * c + re * s


def real_dft(xs):
    n = len(xs)
    if n == 2:
        return [(xs[0] + xs[1], None), (xs[0] - xs[1], None)]
    even, odd = real_dft(xs[0::2]), real_dft(xs[1::2])
    out = [None] * (n // 2 + 1)
    for k in range(n // 4 + 1):
        er, ei = even[k]
        orr, oi = odd[k]
        if k == 0:
            out[0] = (er + orr, None)
            out[n // 2] = (er - orr, None)
        elif 4 * k == n:
            out[k] = (er, -orr)
        else:
            tr, ti = times_root(orr, oi, k, n, -1)
            out[k] = (er + tr, ei + ti)
            out[n // 2 - k] = (er - tr, ti - ei)
    return out


def real_inverse(spec):
    n = 2 * (len(spec) - 1)
    if n == 2:
        return [spec[0][0] + spec[1][0], spec[0][0] - spec[1][0]]
    even, odd = [None] * (n // 4 + 1), [None] * (n // 4 + 1)
    for k in range(n // 4 + 1):
        ar, ai = spec[k]
        br, bi = spec[n // 2 - k]
        if k == 0:
            even[0], odd[0] = (ar + br, None), (ar - br, None)
        elif 4 * k == n:
            even[k], odd[k] = (ar + ar, None), (-(ai + ai), None)
        else:
            even[k] = (ar + br, ai - bi)
            odd[k] = times_root(ar - br, ai + bi, k, n, 1)
    es, os = real_inverse(even), real_inverse(odd)
    out = [None] * n
    out[0::2], out[1::2] = es, os
    return out


def rows_of(ref, field, first_row):
    return jnp.swapaxes(ref[field, :, first_row : first_row + 8, :], 0, 1)


def pack_lat_kernel(tile0_ref, tile1_ref, tile2_ref, south_ref, north_ref):
    lane = lane_index((LEVELS, LANES))
    for out_ref, block, skip in ((south_ref, ROWS - 8, 8 - HALO), (north_ref, 0, 0)):
        rest = None
        for field in range(FIELDS):
            parts = [rows_of(ref, field, block) for ref in (tile0_ref, tile1_ref, tile2_ref)]
            for i in range(HALO):
                n = field * HALO + i
                out_ref[pl.ds(8 * n, 8), :] = parts[0][skip + i]
                out_ref[pl.ds(8 * (STRIP + n), 8), :] = parts[1][skip + i]
                place = n % 8
                tail = parts[2][skip + i]
                if place:
                    tail = jnp.where(lane >= 16 * place, pltpu.roll(tail, 16 * place, 1), rest)
                rest = tail
                if place == 7:
                    out_ref[pl.ds(8 * (2 * STRIP + n // 8), 8), :] = rest


def shifted(tiles, step, lane):
    turned = [pltpu.roll(t, (-step) % LANES, 1) for t in tiles]
    if step > 0:
        return [jnp.where(lane < LANES - step, turned[t], turned[(t + 1) % 3]) for t in range(3)]
    return [jnp.where(lane >= -step, turned[t], turned[(t + 2) % 3]) for t in range(3)]


def tendency(load, row, at, coef_ref, level_ref, lane):
    zonal = coef_ref[0, at]
    sound_zonal = coef_ref[1, at]
    turn = coef_ref[2, at]
    merid = level_ref[0]
    sound = level_ref[1]
    dx, dy, mid = [], [], []
    for field in range(FIELDS):
        centre = load(field, row)
        mid.append(centre)
        p1, m1 = shifted(centre, 1, lane), shifted(centre, -1, lane)
        p2, m2 = shifted(centre, 2, lane), shifted(centre, -2, lane)
        dx.append([8.0 * (p1[t] - m1[t]) - (p2[t] - m2[t]) for t in range(3)])
        n1, s1 = load(field, row + 1), load(field, row - 1)
        n2, s2 = load(field, row + 2), load(field, row - 2)
        dy.append([8.0 * (n1[t] - s1[t]) - (n2[t] - s2[t]) for t in range(3)])
    out = []
    for t in range(3):
        carry = [zonal * dx[f][t] + merid * dy[f][t] for f in range(FIELDS)]
        out.append(
            [
                carry[0] + (sound_zonal * dx[2][t] + turn * mid[1][t]),
                carry[1] + (sound * dy[2][t] - turn * mid[0][t]),
                carry[2] + (sound_zonal * dx[0][t] + sound * dy[1][t]),
                carry[3],
            ]
        )
    return out


def tiles_of(ref, *place):
    return [ref[(*place, slice(None), slice(t * LANES, (t + 1) * LANES))] for t in range(3)]


def put_tiles(ref, tiles, *place):
    for t in range(3):
        ref[(*place, slice(None), slice(t * LANES, (t + 1) * LANES))] = tiles[t]


def put_blocks(out_ref, dest, tends):
    for j, tend in enumerate(tends):
        rest = None
        for field in range(FIELDS):
            g = j * FIELDS + field
            out_ref[dest, pl.ds(8 * g, 8), :] = tend[0][field]
            out_ref[dest, pl.ds(64 + 8 * g, 8), :] = tend[1][field]
            tail = pltpu.roll(tend[2][field], HALO + 32 * field, 1)
            rest = rest + tail if field else tail
        out_ref[dest, pl.ds(128 + 8 * j, 8), :] = rest


def interior_kernel(
    tile0_ref,
    tile1_ref,
    tile2_ref,
    coef_ref,
    level_ref,
    out_ref,
    kept_ref,
    first_ref,
    second_ref,
    third_ref,
):
    lane = lane_index((LEVELS, LANES))
    for field in range(FIELDS):
        for block in range(0, ROWS, 8):
            parts = [rows_of(ref, field, block) for ref in (tile0_ref, tile1_ref, tile2_ref)]
            for i in range(8):
                row = block + i
                tail = jnp.where(lane < TAIL, parts[2][i], 0.0)
                tiles = [parts[0][i], parts[1][i], tail]
                put_tiles(first_ref, tiles, field, row)
                if row < 4:
                    put_tiles(kept_ref, tiles, 0, 0, field, row)
                if row >= ROWS - 4:
                    put_tiles(kept_ref, tiles, 0, 1, field, row - (ROWS - 4))

    def tend_of(ref, row):
        return tendency(
            lambda f, r: tiles_of(ref, f, r), row, row + HALO, coef_ref, level_ref, lane
        )

    def stage(source, target, scale, margin, unroll):
        def body(row, carry):
            tend = tend_of(source, row)
            for field in range(FIELDS):
                base = tiles_of(first_ref, field, row)
                put_tiles(target, [base[t] + tend[t][field] * scale for t in range(3)], field, row)
            return carry

        lax.fori_loop(margin, ROWS - margin, body, 0, unroll=unroll)

    def keep(source, which, margin):
        for field in range(FIELDS):
            for i in range(4):
                put_tiles(kept_ref, tiles_of(source, field, margin + i), which, 0, field, i)
                put_tiles(
                    kept_ref, tiles_of(source, field, ROWS - margin - 4 + i), which, 1, field, i
                )

    stage(first_ref, second_ref, 1.0 / 3.0, 2, 4)
    keep(second_ref, 1, 2)
    stage(second_ref, third_ref, 0.5, 4, 4)
    keep(third_ref, 2, 4)

    def last(dest, carry):
        put_blocks(out_ref, dest, [tend_of(third_ref, dest * 2 + j) for j in range(2)])
        return carry

    lax.fori_loop(EDGE, PARTS - EDGE, last, 0, unroll=2)


def edge_kernel(
    facts_ref,
    north_ref,
    south_ref,
    coef_ref,
    level_ref,
    kept_ref,
    in_ref,
    out_ref,
    first_ref,
    second_ref,
    third_ref,
):
    lane = lane_index((LEVELS, LANES))
    starts = ((-6, -4, -2), (ROWS - 4, ROWS - 6, ROWS - 8))
    scratch = (first_ref, second_ref, third_ref)
    for side, strip in enumerate((north_ref, south_ref)):
        inside = facts_ref[side] == 0
        tail_inside = jnp.logical_and(lane < TAIL, inside)
        for n in range(STRIP):
            field, i = n // HALO, n % HALO
            tail = strip[pl.ds(8 * (2 * STRIP + n // 8), 8), :]
            if n % 8:
                tail = pltpu.roll(tail, LANES - 16 * (n % 8), 1)
            tiles = [
                jnp.where(inside, strip[pl.ds(8 * n, 8), :], 0.0),
                jnp.where(inside, strip[pl.ds(8 * (STRIP + n), 8), :], 0.0),
                jnp.where(tail_inside, tail, 0.0),
            ]
            put_tiles(first_ref, tiles, side, field, i)

    def row_of(which, side, field, row):
        i = row - starts[side][which]
        own = i - 6 * (1 - side)
        if 0 <= own < 4:
            return tiles_of(kept_ref, which, side, field, own)
        return tiles_of(scratch[which], side, field, i - 4 * side)

    def tend_of(which, side, row):
        return tendency(
            lambda f, r: row_of(which, side, f, r), row, row + HALO, coef_ref, level_ref, lane
        )

    for which, scale, margin in ((1, 1.0 / 3.0, 4), (2, 0.5, 2)):
        for k in range(HALO):
            for side in range(2):
                row = starts[side][which] + 4 * side + k
                tend = tend_of(which - 1, side, row)
                outside = row < 0 or row >= ROWS
                for field in range(FIELDS):
                    base = row_of(0, side, field, row)
                    tiles = [base[t] + tend[t][field] * scale for t in range(3)]
                    if outside:
                        inside = facts_ref[side] == 0
                        tiles = [jnp.where(inside, tile, 0.0) for tile in tiles]
                    put_tiles(scratch[which], tiles, side, field, k)

    def copy(dest, carry):
        for part in range(OUT // 8):
            out_ref[dest, pl.ds(8 * part, 8), :] = in_ref[dest, pl.ds(8 * part, 8), :]
        return carry

    lax.fori_loop(EDGE, PARTS - EDGE, copy, 0)
    for pair in range(EDGE):
        for side in range(2):
            row = 2 * pair + side * (ROWS - HALO)
            tends = [tend_of(2, side, row + j) for j in range(2)]
            put_blocks(out_ref, pair + side * (PARTS - EDGE), tends)


def filter_kernel(
    facts_ref, in_ref, twist_ref, mask_ref, table_ref, out_ref, la_ref, lb_ref, sa_ref, sb_ref
):
    count = PARTS // 2 + 1
    bf16 = jnp.bfloat16
    lane8 = lane_index((8, LANES))

    def twist(r, tile):
        at = r * 6 + tile
        return twist_ref[pl.ds(at, 1), :], twist_ref[pl.ds(at + 3, 1), :]

    def forward(xs, tile):
        spec = real_dft(xs)
        out = [(spec[0][0], None)]
        for r in range(1, count):
            cos, sin = twist(r, tile)
            re, im = spec[r]
            if im is None:
                out.append((re * cos, -(re * sin)))
            else:
                out.append((re * cos + im * sin, im * cos - re * sin))
        return out

    def backward(pairs, tile):
        spec = [(pairs[0][0], None)]
        for r in range(1, count):
            cos, sin = twist(r, tile)
            a, b = pairs[r]
            if r == count - 1:
                spec.append((a * cos - b * sin, None))
            else:
                spec.append((a * cos - b * sin, a * sin + b * cos))
        return real_inverse(spec)

    def halves(value):
        high = value.astype(bf16)
        return high, (value - high.astype(jnp.float32)).astype(bf16)

    def put_main(ref, at, tile, value):
        high, low = halves(value)
        ref[at, tile * LANES : (tile + 1) * LANES] = high
        ref[at, WIDE + tile * LANES : WIDE + (tile + 1) * LANES] = low

    for tile in range(2):

        def main(pair, carry):
            xs = [in_ref[d, pl.ds(64 * tile + 16 * pair, 16), :] for d in range(PARTS)]
            for r, (a, b) in enumerate(forward(xs, tile)):
                put_main(la_ref, pl.ds(r * 64 + 16 * pair, 16), tile, a)
                if b is not None:
                    put_main(lb_ref, pl.ds((r - 1) * 64 + 16 * pair, 16), tile, b)
            return carry

        lax.fori_loop(0, 4, main, 0)

    def put_rest(ref, at, value):
        high = value.astype(bf16).astype(jnp.float32)
        for k, part in enumerate((high, value - high)):
            alone = [
                jnp.where((lane8 >= 32 * s) & (lane8 < 32 * s + 32), part, 0.0) for s in range(4)
            ]
            ref[pl.ds(at, 32), k * WIDE + 256 : (k + 1) * WIDE] = jnp.concatenate(alone, 0).astype(
                bf16
            )

    for j in range(2):
        rest_in = [in_ref[d, pl.ds(128 + 8 * j, 8), :] for d in range(PARTS)]
        for r, (a, b) in enumerate(forward(rest_in, 2)):
            put_rest(la_ref, r * 64 + 32 * j, a)
            if b is not None:
                put_rest(lb_ref, (r - 1) * 64 + 32 * j, b)

    def product(l_ref, dim):
        def times(part, table):
            return lax.dot_general(
                l_ref[:, part * WIDE : (part + 1) * WIDE],
                table_ref[table * WIDE : (table + 1) * WIDE, :],
                (((1,), (dim,)), ((), ())),
                preferred_element_type=jnp.float32,
            )

        return times(0, 0) + times(1, 0) + times(0, 1)

    sa_ref[...] = product(la_ref, 0)
    sb_ref[...] = product(lb_ref, 0)

    q = mask_ref[0:1, :].astype(jnp.int32)
    half = mask_ref[1:2, :]
    half_signed = mask_ref[2:3, :]

    def put_all(ref, at, value):
        high, low = halves(value)
        ref[at, 0:WIDE] = high
        ref[at, WIDE : 2 * WIDE] = low

    def swap(value):
        return jnp.concatenate(
            [
                value[:, LANES : 2 * LANES],
                value[:, 0:LANES],
                pltpu.roll(value[:, 2 * LANES :], LANES - REM, 1),
            ],
            axis=1,
        )

    for r in range(count):
        up = 16 * q + r
        up = jnp.minimum(up, NLON - up)
        down = jnp.abs(16 * q - r)
        for j in range(2):
            cut = facts_ref[2 + j]
            keep_up = jnp.where(up <= cut, 1.0, 0.0)
            keep_down = jnp.where(down <= cut, 1.0, 0.0)
            same = half * (keep_up + keep_down)
            cross = half_signed * (keep_up - keep_down)
            for part in range(2):
                at = pl.ds(r * 64 + j * 32 + part * 16, 16)
                a = sa_ref[at, :]
                if r == 0:
                    put_all(la_ref, at, a * same)
                    continue
                at_b = pl.ds((r - 1) * 64 + j * 32 + part * 16, 16)
                b = sb_ref[at_b, :]
                put_all(la_ref, at, a * same + swap(b) * cross)
                put_all(lb_ref, at_b, b * same - swap(a) * cross)

    sa_ref[...] = product(la_ref, 1)
    sb_ref[...] = product(lb_ref, 1)

    for tile in range(2):

        def back(pair, carry):
            pairs = []
            for r in range(count):
                where = slice(tile * LANES, (tile + 1) * LANES)
                a = sa_ref[pl.ds(r * 64 + 16 * pair, 16), where]
                b = sb_ref[pl.ds((r - 1) * 64 + 16 * pair, 16), where] if r else None
                pairs.append((a, b))
            for d, value in enumerate(backward(pairs, tile)):
                out_ref[d, pl.ds(64 * tile + 16 * pair, 16), :] = value
            return carry

        lax.fori_loop(0, 4, back, 0)

    def gathered(ref, at):
        total = ref[pl.ds(at, 8), 256:384]
        for s in range(1, 4):
            total = jnp.where(lane8 >= 32 * s, ref[pl.ds(at + 8 * s, 8), 256:384], total)
        return total

    rests = []
    for j in range(2):
        pairs = []
        for r in range(count):
            a = gathered(sa_ref, r * 64 + 32 * j)
            pairs.append((a, gathered(sb_ref, (r - 1) * 64 + 32 * j) if r else None))
        rests.append(backward(pairs, 2))
    for d in range(PARTS):
        out_ref[d, pl.ds(128, 8), :] = jnp.where(
            lane8 % 32 < 16,
            pltpu.roll(rests[0][d], LANES - HALO, 1),
            pltpu.roll(rests[1][d], 16 - HALO, 1),
        )


def final_kernel(state_ref, back_ref, out_ref):
    tile = pl.program_id(0)
    half = pl.program_id(1)

    def run(load):
        for f in range(FIELDS // 2):
            for block in range(0, ROWS, 8):
                units = [load((block + i) // 2, i % 2, f) for i in range(8)]
                added = jnp.swapaxes(jnp.stack(units), 0, 1)
                at = (f, slice(None), slice(block, block + 8), slice(None))
                out_ref[at] = state_ref[at] + added

    def place(j, f):
        return j * FIELDS + half * (FIELDS // 2) + f

    def rest(dest, j, f):
        turn = LANES - 32 * (half * (FIELDS // 2) + f) - 16 * j
        return pltpu.roll(back_ref[dest, pl.ds(128, 8), :], turn % LANES, 1)

    pl.when(tile == 0)(
        lambda: run(lambda d, j, f: back_ref[d, pl.ds(pl.multiple_of(8 * place(j, f), 8), 8), :])
    )
    pl.when(tile == 1)(
        lambda: run(
            lambda d, j, f: back_ref[d, pl.ds(pl.multiple_of(64 + 8 * place(j, f), 8), 8), :]
        )
    )
    pl.when(tile == 2)(lambda: run(rest))


def latitude_terms(first_row, row_count, all_rows):
    row_index = first_row + jnp.arange(row_count, dtype=jnp.int32)
    latitude = -0.5 * jnp.pi + (row_index.astype(jnp.float32) + 0.5) * (jnp.pi / all_rows)
    inv_cos = 1.0 / jnp.maximum(jnp.cos(latitude), 0.25)
    return inv_cos, jnp.sin(latitude)


def turn(cells, axis, step):
    count = lax.axis_size(axis)
    return lax.ppermute(cells, axis, [(i, (i + step) % count) for i in range(count)])


def tile_spec(tile):
    return pl.BlockSpec((FIELDS, LEVELS, ROWS, LANES), lambda i: (0, 0, 0, tile))


VMEM = pl.BlockSpec(memory_space=pltpu.VMEM)
SMEM = pl.BlockSpec(memory_space=pltpu.SMEM)


def grant(mib):
    return pltpu.CompilerParams(vmem_limit_bytes=mib * 1024 * 1024)


def shape(*dims):
    return jax.ShapeDtypeStruct(dims, jnp.float32)


def on_device(state, zonal_wind, merid_wind, sound_speed, cutoff, polar_mask):
    lat_count = lax.axis_size("lat")
    lat_place = lax.axis_index("lat")
    lon_place = lax.axis_index("lon")
    to_south, to_north = pl.pallas_call(
        pack_lat_kernel,
        grid=(1,),
        out_shape=(shape(STRIP_ROWS, LANES), shape(STRIP_ROWS, LANES)),
        in_specs=[tile_spec(t) for t in range(3)],
        out_specs=[VMEM, VMEM],
        compiler_params=grant(8),
        name="pack_lat",
    )(state, state, state)
    from_north = turn(to_south, "lat", 1)
    from_south = turn(to_north, "lat", -1)

    inv_cos, sin_lat = latitude_terms(lat_place * ROWS - HALO, EXT, lat_count * ROWS)
    level = lambda v: (v / 12.0)[None, :, None]
    full = (EXT, LEVELS, LANES)
    coefs = jnp.stack(
        [
            jnp.broadcast_to(-level(zonal_wind) * inv_cos[:, None, None], full),
            jnp.broadcast_to(-level(sound_speed) * inv_cos[:, None, None], full),
            jnp.broadcast_to((CORIOLIS * sin_lat)[:, None, None], full),
        ]
    )
    levels = jnp.stack(
        [jnp.broadcast_to(-level(v)[0], (LEVELS, LANES)) for v in (merid_wind, sound_speed)]
    )
    cuts = jnp.where(polar_mask == 1, cutoff, NLON // 2).astype(jnp.int32)
    ends = jnp.stack([lat_place == 0, lat_place == lat_count - 1]).astype(jnp.int32)
    facts = jnp.concatenate([ends, lax.dynamic_slice_in_dim(cuts, lon_place * 2, 2)])
    scratch = pltpu.VMEM((FIELDS, ROWS, LEVELS, WIDE), jnp.float32)
    inner, kept = pl.pallas_call(
        interior_kernel,
        grid=(1,),
        out_shape=(shape(PARTS, OUT, LANES), shape(3, 2, FIELDS, 4, LEVELS, WIDE)),
        in_specs=[tile_spec(t) for t in range(3)] + [VMEM] * 2,
        out_specs=(VMEM, VMEM),
        scratch_shapes=[scratch] * 3,
        compiler_params=grant(20),
        cost_estimate=pl.CostEstimate(
            flops=80_000_000, bytes_accessed=6_000_000, transcendentals=0
        ),
        name="interior",
    )(state, state, state, coefs, levels)
    scratch = pltpu.VMEM((2, FIELDS, HALO, LEVELS, WIDE), jnp.float32)
    blocks = pl.pallas_call(
        edge_kernel,
        out_shape=shape(PARTS, OUT, LANES),
        in_specs=[SMEM] + [VMEM] * 6,
        out_specs=VMEM,
        scratch_shapes=[scratch] * 3,
        compiler_params=grant(20),
        name="edge",
    )(facts, from_north, from_south, coefs, levels, kept, inner)

    whole = lax.all_to_all(blocks, "lon", split_axis=0, concat_axis=0, tiled=True)

    count = PARTS // 2 + 1
    filtered = pl.pallas_call(
        filter_kernel,
        out_shape=shape(PARTS, BACK, LANES),
        in_specs=[SMEM] + [VMEM] * 4,
        out_specs=VMEM,
        scratch_shapes=[
            pltpu.VMEM((count * 64, 2 * WIDE), jnp.bfloat16),
            pltpu.VMEM(((count - 1) * 64, 2 * WIDE), jnp.bfloat16),
            pltpu.VMEM((count * 64, WIDE), jnp.float32),
            pltpu.VMEM(((count - 1) * 64, WIDE), jnp.float32),
        ],
        compiler_params=grant(20),
        name="filter",
    )(
        facts,
        whole,
        jnp.asarray(twist_table()),
        jnp.asarray(mask_table()),
        jnp.asarray(dft_table()),
    )

    back = lax.all_to_all(filtered, "lon", split_axis=0, concat_axis=0, tiled=True)
    half_tile = pl.BlockSpec((FIELDS // 2, LEVELS, ROWS, LANES), lambda t, h: (h, 0, 0, t))
    return pl.pallas_call(
        final_kernel,
        grid=(3, 2),
        out_shape=shape(*state.shape),
        in_specs=[half_tile, VMEM],
        out_specs=half_tile,
        compiler_params=grant(12),
        name="final",
    )(state, back)


def solution(mesh):
    placed = (P(None, None, "lat", "lon"), P(), P(), P(), P("lat"), P("lat"))
    return jax.shard_map(
        on_device,
        mesh=mesh,
        in_specs=placed,
        out_specs=P(None, None, "lat", "lon"),
        check_vma=False,
    )
```

```python
import functools
import math

import jax
import jax.numpy as jnp
import ml_dtypes
import numpy as np
from jax import lax
from jax.experimental import pallas as pl
from jax.experimental.pallas import tpu as pltpu
from jax.sharding import PartitionSpec as P

CORIOLIS = 0.2
FIELDS = 4
LEVELS = 8
ROWS = 32
COLS = 270
PARTS = 16
NLON = PARTS * COLS
HALO = 6
EXT = ROWS + 2 * HALO
LANES = 128
WIDE = 3 * LANES
OUT = 144
BACK = 136
STRIP = FIELDS * HALO
STRIP_ROWS = (2 * STRIP + STRIP // 8) * 8
TURN = 48
TAIL = COLS - 2 * LANES
EDGE = HALO // 2
HALF = COLS // 2 + 1
REM = HALF - LANES


def lane_index(shape):
    return lax.broadcasted_iota(jnp.int32, shape, len(shape) - 1)


def frequency_lanes():
    lanes = np.arange(WIDE)
    q = np.where(lanes < 256, lanes % LANES, LANES + lanes % REM)
    is_sin = ((lanes >= LANES) & (lanes < 256)) | ((lanes >= 256 + REM) & (lanes < 256 + 2 * REM))
    is_cos = (lanes < LANES) | ((lanes >= 256) & (lanes < 256 + 3 * REM) & ~is_sin)
    return q, is_cos, is_sin


def column_lanes():
    slot = np.arange(LANES) % 32
    return np.concatenate([np.arange(256), np.where(slot < HALO, slot - HALO, 256 - HALO + slot)])


def dft_tables():
    m = column_lanes()
    m_ok = m < COLS + HALO
    q, is_cos, is_sin = frequency_lanes()
    phase = 2.0 * np.pi * ((m[:, None] * q[None, :]) % COLS) / COLS
    table = np.where(is_cos, np.cos(phase), 0.0) + np.where(is_sin, np.sin(phase), 0.0)
    table = (table * m_ok[:, None]).astype(np.float32)
    out = []
    for one in (table, table.T):
        high = one.astype(ml_dtypes.bfloat16)
        low = (one - high.astype(np.float32)).astype(ml_dtypes.bfloat16)
        wide = np.concatenate([high, low[:, 256:], low[:, :256]], 1)
        out.append(np.concatenate([wide, wide[256:]], 0))
    return np.concatenate(out, 0)


def mask_table():
    q, is_cos, is_sin = frequency_lanes()
    weight = np.where((q == 0) | (q == HALF - 1), 1.0, 2.0) / NLON
    weight = np.where(np.arange(WIDE) < 256 + 2 * REM, weight, 0.0)
    sign = np.where(is_sin, -1.0, 1.0)
    return np.stack([q, 0.5 * weight, 0.5 * sign * weight] + [q * 0] * 5).astype(np.float32)


def twist_table():
    rows = []
    for r in range(PARTS // 2 + 1):
        for fn in (np.cos, np.sin):
            for m in column_lanes().reshape(3, LANES):
                rows.append(fn(2.0 * np.pi * r * m / NLON))
    return np.stack(rows).astype(np.float32)


def times_root(re, im, k, n, sign):
    k = k % n
    if k == 0:
        return re, im
    if 4 * k == n:
        return (im, -re) if sign < 0 else (-im, re)
    if 8 * k == n:
        h = math.sqrt(0.5)
        return ((re + im) * h, (im - re) * h) if sign < 0 else ((re - im) * h, (im + re) * h)
    c, s = math.cos(2 * math.pi * k / n), sign * math.sin(2 * math.pi * k / n)
    return re * c - im * s, im * c + re * s


def real_dft(xs):
    n = len(xs)
    if n == 2:
        return [(xs[0] + xs[1], None), (xs[0] - xs[1], None)]
    even, odd = real_dft(xs[0::2]), real_dft(xs[1::2])
    out = [None] * (n // 2 + 1)
    for k in range(n // 4 + 1):
        er, ei = even[k]
        orr, oi = odd[k]
        if k == 0:
            out[0] = (er + orr, None)
            out[n // 2] = (er - orr, None)
        elif 4 * k == n:
            out[k] = (er, -orr)
        else:
            tr, ti = times_root(orr, oi, k, n, -1)
            out[k] = (er + tr, ei + ti)
            out[n // 2 - k] = (er - tr, ti - ei)
    return out


def real_inverse(spec):
    n = 2 * (len(spec) - 1)
    if n == 2:
        return [spec[0][0] + spec[1][0], spec[0][0] - spec[1][0]]
    even, odd = [None] * (n // 4 + 1), [None] * (n // 4 + 1)
    for k in range(n // 4 + 1):
        ar, ai = spec[k]
        br, bi = spec[n // 2 - k]
        if k == 0:
            even[0], odd[0] = (ar + br, None), (ar - br, None)
        elif 4 * k == n:
            even[k], odd[k] = (ar + ar, None), (-(ai + ai), None)
        else:
            even[k] = (ar + br, ai - bi)
            odd[k] = times_root(ar - br, ai + bi, k, n, 1)
    es, os = real_inverse(even), real_inverse(odd)
    out = [None] * n
    out[0::2], out[1::2] = es, os
    return out


def rows_of(ref, field, first_row):
    return jnp.swapaxes(ref[field, :, first_row : first_row + 8, :], 0, 1)


def pack_lat_kernel(tile0_ref, tile1_ref, tile2_ref, south_ref, north_ref):
    lane = lane_index((LEVELS, LANES))
    for out_ref, block, skip in ((south_ref, ROWS - 8, 8 - HALO), (north_ref, 0, 0)):
        rest = None
        for field in range(FIELDS):
            parts = [rows_of(ref, field, block) for ref in (tile0_ref, tile1_ref, tile2_ref)]
            for i in range(HALO):
                n = field * HALO + i
                out_ref[pl.ds(8 * n, 8), :] = parts[0][skip + i]
                out_ref[pl.ds(8 * (STRIP + n), 8), :] = parts[1][skip + i]
                place = n % 8
                tail = parts[2][skip + i]
                if place:
                    tail = jnp.where(lane >= 16 * place, pltpu.roll(tail, 16 * place, 1), rest)
                rest = tail
                if place == 7:
                    out_ref[pl.ds(8 * (2 * STRIP + n // 8), 8), :] = rest


def shifted(tiles, step, lane):
    turned = [pltpu.roll(t, (-step) % LANES, 1) for t in tiles]
    if step > 0:
        return [jnp.where(lane < LANES - step, turned[t], turned[(t + 1) % 3]) for t in range(3)]
    return [jnp.where(lane >= -step, turned[t], turned[(t + 2) % 3]) for t in range(3)]


def dx_of(tiles, lane):
    p1, m1 = shifted(tiles, 1, lane), shifted(tiles, -1, lane)
    p2, m2 = shifted(tiles, 2, lane), shifted(tiles, -2, lane)
    return [8.0 * (p1[t] - m1[t]) - (p2[t] - m2[t]) for t in range(3)]


def tendency(load, load_dx, row, at, rows_ref, level_ref):
    inv_cos = rows_ref[pl.ds(at, 1), :]
    turn = rows_ref[pl.ds(at + TURN, 1), :]
    zonal = level_ref[0] * inv_cos
    merid = level_ref[1]
    sound = level_ref[2]
    sound_zonal = sound * inv_cos
    dx, dy, mid = [], [], []
    for field in range(FIELDS):
        mid.append(load(field, row))
        dx.append(load_dx(field))
        n1, s1 = load(field, row + 1), load(field, row - 1)
        n2, s2 = load(field, row + 2), load(field, row - 2)
        dy.append([8.0 * (n1[t] - s1[t]) - (n2[t] - s2[t]) for t in range(3)])
    out = []
    for t in range(3):
        carry = [zonal * dx[f][t] + merid * dy[f][t] for f in range(FIELDS)]
        out.append(
            [
                carry[0] + (sound_zonal * dx[2][t] + turn * mid[1][t]),
                carry[1] + (sound * dy[2][t] - turn * mid[0][t]),
                carry[2] + (sound_zonal * dx[0][t] + sound * dy[1][t]),
                carry[3],
            ]
        )
    return out


def tiles_of(ref, *place):
    return [ref[(*place, slice(None), slice(t * LANES, (t + 1) * LANES))] for t in range(3)]


def put_tiles(ref, tiles, *place):
    for t in range(3):
        ref[(*place, slice(None), slice(t * LANES, (t + 1) * LANES))] = tiles[t]


def put_blocks(out_ref, dest, tends):
    for j, tend in enumerate(tends):
        rest = None
        for field in range(FIELDS):
            g = j * FIELDS + field
            out_ref[dest, pl.ds(8 * g, 8), :] = tend[0][field]
            out_ref[dest, pl.ds(64 + 8 * g, 8), :] = tend[1][field]
            tail = pltpu.roll(tend[2][field], HALO + 32 * field, 1)
            rest = rest + tail if field else tail
        out_ref[dest, pl.ds(128 + 8 * j, 8), :] = rest


def interior_kernel(
    tile0_ref,
    tile1_ref,
    tile2_ref,
    rows_ref,
    level_ref,
    out_ref,
    kept_ref,
    kept_dx_ref,
    first_ref,
    second_ref,
    third_ref,
):
    lane = lane_index((LEVELS, LANES))
    for field in range(FIELDS):
        for block in range(0, ROWS, 8):
            parts = [rows_of(ref, field, block) for ref in (tile0_ref, tile1_ref, tile2_ref)]
            for i in range(8):
                row = block + i
                tail = jnp.where(lane < TAIL, parts[2][i], 0.0)
                tiles = [parts[0][i], parts[1][i], tail]
                put_tiles(first_ref, tiles, field, row)
                if row < 4:
                    put_tiles(kept_ref, tiles, 0, 0, field, row)
                if row >= ROWS - 4:
                    put_tiles(kept_ref, tiles, 0, 1, field, row - (ROWS - 4))

    def tend_of(ref, row):
        return tendency(
            lambda f, r: tiles_of(ref, f, r),
            lambda f: dx_of(tiles_of(ref, f, row), lane),
            row,
            row + HALO,
            rows_ref,
            level_ref,
        )

    def stage(source, target, scale, margin, unroll):
        def body(row, carry):
            tend = tend_of(source, row)
            for field in range(FIELDS):
                base = tiles_of(first_ref, field, row)
                put_tiles(target, [base[t] + tend[t][field] * scale for t in range(3)], field, row)
            return carry

        lax.fori_loop(margin, ROWS - margin, body, 0, unroll=unroll)

    def keep(source, which):
        margin = 2 * which
        for field in range(FIELDS):
            for side, start in enumerate((margin, ROWS - margin - 4)):
                for i in range(4):
                    tiles = tiles_of(source, field, start + i)
                    if which:
                        put_tiles(kept_ref, tiles, which, side, field, i)
                    k = i - 2 * side
                    if 0 <= k < 2:
                        put_tiles(kept_dx_ref, dx_of(tiles, lane), which, side, field, k)

    keep(first_ref, 0)
    stage(first_ref, second_ref, 1.0 / 3.0, 2, 4)
    keep(second_ref, 1)
    stage(second_ref, third_ref, 0.5, 4, 4)
    keep(third_ref, 2)

    def last(dest, carry):
        put_blocks(out_ref, dest, [tend_of(third_ref, dest * 2 + j) for j in range(2)])
        return carry

    lax.fori_loop(EDGE, PARTS - EDGE, last, 0, unroll=2)


def edge_kernel(
    facts_ref,
    north_ref,
    south_ref,
    rows_ref,
    level_ref,
    kept_ref,
    kept_dx_ref,
    in_ref,
    out_ref,
    first_ref,
    second_ref,
    third_ref,
):
    lane = lane_index((LEVELS, LANES))
    starts = ((-6, -4, -2), (ROWS - 4, ROWS - 6, ROWS - 8))
    scratch = (first_ref, second_ref, third_ref)
    for side, strip in enumerate((north_ref, south_ref)):
        inside = facts_ref[side] == 0
        tail_inside = jnp.logical_and(lane < TAIL, inside)
        for n in range(STRIP):
            field, i = n // HALO, n % HALO
            tail = strip[pl.ds(8 * (2 * STRIP + n // 8), 8), :]
            if n % 8:
                tail = pltpu.roll(tail, LANES - 16 * (n % 8), 1)
            tiles = [
                jnp.where(inside, strip[pl.ds(8 * n, 8), :], 0.0),
                jnp.where(inside, strip[pl.ds(8 * (STRIP + n), 8), :], 0.0),
                jnp.where(tail_inside, tail, 0.0),
            ]
            put_tiles(first_ref, tiles, side, field, i)

    def row_of(which, side, field, row):
        i = row - starts[side][which]
        own = i - 6 * (1 - side)
        if 0 <= own < 4:
            return tiles_of(kept_ref, which, side, field, own)
        return tiles_of(scratch[which], side, field, i - 4 * side)

    def tend_of(which, side, row):
        def load_dx(field):
            k = row - (2 * which if side == 0 else ROWS - 2 * which - 2)
            if 0 <= k < 2:
                return tiles_of(kept_dx_ref, which, side, field, k)
            return dx_of(row_of(which, side, field, row), lane)

        return tendency(
            lambda f, r: row_of(which, side, f, r), load_dx, row, row + HALO, rows_ref, level_ref
        )

    for which, scale in ((1, 1.0 / 3.0), (2, 0.5)):
        for k in range(HALO):
            for side in range(2):
                row = starts[side][which] + 4 * side + k
                tend = tend_of(which - 1, side, row)
                outside = row < 0 or row >= ROWS
                for field in range(FIELDS):
                    base = row_of(0, side, field, row)
                    tiles = [base[t] + tend[t][field] * scale for t in range(3)]
                    if outside:
                        inside = facts_ref[side] == 0
                        tiles = [jnp.where(inside, tile, 0.0) for tile in tiles]
                    put_tiles(scratch[which], tiles, side, field, k)

    def copy(dest, carry):
        for part in range(OUT // 8):
            out_ref[dest, pl.ds(8 * part, 8), :] = in_ref[dest, pl.ds(8 * part, 8), :]
        return carry

    lax.fori_loop(EDGE, PARTS - EDGE, copy, 0)
    for pair in range(EDGE):
        for side in range(2):
            row = 2 * pair + side * (ROWS - HALO)
            tends = [tend_of(2, side, row + j) for j in range(2)]
            put_blocks(out_ref, pair + side * (PARTS - EDGE), tends)


def filter_kernel(
    facts_ref, in_ref, twist_ref, mask_ref, table_ref, out_ref, la_ref, lb_ref, sa_ref, sb_ref
):
    count = PARTS // 2 + 1
    bf16 = jnp.bfloat16
    lane8 = lane_index((8, LANES))

    def twist(r, tile):
        at = r * 6 + tile
        return twist_ref[pl.ds(at, 1), :], twist_ref[pl.ds(at + 3, 1), :]

    def forward(xs, tile):
        spec = real_dft(xs)
        out = [(spec[0][0], None)]
        for r in range(1, count):
            cos, sin = twist(r, tile)
            re, im = spec[r]
            if im is None:
                out.append((re * cos, -(re * sin)))
            else:
                out.append((re * cos + im * sin, im * cos - re * sin))
        return out

    def backward(pairs, tile):
        spec = [(pairs[0][0], None)]
        for r in range(1, count):
            cos, sin = twist(r, tile)
            a, b = pairs[r]
            if r == count - 1:
                spec.append((a * cos - b * sin, None))
            else:
                spec.append((a * cos - b * sin, a * sin + b * cos))
        return real_inverse(spec)

    def halves(value):
        high = value.astype(bf16)
        return high, (value - high.astype(jnp.float32)).astype(bf16)

    def put_main(ref, at, tile, value):
        high, low = halves(value)
        ref[at, tile * LANES : (tile + 1) * LANES] = high
        ref[at, 256 + tile * LANES : 256 + (tile + 1) * LANES] = low

    for tile in range(2):

        def main(pair, carry):
            xs = [in_ref[d, pl.ds(64 * tile + 16 * pair, 16), :] for d in range(PARTS)]
            for r, (a, b) in enumerate(forward(xs, tile)):
                put_main(la_ref, pl.ds(r * 64 + 16 * pair, 16), tile, a)
                if b is not None:
                    put_main(lb_ref, pl.ds((r - 1) * 64 + 16 * pair, 16), tile, b)
            return carry

        lax.fori_loop(0, 4, main, 0)

    def put_rest(ref, at, value):
        high = value.astype(bf16).astype(jnp.float32)
        for k, part in enumerate((high, value - high)):
            alone = [
                jnp.where((lane8 >= 32 * s) & (lane8 < 32 * s + 32), part, 0.0) for s in range(4)
            ]
            ref[pl.ds(at, 32), 512 + k * LANES : 512 + (k + 1) * LANES] = jnp.concatenate(
                alone, 0
            ).astype(bf16)

    for j in range(2):
        rest_in = [in_ref[d, pl.ds(128 + 8 * j, 8), :] for d in range(PARTS)]
        for r, (a, b) in enumerate(forward(rest_in, 2)):
            put_rest(la_ref, r * 64 + 32 * j, a)
            if b is not None:
                put_rest(lb_ref, (r - 1) * 64 + 32 * j, b)

    def product(s_ref, l_ref, base):
        def times(columns, rows, width):
            return jnp.dot(
                l_ref[:, columns : columns + 256],
                table_ref[base + rows : base + rows + 256, 0:width],
                preferred_element_type=jnp.float32,
            )

        total = times(0, 0, 768) + times(512, 256, 768)
        low = times(256, 0, 512)
        s_ref[:, 0:256] = total[:, 0:256] + total[:, 512:768] + low[:, 0:256]
        rest = total[:, 256:512] + low[:, 256:512]
        s_ref[:, 256:384] = rest[:, 0:LANES] + rest[:, LANES:]

    product(sa_ref, la_ref, 0)
    product(sb_ref, lb_ref, 0)

    q = mask_ref[0:1, :].astype(jnp.int32)
    half = mask_ref[1:2, :]
    half_signed = mask_ref[2:3, :]

    def put_all(ref, at, value):
        high, low = halves(value)
        ref[at, 0:256] = high[:, 0:256]
        ref[at, 256:512] = low[:, 0:256]
        ref[at, 512:640] = high[:, 256:384]
        ref[at, 640:768] = low[:, 256:384]

    def swap(value):
        return jnp.concatenate(
            [
                value[:, LANES : 2 * LANES],
                value[:, 0:LANES],
                pltpu.roll(value[:, 2 * LANES :], LANES - REM, 1),
            ],
            axis=1,
        )

    for r in range(count):
        up = 16 * q + r
        up = jnp.minimum(up, NLON - up)
        down = jnp.abs(16 * q - r)
        for j in range(2):
            cut = facts_ref[2 + j]
            keep_up = jnp.where(up <= cut, 1.0, 0.0)
            keep_down = jnp.where(down <= cut, 1.0, 0.0)
            same = half * (keep_up + keep_down)
            cross = half_signed * (keep_up - keep_down)
            for part in range(2):
                at = pl.ds(r * 64 + j * 32 + part * 16, 16)
                a = sa_ref[at, :]
                if r == 0:
                    put_all(la_ref, at, a * same)
                    continue
                at_b = pl.ds((r - 1) * 64 + j * 32 + part * 16, 16)
                b = sb_ref[at_b, :]
                put_all(la_ref, at, a * same + swap(b) * cross)
                put_all(lb_ref, at_b, b * same - swap(a) * cross)

    product(sa_ref, la_ref, 512)
    product(sb_ref, lb_ref, 512)

    for tile in range(2):

        def back(pair, carry):
            pairs = []
            for r in range(count):
                where = slice(tile * LANES, (tile + 1) * LANES)
                a = sa_ref[pl.ds(r * 64 + 16 * pair, 16), where]
                b = sb_ref[pl.ds((r - 1) * 64 + 16 * pair, 16), where] if r else None
                pairs.append((a, b))
            for d, value in enumerate(backward(pairs, tile)):
                out_ref[d, pl.ds(64 * tile + 16 * pair, 16), :] = value
            return carry

        lax.fori_loop(0, 4, back, 0)

    def gathered(ref, at):
        total = ref[pl.ds(at, 8), 256:384]
        for s in range(1, 4):
            total = jnp.where(lane8 >= 32 * s, ref[pl.ds(at + 8 * s, 8), 256:384], total)
        return total

    rests = []
    for j in range(2):
        pairs = []
        for r in range(count):
            a = gathered(sa_ref, r * 64 + 32 * j)
            pairs.append((a, gathered(sb_ref, (r - 1) * 64 + 32 * j) if r else None))
        rests.append(backward(pairs, 2))
    for d in range(PARTS):
        out_ref[d, pl.ds(128, 8), :] = jnp.where(
            lane8 % 32 < 16,
            pltpu.roll(rests[0][d], LANES - HALO, 1),
            pltpu.roll(rests[1][d], 16 - HALO, 1),
        )


def final_kernel(state_ref, back_ref, out_ref, sum_ref, sems):
    copies = []
    for field in range(FIELDS):
        for block in range(0, ROWS, 8):
            tiles = [[], [], []]
            for i in range(8):
                dest, j = (block + i) // 2, i % 2
                g = j * FIELDS + field
                tiles[0].append(back_ref[dest, pl.ds(8 * g, 8), :])
                tiles[1].append(back_ref[dest, pl.ds(64 + 8 * g, 8), :])
                turn = (LANES - 32 * field - 16 * j) % LANES
                rest = back_ref[dest, pl.ds(128, 8), :]
                tiles[2].append(pltpu.roll(rest, turn, 1) if turn else rest)
            for t in range(3):
                width = min(LANES, COLS - t * LANES)
                added = jnp.swapaxes(jnp.stack(tiles[t]), 0, 1)
                at = (field, slice(None), slice(block, block + 8), slice(t * LANES, t * LANES + width))
                sum_ref[at] = state_ref[at] + added[:, :, :width]
        copy = pltpu.make_async_copy(sum_ref.at[field], out_ref.at[field], sems.at[field])
        copy.start()
        copies.append(copy)
    for copy in copies:
        copy.wait()


def latitude_terms(first_row, row_count, all_rows):
    row_index = first_row + jnp.arange(row_count, dtype=jnp.int32)
    latitude = -0.5 * jnp.pi + (row_index.astype(jnp.float32) + 0.5) * (jnp.pi / all_rows)
    inv_cos = 1.0 / jnp.maximum(jnp.cos(latitude), 0.25)
    return inv_cos, jnp.sin(latitude)


def tile_spec(tile):
    return pl.BlockSpec((FIELDS, LEVELS, ROWS, LANES), lambda i: (0, 0, 0, tile))


VMEM = pl.BlockSpec(memory_space=pltpu.VMEM)
SMEM = pl.BlockSpec(memory_space=pltpu.SMEM)


def grant(mib):
    return pltpu.CompilerParams(vmem_limit_bytes=mib * 1024 * 1024)


def shape(*dims):
    return jax.ShapeDtypeStruct(dims, jnp.float32)


def on_device(state, zonal_wind, merid_wind, sound_speed, cutoff, polar_mask):
    lat_count = lax.axis_size("lat")
    lat_place = lax.axis_index("lat")
    lon_place = lax.axis_index("lon")
    to_south, to_north = pl.pallas_call(
        pack_lat_kernel,
        grid=(1,),
        out_shape=(shape(STRIP_ROWS, LANES), shape(STRIP_ROWS, LANES)),
        in_specs=[tile_spec(t) for t in range(3)],
        out_specs=[VMEM, VMEM],
        compiler_params=grant(8),
        name="pack_lat",
    )(state, state, state)
    places = range(lat_count)
    from_north = lax.ppermute(to_south, "lat", [(i, (i + 1) % lat_count) for i in places])
    from_south = lax.ppermute(to_north, "lat", [((i + 1) % lat_count, i) for i in places])

    inv_cos, sin_lat = latitude_terms(lat_place * ROWS - HALO, EXT, lat_count * ROWS)
    gap = jnp.zeros((TURN - EXT,), jnp.float32)
    row_coefs = jnp.broadcast_to(
        jnp.concatenate([inv_cos, gap, CORIOLIS * sin_lat, gap])[:, None], (2 * TURN, LANES)
    )
    levels = jnp.broadcast_to(
        (jnp.stack([zonal_wind, merid_wind, sound_speed]) * (-1.0 / 12.0))[:, :, None],
        (3, LEVELS, LANES),
    )
    cuts = jnp.where(polar_mask == 1, cutoff, NLON // 2).astype(jnp.int32)
    ends = jnp.stack([lat_place == 0, lat_place == lat_count - 1]).astype(jnp.int32)
    facts = jnp.concatenate([ends, lax.dynamic_slice_in_dim(cuts, lon_place * 2, 2)])
    scratch = pltpu.VMEM((FIELDS, ROWS, LEVELS, WIDE), jnp.float32)
    inner, kept, kept_dx = pl.pallas_call(
        interior_kernel,
        grid=(1,),
        out_shape=(
            shape(PARTS, OUT, LANES),
            shape(3, 2, FIELDS, 4, LEVELS, WIDE),
            shape(3, 2, FIELDS, 2, LEVELS, WIDE),
        ),
        in_specs=[tile_spec(t) for t in range(3)] + [VMEM] * 2,
        out_specs=(VMEM, VMEM, VMEM),
        scratch_shapes=[scratch] * 3,
        compiler_params=grant(20),
        cost_estimate=pl.CostEstimate(
            flops=80_000_000, bytes_accessed=6_000_000, transcendentals=0
        ),
        name="interior",
    )(state, state, state, row_coefs, levels)
    scratch = pltpu.VMEM((2, FIELDS, HALO, LEVELS, WIDE), jnp.float32)
    blocks = pl.pallas_call(
        edge_kernel,
        out_shape=shape(PARTS, OUT, LANES),
        in_specs=[SMEM] + [VMEM] * 7,
        out_specs=VMEM,
        scratch_shapes=[scratch] * 3,
        compiler_params=grant(20),
        name="edge",
    )(facts, from_north, from_south, row_coefs, levels, kept, kept_dx, inner)

    whole = lax.all_to_all(blocks, "lon", split_axis=0, concat_axis=0, tiled=True)

    count = PARTS // 2 + 1
    filtered = pl.pallas_call(
        filter_kernel,
        out_shape=shape(PARTS, BACK, LANES),
        in_specs=[SMEM] + [VMEM] * 4,
        out_specs=VMEM,
        scratch_shapes=[
            pltpu.VMEM((count * 64, 2 * WIDE), jnp.bfloat16),
            pltpu.VMEM(((count - 1) * 64, 2 * WIDE), jnp.bfloat16),
            pltpu.VMEM((count * 64, WIDE), jnp.float32),
            pltpu.VMEM(((count - 1) * 64, WIDE), jnp.float32),
        ],
        compiler_params=grant(20),
        name="filter",
    )(
        facts,
        whole,
        jnp.asarray(twist_table()),
        jnp.asarray(mask_table()),
        jnp.asarray(dft_tables()),
    )

    back = lax.all_to_all(filtered, "lon", split_axis=0, concat_axis=0, tiled=True)
    return pl.pallas_call(
        final_kernel,
        out_shape=shape(*state.shape),
        in_specs=[VMEM, VMEM],
        out_specs=pl.BlockSpec(memory_space=pltpu.HBM),
        scratch_shapes=[
            pltpu.VMEM((FIELDS, LEVELS, ROWS, COLS), jnp.float32),
            pltpu.SemaphoreType.DMA((FIELDS,)),
        ],
        compiler_params=grant(12),
        name="final",
    )(state, back)


def solution(mesh):
    placed = (P(None, None, "lat", "lon"), P(), P(), P(), P("lat"), P("lat"))
    return jax.shard_map(
        on_device,
        mesh=mesh,
        in_specs=placed,
        out_specs=P(None, None, "lat", "lon"),
        check_vma=False,
    )
```

```python
import functools
import math

import jax
import jax.numpy as jnp
import ml_dtypes
import numpy as np
from jax import lax
from jax.experimental import pallas as pl
from jax.experimental.pallas import tpu as pltpu
from jax.sharding import PartitionSpec as P

CORIOLIS = 0.2
FIELDS = 4
LEVELS = 8
ROWS = 32
COLS = 270
PARTS = 16
NLON = PARTS * COLS
HALO = 6
EXT = ROWS + 2 * HALO
LANES = 128
WIDE = 3 * LANES
OUT = 144
BACK = 136
STRIP = FIELDS * HALO
STRIP_ROWS = (2 * STRIP + STRIP // 8) * 8
TURN = 48
TAIL = COLS - 2 * LANES
EDGE = HALO // 2
HALF = COLS // 2 + 1
REM = HALF - LANES


def lane_index(shape):
    return lax.broadcasted_iota(jnp.int32, shape, len(shape) - 1)


def frequency_lanes():
    lanes = np.arange(WIDE)
    q = np.where(lanes < 256, lanes % LANES, LANES + lanes % REM)
    is_sin = ((lanes >= LANES) & (lanes < 256)) | ((lanes >= 256 + REM) & (lanes < 256 + 2 * REM))
    is_cos = (lanes < LANES) | ((lanes >= 256) & (lanes < 256 + 3 * REM) & ~is_sin)
    return q, is_cos, is_sin


def column_lanes():
    slot = np.arange(LANES) % 32
    return np.concatenate([np.arange(256), np.where(slot < HALO, slot - HALO, 256 - HALO + slot)])


def dft_tables():
    m = column_lanes()
    m_ok = m < COLS + HALO
    q, is_cos, is_sin = frequency_lanes()
    phase = 2.0 * np.pi * ((m[:, None] * q[None, :]) % COLS) / COLS
    table = np.where(is_cos, np.cos(phase), 0.0) + np.where(is_sin, np.sin(phase), 0.0)
    table = (table * m_ok[:, None]).astype(np.float32)
    out = []
    for one in (table, table.T):
        high = one.astype(ml_dtypes.bfloat16)
        low = (one - high.astype(np.float32)).astype(ml_dtypes.bfloat16)
        wide = np.concatenate([high, low[:, 256:], low[:, :256]], 1)
        out.append(np.concatenate([wide[:256], wide, wide[256:]], 0))
    return np.concatenate(out, 0)


def mask_table():
    q, is_cos, is_sin = frequency_lanes()
    weight = np.where((q == 0) | (q == HALF - 1), 1.0, 2.0) / NLON
    weight = np.where(np.arange(WIDE) < 256 + 2 * REM, weight, 0.0)
    sign = np.where(is_sin, -1.0, 1.0)
    return np.stack([q, 0.5 * weight, 0.5 * sign * weight] + [q * 0] * 5).astype(np.float32)


def twist_table():
    rows = []
    for r in range(PARTS // 2 + 1):
        for fn in (np.cos, np.sin):
            for m in column_lanes().reshape(3, LANES):
                rows.append(fn(2.0 * np.pi * r * m / NLON))
    return np.stack(rows).astype(np.float32)


def times_root(re, im, k, n, sign):
    k = k % n
    if k == 0:
        return re, im
    if 4 * k == n:
        return (im, -re) if sign < 0 else (-im, re)
    if 8 * k == n:
        h = math.sqrt(0.5)
        return ((re + im) * h, (im - re) * h) if sign < 0 else ((re - im) * h, (im + re) * h)
    c, s = math.cos(2 * math.pi * k / n), sign * math.sin(2 * math.pi * k / n)
    return re * c - im * s, im * c + re * s


def real_dft(xs):
    n = len(xs)
    if n == 2:
        return [(xs[0] + xs[1], None), (xs[0] - xs[1], None)]
    even, odd = real_dft(xs[0::2]), real_dft(xs[1::2])
    out = [None] * (n // 2 + 1)
    for k in range(n // 4 + 1):
        er, ei = even[k]
        orr, oi = odd[k]
        if k == 0:
            out[0] = (er + orr, None)
            out[n // 2] = (er - orr, None)
        elif 4 * k == n:
            out[k] = (er, -orr)
        else:
            tr, ti = times_root(orr, oi, k, n, -1)
            out[k] = (er + tr, ei + ti)
            out[n // 2 - k] = (er - tr, ti - ei)
    return out


def real_inverse(spec):
    n = 2 * (len(spec) - 1)
    if n == 2:
        return [spec[0][0] + spec[1][0], spec[0][0] - spec[1][0]]
    even, odd = [None] * (n // 4 + 1), [None] * (n // 4 + 1)
    for k in range(n // 4 + 1):
        ar, ai = spec[k]
        br, bi = spec[n // 2 - k]
        if k == 0:
            even[0], odd[0] = (ar + br, None), (ar - br, None)
        elif 4 * k == n:
            even[k], odd[k] = (ar + ar, None), (-(ai + ai), None)
        else:
            even[k] = (ar + br, ai - bi)
            odd[k] = times_root(ar - br, ai + bi, k, n, 1)
    es, os = real_inverse(even), real_inverse(odd)
    out = [None] * n
    out[0::2], out[1::2] = es, os
    return out


def rows_of(ref, field, first_row):
    return jnp.swapaxes(ref[field, :, first_row : first_row + 8, :], 0, 1)


def pack_lat_kernel(*refs):
    lane = lane_index((LEVELS, LANES))
    for end, skip in enumerate((8 - HALO, 0)):
        out_ref = refs[6 + end]
        rest = None
        for field in range(FIELDS):
            parts = [rows_of(ref, field, 0) for ref in refs[3 * end : 3 * end + 3]]
            for i in range(HALO):
                n = field * HALO + i
                out_ref[pl.ds(8 * n, 8), :] = parts[0][skip + i]
                out_ref[pl.ds(8 * (STRIP + n), 8), :] = parts[1][skip + i]
                place = n % 8
                tail = parts[2][skip + i]
                if place:
                    tail = jnp.where(lane >= 16 * place, pltpu.roll(tail, 16 * place, 1), rest)
                rest = tail
                if place == 7:
                    out_ref[pl.ds(8 * (2 * STRIP + n // 8), 8), :] = rest


def shifted(tiles, step, lane):
    turned = [pltpu.roll(t, (-step) % LANES, 1) for t in tiles]
    if step > 0:
        return [jnp.where(lane < LANES - step, turned[t], turned[(t + 1) % 3]) for t in range(3)]
    return [jnp.where(lane >= -step, turned[t], turned[(t + 2) % 3]) for t in range(3)]


def dx_of(tiles, lane):
    p1, m1 = shifted(tiles, 1, lane), shifted(tiles, -1, lane)
    p2, m2 = shifted(tiles, 2, lane), shifted(tiles, -2, lane)
    return [8.0 * (p1[t] - m1[t]) - (p2[t] - m2[t]) for t in range(3)]


def tendency(load, load_dx, row, at, rows_ref, level_ref):
    inv_cos = rows_ref[pl.ds(at, 1), :]
    turn = rows_ref[pl.ds(at + TURN, 1), :]
    zonal = level_ref[0] * inv_cos
    merid = level_ref[1]
    sound = level_ref[2]
    sound_zonal = sound * inv_cos
    dx, dy, mid = [], [], []
    for field in range(FIELDS):
        mid.append(load(field, row))
        dx.append(load_dx(field))
        n1, s1 = load(field, row + 1), load(field, row - 1)
        n2, s2 = load(field, row + 2), load(field, row - 2)
        dy.append([8.0 * (n1[t] - s1[t]) - (n2[t] - s2[t]) for t in range(3)])
    out = []
    for t in range(3):
        carry = [zonal * dx[f][t] + merid * dy[f][t] for f in range(FIELDS)]
        out.append(
            [
                carry[0] + (sound_zonal * dx[2][t] + turn * mid[1][t]),
                carry[1] + (sound * dy[2][t] - turn * mid[0][t]),
                carry[2] + (sound_zonal * dx[0][t] + sound * dy[1][t]),
                carry[3],
            ]
        )
    return out


def tiles_of(ref, *place):
    return [ref[(*place, slice(None), slice(t * LANES, (t + 1) * LANES))] for t in range(3)]


def put_tiles(ref, tiles, *place):
    for t in range(3):
        ref[(*place, slice(None), slice(t * LANES, (t + 1) * LANES))] = tiles[t]


def put_blocks(out_ref, dest, tends):
    for j, tend in enumerate(tends):
        rest = None
        for field in range(FIELDS):
            g = j * FIELDS + field
            out_ref[dest, pl.ds(8 * g, 8), :] = tend[0][field]
            out_ref[dest, pl.ds(64 + 8 * g, 8), :] = tend[1][field]
            tail = pltpu.roll(tend[2][field], HALO + 32 * field, 1)
            rest = rest + tail if field else tail
        out_ref[dest, pl.ds(128 + 8 * j, 8), :] = rest


def interior_kernel(
    tile0_ref,
    tile1_ref,
    tile2_ref,
    rows_ref,
    level_ref,
    out_ref,
    kept_ref,
    kept_dx_ref,
    first_ref,
    second_ref,
    third_ref,
):
    lane = lane_index((LEVELS, LANES))
    for field in range(FIELDS):
        for block in range(0, ROWS, 8):
            parts = [rows_of(ref, field, block) for ref in (tile0_ref, tile1_ref, tile2_ref)]
            for i in range(8):
                row = block + i
                tail = jnp.where(lane < TAIL, parts[2][i], 0.0)
                tiles = [parts[0][i], parts[1][i], tail]
                put_tiles(first_ref, tiles, field, row)
                if row < 4:
                    put_tiles(kept_ref, tiles, 0, 0, field, row)
                if row >= ROWS - 4:
                    put_tiles(kept_ref, tiles, 0, 1, field, row - (ROWS - 4))

    def tend_of(ref, row):
        return tendency(
            lambda f, r: tiles_of(ref, f, r),
            lambda f: dx_of(tiles_of(ref, f, row), lane),
            row,
            row + HALO,
            rows_ref,
            level_ref,
        )

    def stage(source, target, scale, margin, unroll):
        def body(row, carry):
            tend = tend_of(source, row)
            for field in range(FIELDS):
                base = tiles_of(first_ref, field, row)
                put_tiles(target, [base[t] + tend[t][field] * scale for t in range(3)], field, row)
            return carry

        lax.fori_loop(margin, ROWS - margin, body, 0, unroll=unroll)

    def keep(source, which):
        margin = 2 * which
        for field in range(FIELDS):
            for side, start in enumerate((margin, ROWS - margin - 4)):
                for i in range(4):
                    tiles = tiles_of(source, field, start + i)
                    if which:
                        put_tiles(kept_ref, tiles, which, side, field, i)
                    k = i - 2 * side
                    if 0 <= k < 2:
                        put_tiles(kept_dx_ref, dx_of(tiles, lane), which, side, field, k)

    keep(first_ref, 0)
    stage(first_ref, second_ref, 1.0 / 3.0, 2, 4)
    keep(second_ref, 1)
    stage(second_ref, third_ref, 0.5, 4, 4)
    keep(third_ref, 2)

    def last(dest, carry):
        put_blocks(out_ref, dest, [tend_of(third_ref, dest * 2 + j) for j in range(2)])
        return carry

    lax.fori_loop(EDGE, PARTS - EDGE, last, 0, unroll=2)


def edge_kernel(
    facts_ref,
    north_ref,
    south_ref,
    rows_ref,
    level_ref,
    kept_ref,
    kept_dx_ref,
    in_ref,
    out_ref,
    first_ref,
    second_ref,
    third_ref,
):
    lane = lane_index((LEVELS, LANES))
    starts = ((-6, -4, -2), (ROWS - 4, ROWS - 6, ROWS - 8))
    scratch = (first_ref, second_ref, third_ref)
    for side, strip in enumerate((north_ref, south_ref)):
        inside = facts_ref[side] == 0
        tail_inside = jnp.logical_and(lane < TAIL, inside)
        for n in range(STRIP):
            field, i = n // HALO, n % HALO
            tail = strip[pl.ds(8 * (2 * STRIP + n // 8), 8), :]
            if n % 8:
                tail = pltpu.roll(tail, LANES - 16 * (n % 8), 1)
            tiles = [
                jnp.where(inside, strip[pl.ds(8 * n, 8), :], 0.0),
                jnp.where(inside, strip[pl.ds(8 * (STRIP + n), 8), :], 0.0),
                jnp.where(tail_inside, tail, 0.0),
            ]
            put_tiles(first_ref, tiles, side, field, i)

    def row_of(which, side, field, row):
        i = row - starts[side][which]
        own = i - 6 * (1 - side)
        if 0 <= own < 4:
            return tiles_of(kept_ref, which, side, field, own)
        return tiles_of(scratch[which], side, field, i - 4 * side)

    def tend_of(which, side, row):
        def load_dx(field):
            k = row - (2 * which if side == 0 else ROWS - 2 * which - 2)
            if 0 <= k < 2:
                return tiles_of(kept_dx_ref, which, side, field, k)
            return dx_of(row_of(which, side, field, row), lane)

        return tendency(
            lambda f, r: row_of(which, side, f, r), load_dx, row, row + HALO, rows_ref, level_ref
        )

    for which, scale in ((1, 1.0 / 3.0), (2, 0.5)):
        for k in range(HALO):
            for side in range(2):
                row = starts[side][which] + 4 * side + k
                tend = tend_of(which - 1, side, row)
                outside = row < 0 or row >= ROWS
                for field in range(FIELDS):
                    base = row_of(0, side, field, row)
                    tiles = [base[t] + tend[t][field] * scale for t in range(3)]
                    if outside:
                        inside = facts_ref[side] == 0
                        tiles = [jnp.where(inside, tile, 0.0) for tile in tiles]
                    put_tiles(scratch[which], tiles, side, field, k)

    def copy(dest, carry):
        for part in range(OUT // 8):
            out_ref[dest, pl.ds(8 * part, 8), :] = in_ref[dest, pl.ds(8 * part, 8), :]
        return carry

    lax.fori_loop(EDGE, PARTS - EDGE, copy, 0)
    for pair in range(EDGE):
        for side in range(2):
            row = 2 * pair + side * (ROWS - HALO)
            tends = [tend_of(2, side, row + j) for j in range(2)]
            put_blocks(out_ref, pair + side * (PARTS - EDGE), tends)


def filter_kernel(
    facts_ref, in_ref, twist_ref, mask_ref, table_ref, out_ref, la_ref, lb_ref, sa_ref, sb_ref
):
    count = PARTS // 2 + 1
    bf16 = jnp.bfloat16
    lane8 = lane_index((8, LANES))

    def twist(r, tile):
        at = r * 6 + tile
        return twist_ref[pl.ds(at, 1), :], twist_ref[pl.ds(at + 3, 1), :]

    def forward(xs, tile):
        spec = real_dft(xs)
        out = [(spec[0][0], None)]
        for r in range(1, count):
            cos, sin = twist(r, tile)
            re, im = spec[r]
            if im is None:
                out.append((re * cos, -(re * sin)))
            else:
                out.append((re * cos + im * sin, im * cos - re * sin))
        return out

    def backward(pairs, tile):
        spec = [(pairs[0][0], None)]
        for r in range(1, count):
            cos, sin = twist(r, tile)
            a, b = pairs[r]
            if r == count - 1:
                spec.append((a * cos - b * sin, None))
            else:
                spec.append((a * cos - b * sin, a * sin + b * cos))
        return real_inverse(spec)

    def halves(value):
        high = value.astype(bf16)
        return high, (value - high.astype(jnp.float32)).astype(bf16)

    def put_main(ref, at, tile, value):
        high, low = halves(value)
        ref[at, tile * LANES : (tile + 1) * LANES] = low
        ref[at, 256 + tile * LANES : 256 + (tile + 1) * LANES] = high

    for tile in range(2):

        def main(pair, carry):
            xs = [in_ref[d, pl.ds(64 * tile + 16 * pair, 16), :] for d in range(PARTS)]
            for r, (a, b) in enumerate(forward(xs, tile)):
                put_main(la_ref, pl.ds(r * 64 + 16 * pair, 16), tile, a)
                if b is not None:
                    put_main(lb_ref, pl.ds((r - 1) * 64 + 16 * pair, 16), tile, b)
            return carry

        lax.fori_loop(0, 4, main, 0, unroll=4)

    def put_rest(ref, at, value):
        high = value.astype(bf16).astype(jnp.float32)
        for k, part in enumerate((high, value - high)):
            alone = [
                jnp.where((lane8 >= 32 * s) & (lane8 < 32 * s + 32), part, 0.0) for s in range(4)
            ]
            ref[pl.ds(at, 32), 512 + k * LANES : 512 + (k + 1) * LANES] = jnp.concatenate(
                alone, 0
            ).astype(bf16)

    for j in range(2):
        rest_in = [in_ref[d, pl.ds(128 + 8 * j, 8), :] for d in range(PARTS)]
        for r, (a, b) in enumerate(forward(rest_in, 2)):
            put_rest(la_ref, r * 64 + 32 * j, a)
            if b is not None:
                put_rest(lb_ref, (r - 1) * 64 + 32 * j, b)

    def product(s_ref, l_ref, base):
        def times(rows, columns):
            return jnp.dot(
                l_ref[:, rows],
                table_ref[base + rows.start : base + rows.stop, columns],
                preferred_element_type=jnp.float32,
            )

        high = times(slice(0, 768), slice(0, 512))
        s_ref[:, 0:256] = high[:, 0:256] + times(slice(256, 768), slice(512, 768))
        s_ref[:, 256:384] = high[:, 256:384] + high[:, 384:512]

    product(sa_ref, la_ref, 0)
    product(sb_ref, lb_ref, 0)

    q = mask_ref[0:1, :].astype(jnp.int32)
    half = mask_ref[1:2, :]
    half_signed = mask_ref[2:3, :]

    def put_all(ref, at, value):
        high, low = halves(value)
        ref[at, 0:256] = low[:, 0:256]
        ref[at, 256:512] = high[:, 0:256]
        ref[at, 512:640] = high[:, 256:384]
        ref[at, 640:768] = low[:, 256:384]

    def swap(value):
        return jnp.concatenate(
            [
                value[:, LANES : 2 * LANES],
                value[:, 0:LANES],
                pltpu.roll(value[:, 2 * LANES :], LANES - REM, 1),
            ],
            axis=1,
        )

    for r in range(count):
        up = 16 * q + r
        up = jnp.minimum(up, NLON - up)
        down = jnp.abs(16 * q - r)
        for j in range(2):
            cut = facts_ref[2 + j]
            keep_up = jnp.where(up <= cut, 1.0, 0.0)
            keep_down = jnp.where(down <= cut, 1.0, 0.0)
            same = half * (keep_up + keep_down)
            cross = half_signed * (keep_up - keep_down)
            for part in range(2):
                at = pl.ds(r * 64 + j * 32 + part * 16, 16)
                a = sa_ref[at, :]
                if r == 0:
                    put_all(la_ref, at, a * same)
                    continue
                at_b = pl.ds((r - 1) * 64 + j * 32 + part * 16, 16)
                b = sb_ref[at_b, :]
                put_all(la_ref, at, a * same + swap(b) * cross)
                put_all(lb_ref, at_b, b * same - swap(a) * cross)

    product(sa_ref, la_ref, 768)
    product(sb_ref, lb_ref, 768)

    for tile in range(2):

        def back(pair, carry):
            pairs = []
            for r in range(count):
                where = slice(tile * LANES, (tile + 1) * LANES)
                a = sa_ref[pl.ds(r * 64 + 16 * pair, 16), where]
                b = sb_ref[pl.ds((r - 1) * 64 + 16 * pair, 16), where] if r else None
                pairs.append((a, b))
            for d, value in enumerate(backward(pairs, tile)):
                out_ref[d, pl.ds(64 * tile + 16 * pair, 16), :] = value
            return carry

        lax.fori_loop(0, 4, back, 0, unroll=4)

    def gathered(ref, at):
        total = ref[pl.ds(at, 8), 256:384]
        for s in range(1, 4):
            total = jnp.where(lane8 >= 32 * s, ref[pl.ds(at + 8 * s, 8), 256:384], total)
        return total

    rests = []
    for j in range(2):
        pairs = []
        for r in range(count):
            a = gathered(sa_ref, r * 64 + 32 * j)
            pairs.append((a, gathered(sb_ref, (r - 1) * 64 + 32 * j) if r else None))
        rests.append(backward(pairs, 2))
    for d in range(PARTS):
        out_ref[d, pl.ds(128, 8), :] = jnp.where(
            lane8 % 32 < 16,
            pltpu.roll(rests[0][d], LANES - HALO, 1),
            pltpu.roll(rests[1][d], 16 - HALO, 1),
        )


def final_kernel(state_ref, back_ref, out_ref, sum_ref, sems):
    copies = []
    for field in range(FIELDS):
        for block in range(0, ROWS, 8):
            tiles = [[], [], []]
            for i in range(8):
                dest, j = (block + i) // 2, i % 2
                g = j * FIELDS + field
                tiles[0].append(back_ref[dest, pl.ds(8 * g, 8), :])
                tiles[1].append(back_ref[dest, pl.ds(64 + 8 * g, 8), :])
                turn = (LANES - 32 * field - 16 * j) % LANES
                rest = back_ref[dest, pl.ds(128, 8), :]
                tiles[2].append(pltpu.roll(rest, turn, 1) if turn else rest)
            for t in range(3):
                width = min(LANES, COLS - t * LANES)
                added = jnp.swapaxes(jnp.stack(tiles[t]), 0, 1)
                at = (field, slice(None), slice(block, block + 8), slice(t * LANES, t * LANES + width))
                sum_ref[at] = state_ref[at] + added[:, :, :width]
        copy = pltpu.make_async_copy(sum_ref.at[field], out_ref.at[field], sems.at[field])
        copy.start()
        copies.append(copy)
    for copy in copies:
        copy.wait()


def latitude_terms(first_row, row_count, all_rows):
    row_index = first_row + jnp.arange(row_count, dtype=jnp.int32)
    latitude = -0.5 * jnp.pi + (row_index.astype(jnp.float32) + 0.5) * (jnp.pi / all_rows)
    inv_cos = 1.0 / jnp.maximum(jnp.cos(latitude), 0.25)
    return inv_cos, jnp.sin(latitude)


def tile_spec(tile):
    return pl.BlockSpec((FIELDS, LEVELS, ROWS, LANES), lambda i: (0, 0, 0, tile))


VMEM = pl.BlockSpec(memory_space=pltpu.VMEM)
SMEM = pl.BlockSpec(memory_space=pltpu.SMEM)


def grant(mib):
    return pltpu.CompilerParams(vmem_limit_bytes=mib * 1024 * 1024)


def shape(*dims):
    return jax.ShapeDtypeStruct(dims, jnp.float32)


def on_device(state, zonal_wind, merid_wind, sound_speed, cutoff, polar_mask):
    lat_count = lax.axis_size("lat")
    lat_place = lax.axis_index("lat")
    lon_place = lax.axis_index("lon")
    edge_rows = [lax.slice_in_dim(state, at, at + 8, axis=2) for at in (ROWS - 8, 0)]
    eight = lambda tile: pl.BlockSpec((FIELDS, LEVELS, 8, LANES), lambda i: (0, 0, 0, tile))
    to_south, to_north = pl.pallas_call(
        pack_lat_kernel,
        grid=(1,),
        out_shape=(shape(STRIP_ROWS, LANES), shape(STRIP_ROWS, LANES)),
        in_specs=[eight(t) for t in range(3)] * 2,
        out_specs=[VMEM, VMEM],
        compiler_params=grant(8),
        name="pack_lat",
    )(*edge_rows[:1] * 3, *edge_rows[1:] * 3)
    places = range(lat_count)
    from_north = lax.ppermute(to_south, "lat", [(i, (i + 1) % lat_count) for i in places])
    from_south = lax.ppermute(to_north, "lat", [((i + 1) % lat_count, i) for i in places])

    inv_cos, sin_lat = latitude_terms(lat_place * ROWS - HALO, EXT, lat_count * ROWS)
    gap = jnp.zeros((TURN - EXT,), jnp.float32)
    row_coefs = jnp.broadcast_to(
        jnp.concatenate([inv_cos, gap, CORIOLIS * sin_lat, gap])[:, None], (2 * TURN, LANES)
    )
    levels = jnp.broadcast_to(
        (jnp.stack([zonal_wind, merid_wind, sound_speed]) * (-1.0 / 12.0))[:, :, None],
        (3, LEVELS, LANES),
    )
    cuts = jnp.where(polar_mask == 1, cutoff, NLON // 2).astype(jnp.int32)
    ends = jnp.stack([lat_place == 0, lat_place == lat_count - 1]).astype(jnp.int32)
    facts = jnp.concatenate([ends, lax.dynamic_slice_in_dim(cuts, lon_place * 2, 2)])
    scratch = pltpu.VMEM((FIELDS, ROWS, LEVELS, WIDE), jnp.float32)
    inner, kept, kept_dx = pl.pallas_call(
        interior_kernel,
        grid=(1,),
        out_shape=(
            shape(PARTS, OUT, LANES),
            shape(3, 2, FIELDS, 4, LEVELS, WIDE),
            shape(3, 2, FIELDS, 2, LEVELS, WIDE),
        ),
        in_specs=[tile_spec(t) for t in range(3)] + [VMEM] * 2,
        out_specs=(VMEM, VMEM, VMEM),
        scratch_shapes=[scratch] * 3,
        compiler_params=grant(20),
        cost_estimate=pl.CostEstimate(
            flops=80_000_000, bytes_accessed=6_000_000, transcendentals=0
        ),
        name="interior",
    )(state, state, state, row_coefs, levels)
    scratch = pltpu.VMEM((2, FIELDS, HALO, LEVELS, WIDE), jnp.float32)
    blocks = pl.pallas_call(
        edge_kernel,
        out_shape=shape(PARTS, OUT, LANES),
        in_specs=[SMEM] + [VMEM] * 7,
        out_specs=VMEM,
        scratch_shapes=[scratch] * 3,
        compiler_params=grant(20),
        name="edge",
    )(facts, from_north, from_south, row_coefs, levels, kept, kept_dx, inner)

    whole = lax.all_to_all(blocks, "lon", split_axis=0, concat_axis=0, tiled=True)

    count = PARTS // 2 + 1
    filtered = pl.pallas_call(
        filter_kernel,
        out_shape=shape(PARTS, BACK, LANES),
        in_specs=[SMEM] + [VMEM] * 4,
        out_specs=VMEM,
        scratch_shapes=[
            pltpu.VMEM((count * 64, 2 * WIDE), jnp.bfloat16),
            pltpu.VMEM(((count - 1) * 64, 2 * WIDE), jnp.bfloat16),
            pltpu.VMEM((count * 64, WIDE), jnp.float32),
            pltpu.VMEM(((count - 1) * 64, WIDE), jnp.float32),
        ],
        compiler_params=grant(20),
        name="filter",
    )(
        facts,
        whole,
        jnp.asarray(twist_table()),
        jnp.asarray(mask_table()),
        jnp.asarray(dft_tables()),
    )

    back = lax.all_to_all(filtered, "lon", split_axis=0, concat_axis=0, tiled=True)
    return pl.pallas_call(
        final_kernel,
        out_shape=shape(*state.shape),
        in_specs=[VMEM, VMEM],
        out_specs=pl.BlockSpec(memory_space=pltpu.HBM),
        scratch_shapes=[
            pltpu.VMEM((FIELDS, LEVELS, ROWS, COLS), jnp.float32),
            pltpu.SemaphoreType.DMA((FIELDS,)),
        ],
        compiler_params=grant(12),
        name="final",
    )(state, back)


def solution(mesh):
    placed = (P(None, None, "lat", "lon"), P(), P(), P(), P("lat"), P("lat"))
    return jax.shard_map(
        on_device,
        mesh=mesh,
        in_specs=placed,
        out_specs=P(None, None, "lat", "lon"),
        check_vma=False,
    )
```

```python
import functools
import math

import jax
import jax.numpy as jnp
import ml_dtypes
import numpy as np
from jax import lax
from jax.experimental import pallas as pl
from jax.experimental.pallas import tpu as pltpu
from jax.sharding import PartitionSpec as P

CORIOLIS = 0.2
FIELDS = 4
LEVELS = 8
ROWS = 32
COLS = 270
PARTS = 16
NLON = PARTS * COLS
HALO = 6
EXT = ROWS + 2 * HALO
LANES = 128
WIDE = 3 * LANES
OUT = 144
BACK = 136
STRIP = FIELDS * HALO
STRIP_ROWS = (2 * STRIP + STRIP // 8) * 8
TURN = 48
TAIL = COLS - 2 * LANES
EDGE = HALO // 2
HALF = COLS // 2 + 1
REM = HALF - LANES


def lane_index(shape):
    return lax.broadcasted_iota(jnp.int32, shape, len(shape) - 1)


def frequency_lanes():
    lanes = np.arange(WIDE)
    q = np.where(lanes < 256, lanes % LANES, LANES + lanes % REM)
    is_sin = ((lanes >= LANES) & (lanes < 256)) | ((lanes >= 256 + REM) & (lanes < 256 + 2 * REM))
    is_cos = (lanes < LANES) | ((lanes >= 256) & (lanes < 256 + 3 * REM) & ~is_sin)
    return q, is_cos, is_sin


def column_lanes():
    slot = np.arange(LANES) % 32
    return np.concatenate([np.arange(256), np.where(slot < HALO, slot - HALO, 256 - HALO + slot)])


def dft_tables():
    m = column_lanes()
    m_ok = m < COLS + HALO
    q, is_cos, is_sin = frequency_lanes()
    phase = 2.0 * np.pi * ((m[:, None] * q[None, :]) % COLS) / COLS
    table = np.where(is_cos, np.cos(phase), 0.0) + np.where(is_sin, np.sin(phase), 0.0)
    table = (table * m_ok[:, None]).astype(np.float32)
    out = []
    for one in (table, table.T):
        high = one.astype(ml_dtypes.bfloat16)
        low = (one - high.astype(np.float32)).astype(ml_dtypes.bfloat16)
        wide = np.concatenate([high, low[:, 256:], low[:, :256]], 1)
        out.append(np.concatenate([wide[:256], wide, wide[256:]], 0))
    return np.concatenate(out, 0)


def mask_table():
    q, is_cos, is_sin = frequency_lanes()
    weight = np.where((q == 0) | (q == HALF - 1), 1.0, 2.0) / NLON
    weight = np.where(np.arange(WIDE) < 256 + 2 * REM, weight, 0.0)
    sign = np.where(is_sin, -1.0, 1.0)
    return np.stack([q, 0.5 * weight, 0.5 * sign * weight] + [q * 0] * 5).astype(np.float32)


def difference_table():
    table = np.zeros((WIDE, WIDE))
    lanes = np.arange(WIDE)
    for step, factor in ((1, 8.0), (-1, -8.0), (2, -1.0), (-2, 1.0)):
        table[(lanes + step) % WIDE, lanes] = factor
    main, rest = table[:256], table[256:]
    return np.concatenate([main, main, rest, rest], 0).astype(ml_dtypes.bfloat16)


def twist_table():
    rows = []
    for r in range(PARTS // 2 + 1):
        for fn in (np.cos, np.sin):
            for m in column_lanes().reshape(3, LANES):
                rows.append(fn(2.0 * np.pi * r * m / NLON))
    return np.stack(rows).astype(np.float32)


def times_root(re, im, k, n, sign):
    k = k % n
    if k == 0:
        return re, im
    if 4 * k == n:
        return (im, -re) if sign < 0 else (-im, re)
    if 8 * k == n:
        h = math.sqrt(0.5)
        return ((re + im) * h, (im - re) * h) if sign < 0 else ((re - im) * h, (im + re) * h)
    c, s = math.cos(2 * math.pi * k / n), sign * math.sin(2 * math.pi * k / n)
    return re * c - im * s, im * c + re * s


def real_dft(xs):
    n = len(xs)
    if n == 2:
        return [(xs[0] + xs[1], None), (xs[0] - xs[1], None)]
    even, odd = real_dft(xs[0::2]), real_dft(xs[1::2])
    out = [None] * (n // 2 + 1)
    for k in range(n // 4 + 1):
        er, ei = even[k]
        orr, oi = odd[k]
        if k == 0:
            out[0] = (er + orr, None)
            out[n // 2] = (er - orr, None)
        elif 4 * k == n:
            out[k] = (er, -orr)
        else:
            tr, ti = times_root(orr, oi, k, n, -1)
            out[k] = (er + tr, ei + ti)
            out[n // 2 - k] = (er - tr, ti - ei)
    return out


def real_inverse(spec):
    n = 2 * (len(spec) - 1)
    if n == 2:
        return [spec[0][0] + spec[1][0], spec[0][0] - spec[1][0]]
    even, odd = [None] * (n // 4 + 1), [None] * (n // 4 + 1)
    for k in range(n // 4 + 1):
        ar, ai = spec[k]
        br, bi = spec[n // 2 - k]
        if k == 0:
            even[0], odd[0] = (ar + br, None), (ar - br, None)
        elif 4 * k == n:
            even[k], odd[k] = (ar + ar, None), (-(ai + ai), None)
        else:
            even[k] = (ar + br, ai - bi)
            odd[k] = times_root(ar - br, ai + bi, k, n, 1)
    es, os = real_inverse(even), real_inverse(odd)
    out = [None] * n
    out[0::2], out[1::2] = es, os
    return out


def rows_of(ref, field, first_row):
    return jnp.swapaxes(ref[field, :, first_row : first_row + 8, :], 0, 1)


def pack_lat_kernel(end, place_ref, *refs):
    lane = lane_index((LEVELS, LANES))
    odd = place_ref[0] % 2 == 1
    out_ref = refs[-1]
    rest = None
    for field in range(FIELDS):
        south = [rows_of(ref, field, 0) for ref in refs[0:3]]
        north = [rows_of(ref, field, 0) for ref in refs[3:6]]
        for i in range(HALO):
            n = field * HALO + i
            place = n % 8
            row = []
            for t in range(3):
                pair = (north[t][i], south[t][8 - HALO + i])
                row.append(jnp.where(odd, pair[1 - end], pair[end]))
            out_ref[pl.ds(8 * n, 8), :] = row[0]
            out_ref[pl.ds(8 * (STRIP + n), 8), :] = row[1]
            tail = row[2]
            if place:
                tail = jnp.where(lane >= 16 * place, pltpu.roll(tail, 16 * place, 1), rest)
            rest = tail
            if place == 7:
                out_ref[pl.ds(8 * (2 * STRIP + n // 8), 8), :] = tail


def shifted(tiles, step, lane):
    turned = [pltpu.roll(t, (-step) % LANES, 1) for t in tiles]
    if step > 0:
        return [jnp.where(lane < LANES - step, turned[t], turned[(t + 1) % 3]) for t in range(3)]
    return [jnp.where(lane >= -step, turned[t], turned[(t + 2) % 3]) for t in range(3)]


def dx_of(tiles, lane):
    p1, m1 = shifted(tiles, 1, lane), shifted(tiles, -1, lane)
    p2, m2 = shifted(tiles, 2, lane), shifted(tiles, -2, lane)
    return [8.0 * (p1[t] - m1[t]) - (p2[t] - m2[t]) for t in range(3)]


def tendency(load, load_dx, row, at, rows_ref, level_ref):
    inv_cos = rows_ref[pl.ds(at, 1), :]
    turn = rows_ref[pl.ds(at + TURN, 1), :]
    zonal = level_ref[0] * inv_cos
    merid = level_ref[1]
    sound = level_ref[2]
    sound_zonal = sound * inv_cos
    dx, dy, mid = [], [], []
    for field in range(FIELDS):
        mid.append(load(field, row))
        dx.append(load_dx(field))
        n1, s1 = load(field, row + 1), load(field, row - 1)
        n2, s2 = load(field, row + 2), load(field, row - 2)
        dy.append([8.0 * (n1[t] - s1[t]) - (n2[t] - s2[t]) for t in range(3)])
    out = []
    for t in range(3):
        carry = [zonal * dx[f][t] + merid * dy[f][t] for f in range(FIELDS)]
        out.append(
            [
                carry[0] + (sound_zonal * dx[2][t] + turn * mid[1][t]),
                carry[1] + (sound * dy[2][t] - turn * mid[0][t]),
                carry[2] + (sound_zonal * dx[0][t] + sound * dy[1][t]),
                carry[3],
            ]
        )
    return out


def tiles_of(ref, *place):
    return [ref[(*place, slice(None), slice(t * LANES, (t + 1) * LANES))] for t in range(3)]


def put_tiles(ref, tiles, *place):
    for t in range(3):
        ref[(*place, slice(None), slice(t * LANES, (t + 1) * LANES))] = tiles[t]


def put_blocks(out_ref, dest, tends):
    for j, tend in enumerate(tends):
        rest = None
        for field in range(FIELDS):
            g = j * FIELDS + field
            out_ref[dest, pl.ds(8 * g, 8), :] = tend[0][field]
            out_ref[dest, pl.ds(64 + 8 * g, 8), :] = tend[1][field]
            tail = pltpu.roll(tend[2][field], HALO + 32 * field, 1)
            rest = rest + tail if field else tail
        out_ref[dest, pl.ds(128 + 8 * j, 8), :] = rest


def interior_kernel(
    tile0_ref,
    tile1_ref,
    tile2_ref,
    rows_ref,
    level_ref,
    table_ref,
    out_ref,
    kept_ref,
    kept_dx_ref,
    first_ref,
    second_ref,
    third_ref,
    split_ref,
    dx_ref,
):
    lane = lane_index((LEVELS, LANES))
    for field in range(FIELDS):
        for block in range(0, ROWS, 8):
            parts = [rows_of(ref, field, block) for ref in (tile0_ref, tile1_ref, tile2_ref)]
            parts[2] = [jnp.where(lane < TAIL, tail, 0.0) for tail in parts[2]]
            for i in range(8):
                row = block + i
                tiles = [part[i] for part in parts]
                put_tiles(first_ref, tiles, field, row)
                if row < 4:
                    put_tiles(kept_ref, tiles, 0, 0, field, row)
                if row >= ROWS - 4:
                    put_tiles(kept_ref, tiles, 0, 1, field, row - (ROWS - 4))
            for i in range(0, 8, 2):
                at = pl.ds((field * ROWS + block + i) * LEVELS, 16)
                for k, part in enumerate(parts):
                    both = jnp.concatenate([part[i], part[i + 1]], 0)
                    high = both.astype(jnp.bfloat16)
                    low = (both - high.astype(jnp.float32)).astype(jnp.bfloat16)
                    high_at, low_at = (512, 640) if k == 2 else (256 + k * LANES, k * LANES)
                    split_ref[at, high_at : high_at + LANES] = high
                    split_ref[at, low_at : low_at + LANES] = low

    dx_ref[...] = jnp.dot(split_ref[...], table_ref[...], preferred_element_type=jnp.float32)

    def state_dx(field, row):
        at = pl.ds(pl.multiple_of((field * ROWS + row) * LEVELS, LEVELS), LEVELS)
        return [dx_ref[at, t * LANES : (t + 1) * LANES] for t in range(3)]

    def dx_at(ref, field, row):
        return state_dx(field, row) if ref is first_ref else dx_of(tiles_of(ref, field, row), lane)

    def tend_of(ref, row):
        return tendency(
            lambda f, r: tiles_of(ref, f, r),
            lambda f: dx_at(ref, f, row),
            row,
            row + HALO,
            rows_ref,
            level_ref,
        )

    def stage(source, target, scale, margin, unroll):
        def body(row, carry):
            tend = tend_of(source, row)
            for field in range(FIELDS):
                base = tiles_of(first_ref, field, row)
                put_tiles(target, [base[t] + tend[t][field] * scale for t in range(3)], field, row)
            return carry

        lax.fori_loop(margin, ROWS - margin, body, 0, unroll=unroll)

    def keep(source, which):
        margin = 2 * which
        for field in range(FIELDS):
            for side, start in enumerate((margin, ROWS - margin - 4)):
                for i in range(4):
                    tiles = tiles_of(source, field, start + i)
                    if which:
                        put_tiles(kept_ref, tiles, which, side, field, i)
                    k = i - 2 * side
                    if 0 <= k < 2:
                        put_tiles(kept_dx_ref, dx_at(source, field, start + i), which, side, field, k)

    keep(first_ref, 0)
    stage(first_ref, second_ref, 1.0 / 3.0, 2, 4)
    keep(second_ref, 1)
    stage(second_ref, third_ref, 0.5, 4, 4)
    keep(third_ref, 2)

    def last(dest, carry):
        put_blocks(out_ref, dest, [tend_of(third_ref, dest * 2 + j) for j in range(2)])
        return carry

    lax.fori_loop(EDGE, PARTS - EDGE, last, 0, unroll=2)


def edge_kernel(
    facts_ref,
    strip_a_ref,
    strip_b_ref,
    rows_ref,
    level_ref,
    kept_ref,
    kept_dx_ref,
    in_ref,
    out_ref,
    first_ref,
    second_ref,
    third_ref,
):
    lane = lane_index((LEVELS, LANES))
    starts = ((-6, -4, -2), (ROWS - 4, ROWS - 6, ROWS - 8))
    scratch = (first_ref, second_ref, third_ref)
    odd = facts_ref[4] == 1
    for side in range(2):
        inside = facts_ref[side] == 0
        tail_inside = jnp.logical_and(lane < TAIL, inside)

        def strip(at):
            pair = (strip_a_ref[pl.ds(at, 8), :], strip_b_ref[pl.ds(at, 8), :])
            return jnp.where(odd, pair[1 - side], pair[side])

        for n in range(STRIP):
            field, i = n // HALO, n % HALO
            tail = strip(8 * (2 * STRIP + n // 8))
            if n % 8:
                tail = pltpu.roll(tail, LANES - 16 * (n % 8), 1)
            tiles = [
                jnp.where(inside, strip(8 * n), 0.0),
                jnp.where(inside, strip(8 * (STRIP + n)), 0.0),
                jnp.where(tail_inside, tail, 0.0),
            ]
            put_tiles(first_ref, tiles, side, field, i)

    def row_of(which, side, field, row):
        i = row - starts[side][which]
        own = i - 6 * (1 - side)
        if 0 <= own < 4:
            return tiles_of(kept_ref, which, side, field, own)
        return tiles_of(scratch[which], side, field, i - 4 * side)

    def tend_of(which, side, row):
        def load_dx(field):
            k = row - (2 * which if side == 0 else ROWS - 2 * which - 2)
            if 0 <= k < 2:
                return tiles_of(kept_dx_ref, which, side, field, k)
            return dx_of(row_of(which, side, field, row), lane)

        return tendency(
            lambda f, r: row_of(which, side, f, r), load_dx, row, row + HALO, rows_ref, level_ref
        )

    for which, scale in ((1, 1.0 / 3.0), (2, 0.5)):
        for k in range(HALO):
            for side in range(2):
                row = starts[side][which] + 4 * side + k
                tend = tend_of(which - 1, side, row)
                outside = row < 0 or row >= ROWS
                for field in range(FIELDS):
                    base = row_of(0, side, field, row)
                    tiles = [base[t] + tend[t][field] * scale for t in range(3)]
                    if outside:
                        inside = facts_ref[side] == 0
                        tiles = [jnp.where(inside, tile, 0.0) for tile in tiles]
                    put_tiles(scratch[which], tiles, side, field, k)

    def copy(dest, carry):
        for part in range(OUT // 8):
            out_ref[dest, pl.ds(8 * part, 8), :] = in_ref[dest, pl.ds(8 * part, 8), :]
        return carry

    lax.fori_loop(EDGE, PARTS - EDGE, copy, 0)
    for pair in range(EDGE):
        for side in range(2):
            row = 2 * pair + side * (ROWS - HALO)
            tends = [tend_of(2, side, row + j) for j in range(2)]
            put_blocks(out_ref, pair + side * (PARTS - EDGE), tends)


def filter_kernel(
    facts_ref, in_ref, twist_ref, mask_ref, table_ref, out_ref, la_ref, lb_ref, sa_ref, sb_ref
):
    count = PARTS // 2 + 1
    bf16 = jnp.bfloat16
    lane8 = lane_index((8, LANES))

    def twist(r, tile):
        at = r * 6 + tile
        return twist_ref[pl.ds(at, 1), :], twist_ref[pl.ds(at + 3, 1), :]

    def forward(xs, tile):
        spec = real_dft(xs)
        out = [(spec[0][0], None)]
        for r in range(1, count):
            cos, sin = twist(r, tile)
            re, im = spec[r]
            if im is None:
                out.append((re * cos, -(re * sin)))
            else:
                out.append((re * cos + im * sin, im * cos - re * sin))
        return out

    def backward(pairs, tile):
        spec = [(pairs[0][0], None)]
        for r in range(1, count):
            cos, sin = twist(r, tile)
            a, b = pairs[r]
            if r == count - 1:
                spec.append((a * cos - b * sin, None))
            else:
                spec.append((a * cos - b * sin, a * sin + b * cos))
        return real_inverse(spec)

    def halves(value):
        high = value.astype(bf16)
        return high, (value - high.astype(jnp.float32)).astype(bf16)

    def put_main(ref, at, tile, value):
        high, low = halves(value)
        ref[at, tile * LANES : (tile + 1) * LANES] = low
        ref[at, 256 + tile * LANES : 256 + (tile + 1) * LANES] = high

    for tile in range(2):

        def main(pair, carry):
            xs = [in_ref[d, pl.ds(64 * tile + 16 * pair, 16), :] for d in range(PARTS)]
            for r, (a, b) in enumerate(forward(xs, tile)):
                put_main(la_ref, pl.ds(r * 64 + 16 * pair, 16), tile, a)
                if b is not None:
                    put_main(lb_ref, pl.ds((r - 1) * 64 + 16 * pair, 16), tile, b)
            return carry

        lax.fori_loop(0, 4, main, 0, unroll=4)

    def put_rest(ref, at, value):
        high = value.astype(bf16).astype(jnp.float32)
        for k, part in enumerate((high, value - high)):
            alone = [
                jnp.where((lane8 >= 32 * s) & (lane8 < 32 * s + 32), part, 0.0) for s in range(4)
            ]
            ref[pl.ds(at, 32), 512 + k * LANES : 512 + (k + 1) * LANES] = jnp.concatenate(
                alone, 0
            ).astype(bf16)

    for j in range(2):
        rest_in = [in_ref[d, pl.ds(128 + 8 * j, 8), :] for d in range(PARTS)]
        for r, (a, b) in enumerate(forward(rest_in, 2)):
            put_rest(la_ref, r * 64 + 32 * j, a)
            if b is not None:
                put_rest(lb_ref, (r - 1) * 64 + 32 * j, b)

    def product(s_ref, l_ref, base):
        def times(rows, columns):
            return jnp.dot(
                l_ref[:, rows],
                table_ref[base + rows.start : base + rows.stop, columns],
                preferred_element_type=jnp.float32,
            )

        high = times(slice(0, 768), slice(0, 512))
        s_ref[:, 0:256] = high[:, 0:256] + times(slice(256, 768), slice(512, 768))
        s_ref[:, 256:384] = high[:, 256:384] + high[:, 384:512]

    product(sa_ref, la_ref, 0)
    product(sb_ref, lb_ref, 0)

    q = mask_ref[0:1, :].astype(jnp.int32)
    half = mask_ref[1:2, :]
    half_signed = mask_ref[2:3, :]

    def put_all(ref, at, value):
        high, low = halves(value)
        ref[at, 0:256] = low[:, 0:256]
        ref[at, 256:512] = high[:, 0:256]
        ref[at, 512:640] = high[:, 256:384]
        ref[at, 640:768] = low[:, 256:384]

    def swap(value):
        return jnp.concatenate(
            [
                value[:, LANES : 2 * LANES],
                value[:, 0:LANES],
                pltpu.roll(value[:, 2 * LANES :], LANES - REM, 1),
            ],
            axis=1,
        )

    for r in range(count):
        up = 16 * q + r
        up = jnp.minimum(up, NLON - up)
        down = jnp.abs(16 * q - r)
        for j in range(2):
            cut = facts_ref[2 + j]
            keep_up = jnp.where(up <= cut, 1.0, 0.0)
            keep_down = jnp.where(down <= cut, 1.0, 0.0)
            same = half * (keep_up + keep_down)
            cross = half_signed * (keep_up - keep_down)
            for part in range(2):
                at = pl.ds(r * 64 + j * 32 + part * 16, 16)
                a = sa_ref[at, :]
                if r == 0:
                    put_all(la_ref, at, a * same)
                    continue
                at_b = pl.ds((r - 1) * 64 + j * 32 + part * 16, 16)
                b = sb_ref[at_b, :]
                put_all(la_ref, at, a * same + swap(b) * cross)
                put_all(lb_ref, at_b, b * same - swap(a) * cross)

    product(sa_ref, la_ref, 768)
    product(sb_ref, lb_ref, 768)

    for tile in range(2):

        def back(pair, carry):
            pairs = []
            for r in range(count):
                where = slice(tile * LANES, (tile + 1) * LANES)
                a = sa_ref[pl.ds(r * 64 + 16 * pair, 16), where]
                b = sb_ref[pl.ds((r - 1) * 64 + 16 * pair, 16), where] if r else None
                pairs.append((a, b))
            for d, value in enumerate(backward(pairs, tile)):
                out_ref[d, pl.ds(64 * tile + 16 * pair, 16), :] = value
            return carry

        lax.fori_loop(0, 4, back, 0, unroll=4)

    def gathered(ref, at):
        total = ref[pl.ds(at, 8), 256:384]
        for s in range(1, 4):
            total = jnp.where(lane8 >= 32 * s, ref[pl.ds(at + 8 * s, 8), 256:384], total)
        return total

    rests = []
    for j in range(2):
        pairs = []
        for r in range(count):
            a = gathered(sa_ref, r * 64 + 32 * j)
            pairs.append((a, gathered(sb_ref, (r - 1) * 64 + 32 * j) if r else None))
        rests.append(backward(pairs, 2))
    for d in range(PARTS):
        out_ref[d, pl.ds(128, 8), :] = jnp.where(
            lane8 % 32 < 16,
            pltpu.roll(rests[0][d], LANES - HALO, 1),
            pltpu.roll(rests[1][d], 16 - HALO, 1),
        )


def final_kernel(state_ref, back_ref, out_ref, sum_ref, sems):
    copies = []
    for field in range(FIELDS):
        for block in range(0, ROWS, 8):
            tiles = [[], [], []]
            for i in range(8):
                dest, j = (block + i) // 2, i % 2
                g = j * FIELDS + field
                tiles[0].append(back_ref[dest, pl.ds(8 * g, 8), :])
                tiles[1].append(back_ref[dest, pl.ds(64 + 8 * g, 8), :])
                turn = (LANES - 32 * field - 16 * j) % LANES
                rest = back_ref[dest, pl.ds(128, 8), :]
                tiles[2].append(pltpu.roll(rest, turn, 1) if turn else rest)
            for t in range(3):
                width = min(LANES, COLS - t * LANES)
                added = jnp.swapaxes(jnp.stack(tiles[t]), 0, 1)
                at = (field, slice(None), slice(block, block + 8), slice(t * LANES, t * LANES + width))
                sum_ref[at] = state_ref[at] + added[:, :, :width]
        copy = pltpu.make_async_copy(sum_ref.at[field], out_ref.at[field], sems.at[field])
        copy.start()
        copies.append(copy)
    for copy in copies:
        copy.wait()


def latitude_terms(first_row, row_count, all_rows):
    row_index = first_row + jnp.arange(row_count, dtype=jnp.int32)
    latitude = -0.5 * jnp.pi + (row_index.astype(jnp.float32) + 0.5) * (jnp.pi / all_rows)
    inv_cos = 1.0 / jnp.maximum(jnp.cos(latitude), 0.25)
    return inv_cos, jnp.sin(latitude)


def tile_spec(tile):
    return pl.BlockSpec((FIELDS, LEVELS, ROWS, LANES), lambda i: (0, 0, 0, tile))


VMEM = pl.BlockSpec(memory_space=pltpu.VMEM)
SMEM = pl.BlockSpec(memory_space=pltpu.SMEM)


def grant(mib):
    return pltpu.CompilerParams(vmem_limit_bytes=mib * 1024 * 1024)


def shape(*dims):
    return jax.ShapeDtypeStruct(dims, jnp.float32)


def on_device(state, zonal_wind, merid_wind, sound_speed, cutoff, polar_mask):
    lat_count = lax.axis_size("lat")
    lat_place = lax.axis_index("lat")
    lon_place = lax.axis_index("lon")
    edge_rows = [lax.slice_in_dim(state, at, at + 8, axis=2) for at in (ROWS - 8, 0)]
    eight = lambda tile: pl.BlockSpec((FIELDS, LEVELS, 8, LANES), lambda i: (0, 0, 0, tile))
    def packed(end, *after):
        return pl.pallas_call(
            functools.partial(pack_lat_kernel, end),
            grid=(1,),
            out_shape=shape(STRIP_ROWS, LANES),
            in_specs=[SMEM] + [eight(t) for t in range(3)] * 2 + [VMEM] * len(after),
            out_specs=VMEM,
            compiler_params=grant(8),
            name="pack_lat",
        )(
            lat_place.astype(jnp.int32).reshape(1),
            *edge_rows[:1] * 3,
            *edge_rows[1:] * 3,
            *after,
        )

    second = packed(1)
    first = packed(0, second)
    last_place = lat_count - 1
    others = [(i, i if i in (0, last_place) else ((i + 1) ^ 1) - 1) for i in range(lat_count)]
    strip_a = lax.ppermute(first, "lat", others)
    strip_b = lax.ppermute(second, "lat", [(i, i ^ 1) for i in range(lat_count)])

    inv_cos, sin_lat = latitude_terms(lat_place * ROWS - HALO, EXT, lat_count * ROWS)
    gap = jnp.zeros((TURN - EXT,), jnp.float32)
    row_coefs = jnp.broadcast_to(
        jnp.concatenate([inv_cos, gap, CORIOLIS * sin_lat, gap])[:, None], (2 * TURN, LANES)
    )
    levels = jnp.broadcast_to(
        (jnp.stack([zonal_wind, merid_wind, sound_speed]) * (-1.0 / 12.0))[:, :, None],
        (3, LEVELS, LANES),
    )
    cuts = jnp.where(polar_mask == 1, cutoff, NLON // 2).astype(jnp.int32)
    ends = jnp.stack([lat_place == 0, lat_place == lat_count - 1]).astype(jnp.int32)
    odd = (lat_place % 2).astype(jnp.int32).reshape(1)
    facts = jnp.concatenate([ends, lax.dynamic_slice_in_dim(cuts, lon_place * 2, 2), odd])
    scratch = pltpu.VMEM((FIELDS, ROWS, LEVELS, WIDE), jnp.float32)
    inner, kept, kept_dx = pl.pallas_call(
        interior_kernel,
        grid=(1,),
        out_shape=(
            shape(PARTS, OUT, LANES),
            shape(3, 2, FIELDS, 4, LEVELS, WIDE),
            shape(3, 2, FIELDS, 2, LEVELS, WIDE),
        ),
        in_specs=[tile_spec(t) for t in range(3)] + [VMEM] * 3,
        out_specs=(VMEM, VMEM, VMEM),
        scratch_shapes=[scratch] * 3
        + [
            pltpu.VMEM((FIELDS * ROWS * LEVELS, 2 * WIDE), jnp.bfloat16),
            pltpu.VMEM((FIELDS * ROWS * LEVELS, WIDE), jnp.float32),
        ],
        compiler_params=grant(20),
        cost_estimate=pl.CostEstimate(
            flops=80_000_000, bytes_accessed=6_000_000, transcendentals=0
        ),
        name="interior",
    )(state, state, state, row_coefs, levels, jnp.asarray(difference_table()))
    scratch = pltpu.VMEM((2, FIELDS, HALO, LEVELS, WIDE), jnp.float32)
    blocks = pl.pallas_call(
        edge_kernel,
        out_shape=shape(PARTS, OUT, LANES),
        in_specs=[SMEM] + [VMEM] * 7,
        out_specs=VMEM,
        scratch_shapes=[scratch] * 3,
        compiler_params=grant(20),
        name="edge",
    )(facts, strip_a, strip_b, row_coefs, levels, kept, kept_dx, inner)

    whole = lax.all_to_all(blocks, "lon", split_axis=0, concat_axis=0, tiled=True)

    count = PARTS // 2 + 1
    filtered = pl.pallas_call(
        filter_kernel,
        out_shape=shape(PARTS, BACK, LANES),
        in_specs=[SMEM] + [VMEM] * 4,
        out_specs=VMEM,
        scratch_shapes=[
            pltpu.VMEM((count * 64, 2 * WIDE), jnp.bfloat16),
            pltpu.VMEM(((count - 1) * 64, 2 * WIDE), jnp.bfloat16),
            pltpu.VMEM((count * 64, WIDE), jnp.float32),
            pltpu.VMEM(((count - 1) * 64, WIDE), jnp.float32),
        ],
        compiler_params=grant(20),
        name="filter",
    )(
        facts,
        whole,
        jnp.asarray(twist_table()),
        jnp.asarray(mask_table()),
        jnp.asarray(dft_tables()),
    )

    back = lax.all_to_all(filtered, "lon", split_axis=0, concat_axis=0, tiled=True)
    return pl.pallas_call(
        final_kernel,
        out_shape=shape(*state.shape),
        in_specs=[VMEM, VMEM],
        out_specs=pl.BlockSpec(memory_space=pltpu.HBM),
        scratch_shapes=[
            pltpu.VMEM((FIELDS, LEVELS, ROWS, COLS), jnp.float32),
            pltpu.SemaphoreType.DMA((FIELDS,)),
        ],
        compiler_params=grant(12),
        name="final",
    )(state, back)


def solution(mesh):
    placed = (P(None, None, "lat", "lon"), P(), P(), P(), P("lat"), P("lat"))
    return jax.shard_map(
        on_device,
        mesh=mesh,
        in_specs=placed,
        out_specs=P(None, None, "lat", "lon"),
        check_vma=False,
    )
```

```python
import functools
import math

import jax
import jax.numpy as jnp
import ml_dtypes
import numpy as np
from jax import lax
from jax.experimental import pallas as pl
from jax.experimental.pallas import tpu as pltpu
from jax.sharding import PartitionSpec as P

CORIOLIS = 0.2
FIELDS = 4
LEVELS = 8
ROWS = 32
COLS = 270
PARTS = 16
NLON = PARTS * COLS
HALO = 6
EXT = ROWS + 2 * HALO
LANES = 128
WIDE = 3 * LANES
OUT = 144
BACK = 136
STRIP = FIELDS * HALO
STRIP_ROWS = (2 * STRIP + STRIP // 8) * 8
TURN = 48
TAIL = COLS - 2 * LANES
EDGE = HALO // 2
HALF = COLS // 2 + 1
REM = HALF - LANES


def lane_index(shape):
    return lax.broadcasted_iota(jnp.int32, shape, len(shape) - 1)


def frequency_lanes():
    lanes = np.arange(WIDE)
    q = np.where(lanes < 256, lanes % LANES, LANES + lanes % REM)
    is_sin = ((lanes >= LANES) & (lanes < 256)) | ((lanes >= 256 + REM) & (lanes < 256 + 2 * REM))
    is_cos = (lanes < LANES) | ((lanes >= 256) & (lanes < 256 + 3 * REM) & ~is_sin)
    return q, is_cos, is_sin


def column_lanes():
    slot = np.arange(LANES) % 32
    return np.concatenate([np.arange(256), np.where(slot < HALO, slot - HALO, 256 - HALO + slot)])


def dft_tables():
    m = column_lanes()
    m_ok = m < COLS + HALO
    q, is_cos, is_sin = frequency_lanes()
    phase = 2.0 * np.pi * ((m[:, None] * q[None, :]) % COLS) / COLS
    table = np.where(is_cos, np.cos(phase), 0.0) + np.where(is_sin, np.sin(phase), 0.0)
    table = (table * m_ok[:, None]).astype(np.float32)
    out = []
    for one in (table, table.T):
        high = one.astype(ml_dtypes.bfloat16)
        low = (one - high.astype(np.float32)).astype(ml_dtypes.bfloat16)
        wide = np.concatenate([high, low[:, 256:], low[:, :256]], 1)
        out.append(np.concatenate([wide[:256], wide, wide[256:]], 0))
    return np.concatenate(out, 0)


def mask_table():
    q, is_cos, is_sin = frequency_lanes()
    weight = np.where((q == 0) | (q == HALF - 1), 1.0, 2.0) / NLON
    weight = np.where(np.arange(WIDE) < 256 + 2 * REM, weight, 0.0)
    sign = np.where(is_sin, -1.0, 1.0)
    return np.stack([q, 0.5 * weight, 0.5 * sign * weight] + [q * 0] * 5).astype(np.float32)


def difference_table():
    table = np.zeros((WIDE, WIDE))
    lanes = np.arange(WIDE)
    for step, factor in ((1, 8.0), (-1, -8.0), (2, -1.0), (-2, 1.0)):
        table[(lanes + step) % WIDE, lanes] = factor
    main, rest = table[:256], table[256:]
    return np.concatenate([main, main, rest, rest], 0).astype(ml_dtypes.bfloat16)


def twist_table():
    rows = []
    for r in range(PARTS // 2 + 1):
        for fn in (np.cos, np.sin):
            for m in column_lanes().reshape(3, LANES):
                rows.append(fn(2.0 * np.pi * r * m / NLON))
    return np.stack(rows).astype(np.float32)


def times_root(re, im, k, n, sign):
    k = k % n
    if k == 0:
        return re, im
    if 4 * k == n:
        return (im, -re) if sign < 0 else (-im, re)
    if 8 * k == n:
        h = math.sqrt(0.5)
        return ((re + im) * h, (im - re) * h) if sign < 0 else ((re - im) * h, (im + re) * h)
    c, s = math.cos(2 * math.pi * k / n), sign * math.sin(2 * math.pi * k / n)
    return re * c - im * s, im * c + re * s


def real_dft(xs):
    n = len(xs)
    if n == 2:
        return [(xs[0] + xs[1], None), (xs[0] - xs[1], None)]
    even, odd = real_dft(xs[0::2]), real_dft(xs[1::2])
    out = [None] * (n // 2 + 1)
    for k in range(n // 4 + 1):
        er, ei = even[k]
        orr, oi = odd[k]
        if k == 0:
            out[0] = (er + orr, None)
            out[n // 2] = (er - orr, None)
        elif 4 * k == n:
            out[k] = (er, -orr)
        else:
            tr, ti = times_root(orr, oi, k, n, -1)
            out[k] = (er + tr, ei + ti)
            out[n // 2 - k] = (er - tr, ti - ei)
    return out


def real_inverse(spec):
    n = 2 * (len(spec) - 1)
    if n == 2:
        return [spec[0][0] + spec[1][0], spec[0][0] - spec[1][0]]
    even, odd = [None] * (n // 4 + 1), [None] * (n // 4 + 1)
    for k in range(n // 4 + 1):
        ar, ai = spec[k]
        br, bi = spec[n // 2 - k]
        if k == 0:
            even[0], odd[0] = (ar + br, None), (ar - br, None)
        elif 4 * k == n:
            even[k], odd[k] = (ar + ar, None), (-(ai + ai), None)
        else:
            even[k] = (ar + br, ai - bi)
            odd[k] = times_root(ar - br, ai + bi, k, n, 1)
    es, os = real_inverse(even), real_inverse(odd)
    out = [None] * n
    out[0::2], out[1::2] = es, os
    return out


def rows_of(ref, field, first_row):
    return jnp.swapaxes(ref[field, :, first_row : first_row + 8, :], 0, 1)


def pack_lat_kernel(end, place_ref, *refs):
    lane = lane_index((LEVELS, LANES))
    odd = place_ref[0] % 2 == 1
    out_ref = refs[-1]
    rest = None
    for field in range(FIELDS):
        south = [rows_of(ref, field, 0) for ref in refs[0:3]]
        north = [rows_of(ref, field, 0) for ref in refs[3:6]]
        for i in range(HALO):
            n = field * HALO + i
            place = n % 8
            row = []
            for t in range(3):
                pair = (north[t][i], south[t][8 - HALO + i])
                row.append(jnp.where(odd, pair[1 - end], pair[end]))
            out_ref[pl.ds(8 * n, 8), :] = row[0]
            out_ref[pl.ds(8 * (STRIP + n), 8), :] = row[1]
            tail = row[2]
            if place:
                tail = jnp.where(lane >= 16 * place, pltpu.roll(tail, 16 * place, 1), rest)
            rest = tail
            if place == 7:
                out_ref[pl.ds(8 * (2 * STRIP + n // 8), 8), :] = tail


def shifted(tiles, step, lane):
    turned = [pltpu.roll(t, (-step) % LANES, 1) for t in tiles]
    if step > 0:
        return [jnp.where(lane < LANES - step, turned[t], turned[(t + 1) % 3]) for t in range(3)]
    return [jnp.where(lane >= -step, turned[t], turned[(t + 2) % 3]) for t in range(3)]


def dx_of(tiles, lane):
    p1, m1 = shifted(tiles, 1, lane), shifted(tiles, -1, lane)
    p2, m2 = shifted(tiles, 2, lane), shifted(tiles, -2, lane)
    return [8.0 * (p1[t] - m1[t]) - (p2[t] - m2[t]) for t in range(3)]


def tendency(load, load_dx, row, at, rows_ref, level_ref):
    inv_cos = rows_ref[pl.ds(at, 1), :]
    turn = rows_ref[pl.ds(at + TURN, 1), :]
    zonal = level_ref[0] * inv_cos
    merid = level_ref[1]
    sound = level_ref[2]
    sound_zonal = sound * inv_cos
    dx, dy, mid = [], [], []
    for field in range(FIELDS):
        mid.append(load(field, row))
        dx.append(load_dx(field))
        n1, s1 = load(field, row + 1), load(field, row - 1)
        n2, s2 = load(field, row + 2), load(field, row - 2)
        dy.append([8.0 * (n1[t] - s1[t]) - (n2[t] - s2[t]) for t in range(3)])
    out = []
    for t in range(3):
        carry = [zonal * dx[f][t] + merid * dy[f][t] for f in range(FIELDS)]
        out.append(
            [
                carry[0] + (sound_zonal * dx[2][t] + turn * mid[1][t]),
                carry[1] + (sound * dy[2][t] - turn * mid[0][t]),
                carry[2] + (sound_zonal * dx[0][t] + sound * dy[1][t]),
                carry[3],
            ]
        )
    return out


def tiles_of(ref, *place):
    return [ref[(*place, slice(None), slice(t * LANES, (t + 1) * LANES))] for t in range(3)]


def put_tiles(ref, tiles, *place):
    for t in range(3):
        ref[(*place, slice(None), slice(t * LANES, (t + 1) * LANES))] = tiles[t]


def put_blocks(out_ref, dest, tends):
    for j, tend in enumerate(tends):
        rest = None
        for field in range(FIELDS):
            g = j * FIELDS + field
            out_ref[dest, pl.ds(8 * g, 8), :] = tend[0][field]
            out_ref[dest, pl.ds(64 + 8 * g, 8), :] = tend[1][field]
            tail = pltpu.roll(tend[2][field], HALO + 32 * field, 1)
            rest = rest + tail if field else tail
        out_ref[dest, pl.ds(128 + 8 * j, 8), :] = rest


def interior_kernel(
    tile0_ref,
    tile1_ref,
    tile2_ref,
    rows_ref,
    level_ref,
    table_ref,
    out_ref,
    kept_ref,
    kept_dx_ref,
    first_ref,
    second_ref,
    third_ref,
    split_ref,
    dx_ref,
):
    lane = lane_index((LEVELS, LANES))
    for field in range(FIELDS):
        for block in range(0, ROWS, 8):
            parts = [rows_of(ref, field, block) for ref in (tile0_ref, tile1_ref, tile2_ref)]
            parts[2] = [jnp.where(lane < TAIL, tail, 0.0) for tail in parts[2]]
            for i in range(8):
                row = block + i
                tiles = [part[i] for part in parts]
                put_tiles(first_ref, tiles, field, row)
                if row < 4:
                    put_tiles(kept_ref, tiles, 0, 0, field, row)
                if row >= ROWS - 4:
                    put_tiles(kept_ref, tiles, 0, 1, field, row - (ROWS - 4))
            for i in range(0, 8, 2):
                at = pl.ds((field * ROWS + block + i) * LEVELS, 16)
                for k, part in enumerate(parts):
                    both = jnp.concatenate([part[i], part[i + 1]], 0)
                    high = both.astype(jnp.bfloat16)
                    low = (both - high.astype(jnp.float32)).astype(jnp.bfloat16)
                    high_at, low_at = (512, 640) if k == 2 else (256 + k * LANES, k * LANES)
                    split_ref[at, high_at : high_at + LANES] = high
                    split_ref[at, low_at : low_at + LANES] = low

    dx_ref[...] = jnp.dot(split_ref[...], table_ref[...], preferred_element_type=jnp.float32)

    def state_dx(field, row):
        at = pl.ds(pl.multiple_of((field * ROWS + row) * LEVELS, LEVELS), LEVELS)
        return [dx_ref[at, t * LANES : (t + 1) * LANES] for t in range(3)]

    def dx_at(ref, field, row):
        return state_dx(field, row) if ref is first_ref else dx_of(tiles_of(ref, field, row), lane)

    def tend_of(ref, row):
        return tendency(
            lambda f, r: tiles_of(ref, f, r),
            lambda f: dx_at(ref, f, row),
            row,
            row + HALO,
            rows_ref,
            level_ref,
        )

    def stage(source, target, scale, margin, unroll):
        def body(row, carry):
            tend = tend_of(source, row)
            for field in range(FIELDS):
                base = tiles_of(first_ref, field, row)
                put_tiles(target, [base[t] + tend[t][field] * scale for t in range(3)], field, row)
            return carry

        lax.fori_loop(margin, ROWS - margin, body, 0, unroll=unroll)

    def keep(source, which):
        margin = 2 * which
        for field in range(FIELDS):
            for side, start in enumerate((margin, ROWS - margin - 4)):
                for i in range(4):
                    tiles = tiles_of(source, field, start + i)
                    if which:
                        put_tiles(kept_ref, tiles, which, side, field, i)
                    k = i - 2 * side
                    if 0 <= k < 2:
                        put_tiles(kept_dx_ref, dx_at(source, field, start + i), which, side, field, k)

    keep(first_ref, 0)
    stage(first_ref, second_ref, 1.0 / 3.0, 2, 4)
    keep(second_ref, 1)
    stage(second_ref, third_ref, 0.5, 4, 4)
    keep(third_ref, 2)

    def last(dest, carry):
        put_blocks(out_ref, dest, [tend_of(third_ref, dest * 2 + j) for j in range(2)])
        return carry

    lax.fori_loop(EDGE, PARTS - EDGE, last, 0, unroll=2)


def edge_kernel(
    facts_ref,
    strip_a_ref,
    strip_b_ref,
    rows_ref,
    level_ref,
    table_ref,
    kept_ref,
    kept_dx_ref,
    in_ref,
    out_ref,
    first_ref,
    second_ref,
    third_ref,
    split_ref,
    dx_ref,
):
    lane = lane_index((LEVELS, LANES))
    starts = ((-6, -4, -2), (ROWS - 4, ROWS - 6, ROWS - 8))
    scratch = (first_ref, second_ref, third_ref)
    odd = facts_ref[4] == 1
    for side in range(2):
        inside = facts_ref[side] == 0
        tail_inside = jnp.logical_and(lane < TAIL, inside)

        def strip(at):
            pair = (strip_a_ref[pl.ds(at, 8), :], strip_b_ref[pl.ds(at, 8), :])
            return jnp.where(odd, pair[1 - side], pair[side])

        for n in range(STRIP):
            field, i = n // HALO, n % HALO
            tail = strip(8 * (2 * STRIP + n // 8))
            if n % 8:
                tail = pltpu.roll(tail, LANES - 16 * (n % 8), 1)
            tiles = [
                jnp.where(inside, strip(8 * n), 0.0),
                jnp.where(inside, strip(8 * (STRIP + n)), 0.0),
                jnp.where(tail_inside, tail, 0.0),
            ]
            put_tiles(first_ref, tiles, side, field, i)

    for side in range(2):
        for field in range(FIELDS):
            for k in range(0, 4, 2):
                at = slice(((side * FIELDS + field) * 4 + k) * 8, ((side * FIELDS + field) * 4 + k + 2) * 8)
                pair = [tiles_of(first_ref, side, field, 2 * (1 - side) + k + d) for d in range(2)]
                for t in range(3):
                    both = jnp.concatenate([pair[0][t], pair[1][t]], 0)
                    high = both.astype(jnp.bfloat16)
                    low = (both - high.astype(jnp.float32)).astype(jnp.bfloat16)
                    high_at, low_at = (512, 640) if t == 2 else (256 + t * LANES, t * LANES)
                    split_ref[at, high_at : high_at + LANES] = high
                    split_ref[at, low_at : low_at + LANES] = low
    dx_ref[...] = jnp.dot(split_ref[...], table_ref[...], preferred_element_type=jnp.float32)

    def row_of(which, side, field, row):
        i = row - starts[side][which]
        own = i - 6 * (1 - side)
        if 0 <= own < 4:
            return tiles_of(kept_ref, which, side, field, own)
        return tiles_of(scratch[which], side, field, i - 4 * side)

    def tend_of(which, side, row):
        def load_dx(field):
            k = row - (2 * which if side == 0 else ROWS - 2 * which - 2)
            if 0 <= k < 2:
                return tiles_of(kept_dx_ref, which, side, field, k)
            if which == 0:
                k = row + 4 if side == 0 else row - ROWS
                at = ((side * FIELDS + field) * 4 + k) * 8
                return [dx_ref[at : at + 8, t * LANES : (t + 1) * LANES] for t in range(3)]
            return dx_of(row_of(which, side, field, row), lane)

        return tendency(
            lambda f, r: row_of(which, side, f, r), load_dx, row, row + HALO, rows_ref, level_ref
        )

    for which, scale in ((1, 1.0 / 3.0), (2, 0.5)):
        for k in range(HALO):
            for side in range(2):
                row = starts[side][which] + 4 * side + k
                tend = tend_of(which - 1, side, row)
                outside = row < 0 or row >= ROWS
                for field in range(FIELDS):
                    base = row_of(0, side, field, row)
                    tiles = [base[t] + tend[t][field] * scale for t in range(3)]
                    if outside:
                        inside = facts_ref[side] == 0
                        tiles = [jnp.where(inside, tile, 0.0) for tile in tiles]
                    put_tiles(scratch[which], tiles, side, field, k)

    def copy(dest, carry):
        for part in range(OUT // 8):
            out_ref[dest, pl.ds(8 * part, 8), :] = in_ref[dest, pl.ds(8 * part, 8), :]
        return carry

    lax.fori_loop(EDGE, PARTS - EDGE, copy, 0)
    for pair in range(EDGE):
        for side in range(2):
            row = 2 * pair + side * (ROWS - HALO)
            tends = [tend_of(2, side, row + j) for j in range(2)]
            put_blocks(out_ref, pair + side * (PARTS - EDGE), tends)


def filter_kernel(
    facts_ref, in_ref, twist_ref, mask_ref, table_ref, out_ref, la_ref, lb_ref, sa_ref, sb_ref
):
    count = PARTS // 2 + 1
    bf16 = jnp.bfloat16
    lane8 = lane_index((8, LANES))

    def twist(r, tile):
        at = r * 6 + tile
        return twist_ref[pl.ds(at, 1), :], twist_ref[pl.ds(at + 3, 1), :]

    def forward(xs, tile):
        spec = real_dft(xs)
        out = [(spec[0][0], None)]
        for r in range(1, count):
            cos, sin = twist(r, tile)
            re, im = spec[r]
            if im is None:
                out.append((re * cos, -(re * sin)))
            else:
                out.append((re * cos + im * sin, im * cos - re * sin))
        return out

    def backward(pairs, tile):
        spec = [(pairs[0][0], None)]
        for r in range(1, count):
            cos, sin = twist(r, tile)
            a, b = pairs[r]
            if r == count - 1:
                spec.append((a * cos - b * sin, None))
            else:
                spec.append((a * cos - b * sin, a * sin + b * cos))
        return real_inverse(spec)

    def halves(value):
        high = value.astype(bf16)
        return high, (value - high.astype(jnp.float32)).astype(bf16)

    def put_main(ref, at, tile, value):
        high, low = halves(value)
        ref[at, tile * LANES : (tile + 1) * LANES] = low
        ref[at, 256 + tile * LANES : 256 + (tile + 1) * LANES] = high

    for tile in range(2):

        def main(pair, carry):
            xs = [in_ref[d, pl.ds(64 * tile + 16 * pair, 16), :] for d in range(PARTS)]
            for r, (a, b) in enumerate(forward(xs, tile)):
                put_main(la_ref, pl.ds(r * 64 + 16 * pair, 16), tile, a)
                if b is not None:
                    put_main(lb_ref, pl.ds((r - 1) * 64 + 16 * pair, 16), tile, b)
            return carry

        lax.fori_loop(0, 4, main, 0, unroll=4)

    def put_rest(ref, at, value):
        high = value.astype(bf16).astype(jnp.float32)
        for k, part in enumerate((high, value - high)):
            alone = [
                jnp.where((lane8 >= 32 * s) & (lane8 < 32 * s + 32), part, 0.0) for s in range(4)
            ]
            ref[pl.ds(at, 32), 512 + k * LANES : 512 + (k + 1) * LANES] = jnp.concatenate(
                alone, 0
            ).astype(bf16)

    for j in range(2):
        rest_in = [in_ref[d, pl.ds(128 + 8 * j, 8), :] for d in range(PARTS)]
        for r, (a, b) in enumerate(forward(rest_in, 2)):
            put_rest(la_ref, r * 64 + 32 * j, a)
            if b is not None:
                put_rest(lb_ref, (r - 1) * 64 + 32 * j, b)

    def product(s_ref, l_ref, base):
        def times(rows, columns):
            return jnp.dot(
                l_ref[:, rows],
                table_ref[base + rows.start : base + rows.stop, columns],
                preferred_element_type=jnp.float32,
            )

        high = times(slice(0, 768), slice(0, 512))
        s_ref[:, 0:256] = high[:, 0:256] + times(slice(256, 768), slice(512, 768))
        s_ref[:, 256:384] = high[:, 256:384] + high[:, 384:512]

    product(sa_ref, la_ref, 0)
    product(sb_ref, lb_ref, 0)

    q = mask_ref[0:1, :].astype(jnp.int32)
    half = mask_ref[1:2, :]
    half_signed = mask_ref[2:3, :]

    def put_all(ref, at, value):
        high, low = halves(value)
        ref[at, 0:256] = low[:, 0:256]
        ref[at, 256:512] = high[:, 0:256]
        ref[at, 512:640] = high[:, 256:384]
        ref[at, 640:768] = low[:, 256:384]

    def swap(value):
        return jnp.concatenate(
            [
                value[:, LANES : 2 * LANES],
                value[:, 0:LANES],
                pltpu.roll(value[:, 2 * LANES :], LANES - REM, 1),
            ],
            axis=1,
        )

    for r in range(count):
        up = 16 * q + r
        up = jnp.minimum(up, NLON - up)
        down = jnp.abs(16 * q - r)
        for j in range(2):
            cut = facts_ref[2 + j]
            keep_up = jnp.where(up <= cut, 1.0, 0.0)
            keep_down = jnp.where(down <= cut, 1.0, 0.0)
            same = half * (keep_up + keep_down)
            cross = half_signed * (keep_up - keep_down)
            for part in range(2):
                at = pl.ds(r * 64 + j * 32 + part * 16, 16)
                a = sa_ref[at, :]
                if r == 0:
                    put_all(la_ref, at, a * same)
                    continue
                at_b = pl.ds((r - 1) * 64 + j * 32 + part * 16, 16)
                b = sb_ref[at_b, :]
                put_all(la_ref, at, a * same + swap(b) * cross)
                put_all(lb_ref, at_b, b * same - swap(a) * cross)

    product(sa_ref, la_ref, 768)
    product(sb_ref, lb_ref, 768)

    for tile in range(2):

        def back(pair, carry):
            pairs = []
            for r in range(count):
                where = slice(tile * LANES, (tile + 1) * LANES)
                a = sa_ref[pl.ds(r * 64 + 16 * pair, 16), where]
                b = sb_ref[pl.ds((r - 1) * 64 + 16 * pair, 16), where] if r else None
                pairs.append((a, b))
            for d, value in enumerate(backward(pairs, tile)):
                out_ref[d, pl.ds(64 * tile + 16 * pair, 16), :] = value
            return carry

        lax.fori_loop(0, 4, back, 0, unroll=4)

    def gathered(ref, at):
        total = ref[pl.ds(at, 8), 256:384]
        for s in range(1, 4):
            total = jnp.where(lane8 >= 32 * s, ref[pl.ds(at + 8 * s, 8), 256:384], total)
        return total

    rests = []
    for j in range(2):
        pairs = []
        for r in range(count):
            a = gathered(sa_ref, r * 64 + 32 * j)
            pairs.append((a, gathered(sb_ref, (r - 1) * 64 + 32 * j) if r else None))
        rests.append(backward(pairs, 2))
    for d in range(PARTS):
        out_ref[d, pl.ds(128, 8), :] = jnp.where(
            lane8 % 32 < 16,
            pltpu.roll(rests[0][d], LANES - HALO, 1),
            pltpu.roll(rests[1][d], 16 - HALO, 1),
        )


def final_kernel(state_ref, back_ref, out_ref, sum_ref, sems):
    copies = []
    for field in range(FIELDS):
        for block in range(0, ROWS, 8):
            tiles = [[], [], []]
            for i in range(8):
                dest, j = (block + i) // 2, i % 2
                g = j * FIELDS + field
                tiles[0].append(back_ref[dest, pl.ds(8 * g, 8), :])
                tiles[1].append(back_ref[dest, pl.ds(64 + 8 * g, 8), :])
                turn = (LANES - 32 * field - 16 * j) % LANES
                rest = back_ref[dest, pl.ds(128, 8), :]
                tiles[2].append(pltpu.roll(rest, turn, 1) if turn else rest)
            for t in range(3):
                width = min(LANES, COLS - t * LANES)
                added = jnp.swapaxes(jnp.stack(tiles[t]), 0, 1)
                at = (field, slice(None), slice(block, block + 8), slice(t * LANES, t * LANES + width))
                sum_ref[at] = state_ref[at] + added[:, :, :width]
        copy = pltpu.make_async_copy(sum_ref.at[field], out_ref.at[field], sems.at[field])
        copy.start()
        copies.append(copy)
    for copy in copies:
        copy.wait()


def latitude_terms(first_row, row_count, all_rows):
    row_index = first_row + jnp.arange(row_count, dtype=jnp.int32)
    latitude = -0.5 * jnp.pi + (row_index.astype(jnp.float32) + 0.5) * (jnp.pi / all_rows)
    inv_cos = 1.0 / jnp.maximum(jnp.cos(latitude), 0.25)
    return inv_cos, jnp.sin(latitude)


def tile_spec(tile):
    return pl.BlockSpec((FIELDS, LEVELS, ROWS, LANES), lambda i: (0, 0, 0, tile))


VMEM = pl.BlockSpec(memory_space=pltpu.VMEM)
SMEM = pl.BlockSpec(memory_space=pltpu.SMEM)


def grant(mib):
    return pltpu.CompilerParams(vmem_limit_bytes=mib * 1024 * 1024)


def shape(*dims):
    return jax.ShapeDtypeStruct(dims, jnp.float32)


def on_device(state, zonal_wind, merid_wind, sound_speed, cutoff, polar_mask):
    lat_count = lax.axis_size("lat")
    lat_place = lax.axis_index("lat")
    lon_place = lax.axis_index("lon")
    edge_rows = [lax.slice_in_dim(state, at, at + 8, axis=2) for at in (ROWS - 8, 0)]
    eight = lambda tile: pl.BlockSpec((FIELDS, LEVELS, 8, LANES), lambda i: (0, 0, 0, tile))
    def packed(end, *after):
        return pl.pallas_call(
            functools.partial(pack_lat_kernel, end),
            grid=(1,),
            out_shape=shape(STRIP_ROWS, LANES),
            in_specs=[SMEM] + [eight(t) for t in range(3)] * 2 + [VMEM] * len(after),
            out_specs=VMEM,
            compiler_params=grant(8),
            name="pack_lat",
        )(
            lat_place.astype(jnp.int32).reshape(1),
            *edge_rows[:1] * 3,
            *edge_rows[1:] * 3,
            *after,
        )

    second = packed(1)
    first = packed(0, second)
    last_place = lat_count - 1
    others = [(i, i if i in (0, last_place) else ((i + 1) ^ 1) - 1) for i in range(lat_count)]
    strip_a = lax.ppermute(first, "lat", others)
    strip_b = lax.ppermute(second, "lat", [(i, i ^ 1) for i in range(lat_count)])

    inv_cos, sin_lat = latitude_terms(lat_place * ROWS - HALO, EXT, lat_count * ROWS)
    gap = jnp.zeros((TURN - EXT,), jnp.float32)
    row_coefs = jnp.broadcast_to(
        jnp.concatenate([inv_cos, gap, CORIOLIS * sin_lat, gap])[:, None], (2 * TURN, LANES)
    )
    levels = jnp.broadcast_to(
        (jnp.stack([zonal_wind, merid_wind, sound_speed]) * (-1.0 / 12.0))[:, :, None],
        (3, LEVELS, LANES),
    )
    cuts = jnp.where(polar_mask == 1, cutoff, NLON // 2).astype(jnp.int32)
    ends = jnp.stack([lat_place == 0, lat_place == lat_count - 1]).astype(jnp.int32)
    odd = (lat_place % 2).astype(jnp.int32).reshape(1)
    facts = jnp.concatenate([ends, lax.dynamic_slice_in_dim(cuts, lon_place * 2, 2), odd])
    scratch = pltpu.VMEM((FIELDS, ROWS, LEVELS, WIDE), jnp.float32)
    difference = jnp.asarray(difference_table())
    inner, kept, kept_dx = pl.pallas_call(
        interior_kernel,
        grid=(1,),
        out_shape=(
            shape(PARTS, OUT, LANES),
            shape(3, 2, FIELDS, 4, LEVELS, WIDE),
            shape(3, 2, FIELDS, 2, LEVELS, WIDE),
        ),
        in_specs=[tile_spec(t) for t in range(3)] + [VMEM] * 3,
        out_specs=(VMEM, VMEM, VMEM),
        scratch_shapes=[scratch] * 3
        + [
            pltpu.VMEM((FIELDS * ROWS * LEVELS, 2 * WIDE), jnp.bfloat16),
            pltpu.VMEM((FIELDS * ROWS * LEVELS, WIDE), jnp.float32),
        ],
        compiler_params=grant(20),
        cost_estimate=pl.CostEstimate(
            flops=80_000_000, bytes_accessed=6_000_000, transcendentals=0
        ),
        name="interior",
    )(state, state, state, row_coefs, levels, difference)
    scratch = pltpu.VMEM((2, FIELDS, HALO, LEVELS, WIDE), jnp.float32)
    blocks = pl.pallas_call(
        edge_kernel,
        out_shape=shape(PARTS, OUT, LANES),
        in_specs=[SMEM] + [VMEM] * 8,
        out_specs=VMEM,
        scratch_shapes=[scratch] * 3
        + [pltpu.VMEM((256, 2 * WIDE), jnp.bfloat16), pltpu.VMEM((256, WIDE), jnp.float32)],
        compiler_params=grant(20),
        name="edge",
    )(facts, strip_a, strip_b, row_coefs, levels, difference, kept, kept_dx, inner)

    whole = lax.all_to_all(blocks, "lon", split_axis=0, concat_axis=0, tiled=True)

    count = PARTS // 2 + 1
    filtered = pl.pallas_call(
        filter_kernel,
        out_shape=shape(PARTS, BACK, LANES),
        in_specs=[SMEM] + [VMEM] * 4,
        out_specs=VMEM,
        scratch_shapes=[
            pltpu.VMEM((count * 64, 2 * WIDE), jnp.bfloat16),
            pltpu.VMEM(((count - 1) * 64, 2 * WIDE), jnp.bfloat16),
            pltpu.VMEM((count * 64, WIDE), jnp.float32),
            pltpu.VMEM(((count - 1) * 64, WIDE), jnp.float32),
        ],
        compiler_params=grant(20),
        name="filter",
    )(
        facts,
        whole,
        jnp.asarray(twist_table()),
        jnp.asarray(mask_table()),
        jnp.asarray(dft_tables()),
    )

    back = lax.all_to_all(filtered, "lon", split_axis=0, concat_axis=0, tiled=True)
    return pl.pallas_call(
        final_kernel,
        out_shape=shape(*state.shape),
        in_specs=[VMEM, VMEM],
        out_specs=pl.BlockSpec(memory_space=pltpu.HBM),
        scratch_shapes=[
            pltpu.VMEM((FIELDS, LEVELS, ROWS, COLS), jnp.float32),
            pltpu.SemaphoreType.DMA((FIELDS,)),
        ],
        compiler_params=grant(12),
        name="final",
    )(state, back)


def solution(mesh):
    placed = (P(None, None, "lat", "lon"), P(), P(), P(), P("lat"), P("lat"))
    return jax.shard_map(
        on_device,
        mesh=mesh,
        in_specs=placed,
        out_specs=P(None, None, "lat", "lon"),
        check_vma=False,
    )
```
